32 devices in a mesh: row: 4 (over y, x), col: 8 (over z, core).
Axes of the slice: x: 2, y: 2, z: 4, core: 2. Of those that a mesh axis runs over, the one named last changes fastest.
Arguments:
- density_block_entries: bfloat16 [32, 16, 128, 128], P('row', 'col'), as said below
- density_cols: int32 [32, 16], P('row', 'col'), may hold values from 0 to 31, as said below
- hamilton_values: bfloat16 [32, 16, 128, 128], P('row', 'col'), as said below
- hamilton_cols: int32 [32, 16], P('row', 'col'), may hold values from 0 to 31, as said below
- filter_cols: int32 [32, 32], P('row', 'col'), may hold values from 0 to 31, as said below
Outputs:
- squared_density: bfloat16 [32, 32, 128, 128], P('row', 'col')
- mixed_product: bfloat16 [32, 32, 128, 128], P('row', 'col')
- gradient: bfloat16 [32, 16, 128, 128], P('row', 'col')
The draws below stay inside these ranges and needn't reach their ends.
Inputs may be any that keep to these rules, and one draw needn't show every extreme that they name: `density_cols`: in every block row, slots c * 2 to (c + 1) * 2 - 1 hold distinct block columns of c * 4 to (c + 1) * 4 - 1. The pattern is symmetric: j is listed in row i exactly when i is listed in row j. `hamilton_cols`: in every block row, slots c * 2 to (c + 1) * 2 - 1 hold distinct block columns of c * 4 to (c + 1) * 4 - 1. The pattern is symmetric: j is listed in row i exactly when i is listed in row j. `filter_cols`: in every block row, slots c * 4 to (c + 1) * 4 - 1 hold distinct block columns of c * 4 to (c + 1) * 4 - 1. `density_block_entries`: the density matrix is symmetric: the block of row i and column j is the transpose of the block of row j and column i. `hamilton_values`: the Hamiltonian is symmetric: the block of row i and column j is the transpose of the block of row j and column i.
All inputs are finite; a program needn't handle non-finite values.
Results may differ from the reference program's by a relative error of at most 0.015.
Values may be sent and summed in bfloat16 or wider, within the bound.
No kernel may reach another device: no remote copies, remote signals or barrier semaphores. Data moves between devices by JAX's collectives and lax.ppermute only.
A program may use at most 128 MiB of HBM per device.

```python
import jax
import jax.numpy as jnp
from jax import lax

BS = 128
BC = 4
KA = 2
KH = 2
KF = 4
NB = 32


def block_pattern(key, tag, count):
    folded = jax.random.fold_in(key, tag)
    offset_key, shift_key = jax.random.split(folded)
    offsets = jax.random.permutation(offset_key, BC)[:count].astype(jnp.int32)
    group_count = NB // BC
    drawn = jax.random.randint(shift_key, (group_count, group_count), 0, BC)
    shifts = jnp.triu(drawn) + jnp.triu(drawn, 1).T
    row_numbers = jnp.arange(NB, dtype=jnp.int32)
    group_starts = jnp.arange(group_count, dtype=jnp.int32) * BC
    row_shifts = shifts[row_numbers // BC]
    slot_location = (offsets[None, None, :] - row_numbers[:, None, None] - group_starts[None, :, None] - row_shifts[:, :, None]) % BC
    return (group_starts[None, :, None] + slot_location).reshape(NB, group_count * count).astype(jnp.int32)


def block_values(key, tag, columns, scale):
    row_numbers = jnp.arange(NB, dtype=jnp.int32)[:, None] + jnp.zeros_like(columns)
    lower = jnp.minimum(row_numbers, columns)
    higher = jnp.maximum(row_numbers, columns)
    pairing = (lower * NB + higher).reshape(-1)
    folded = jax.random.fold_in(key, tag)

    def single_block(pair_index):
        pair_key = jax.random.fold_in(folded, pair_index)
        return jax.random.normal(pair_key, (BS, BS), jnp.float32)
    blocks = jax.vmap(single_block)(pairing).reshape(NB, columns.shape[1], BS, BS)
    turned = jnp.swapaxes(blocks, 2, 3)
    above = (row_numbers > columns)[:, :, None, None]
    diagonal = (row_numbers == columns)[:, :, None, None]
    is_symmetric_matrix = jnp.where(diagonal, (blocks + turned) * 0.7071, jnp.where(above, turned, blocks))
    return (is_symmetric_matrix * scale).astype(jnp.bfloat16)


def draw_density_cols(key, part):
    return block_pattern(key, 1, KA)


def draw_hamilton_cols(key, part):
    return block_pattern(key, 2, KH)


def draw_filter_cols(key, part):
    return block_pattern(key, 3, KF)


def draw_density_block_entries(key, part):
    scale = (BS * (NB // BC) * KA * KA / BC) ** (-0.25)
    return block_values(key, 11, block_pattern(key, 1, KA), scale)


def draw_hamilton_values(key, part):
    scale = (BS * (NB // BC) * KF * KH / BC) ** (-0.5)
    return block_values(key, 12, block_pattern(key, 2, KH), scale)


def setup_inputs(seed: int = 0) -> dict:
    seeds = jax.random.split(jax.random.key(seed), 6)
    density_block_entries = draw_density_block_entries(jax.random.fold_in(seeds[5], 71), 0)
    density_cols = draw_density_cols(jax.random.fold_in(seeds[5], 71), 0)
    hamilton_values = draw_hamilton_values(jax.random.fold_in(seeds[5], 71), 0)
    hamilton_cols = draw_hamilton_cols(jax.random.fold_in(seeds[5], 71), 0)
    filter_cols = draw_filter_cols(jax.random.fold_in(seeds[5], 71), 0)
    return dict(density_block_entries=density_block_entries, density_cols=density_cols, hamilton_values=hamilton_values, hamilton_cols=hamilton_cols, filter_cols=filter_cols)


def block_products(left_vals, left_cols, right_vals, right_cols):
    chosen = right_vals[left_cols].astype(jnp.float32)
    block_product_list = jnp.einsum("sab,stbc->stac", left_vals.astype(jnp.float32), chosen, precision=lax.Precision.HIGHEST)
    return block_product_list.reshape(-1, BS, BS), right_cols[left_cols].reshape(-1)


def to_slots(block_product_list, product_cols, targets):
    filter_picker = (targets[:, None] == product_cols[None, :]).astype(jnp.float32)
    return jnp.einsum("wv,vug->wug", filter_picker, block_product_list, precision=lax.Precision.HIGHEST)


def reference(density_block_entries, density_cols, hamilton_values, hamilton_cols, filter_cols):
    def first_pass(row_index):
        left_vals = density_block_entries[row_index]
        left_cols = density_cols[row_index]
        square_terms, square_cols = block_products(left_vals, left_cols, density_block_entries, density_cols)
        mixed_terms, mixed_cols = block_products(left_vals, left_cols, hamilton_values, hamilton_cols)
        square_slots = to_slots(square_terms, square_cols, filter_cols[row_index]).astype(jnp.bfloat16)
        mixed_slots = to_slots(mixed_terms, mixed_cols, filter_cols[row_index]).astype(jnp.bfloat16)
        direct_slots = to_slots(mixed_terms, mixed_cols, left_cols)
        return square_slots, mixed_slots, direct_slots

    row_numbers = jnp.arange(NB, dtype=jnp.int32)
    square_term, mixed_term, direct_term = lax.map(first_pass, row_numbers)

    def second_pass(row_index):
        cubic_terms, cubic_cols = block_products(square_term[row_index], filter_cols[row_index], hamilton_values, hamilton_cols)
        return to_slots(cubic_terms, cubic_cols, density_cols[row_index])

    cubic_term = lax.map(second_pass, row_numbers)
    gradient = (3.0 * direct_term - 2.0 * cubic_term).astype(jnp.bfloat16)
    return square_term, mixed_term, gradient
```

```python
import functools

import jax
import jax.numpy as jnp
from jax import lax
from jax.experimental import pallas as pl
from jax.experimental.pallas import tpu as pltpu
from jax.sharding import PartitionSpec as P

VMEM_LIMIT = 56 * 1024 * 1024
DENSE_LIMIT = 16 * 1024 * 1024


class Sizes:
    def __init__(self, n_row, n_col, density, hamilton, filt):
        self.n_row, self.n_col = n_row, n_col
        self.rows, self.ka, self.bs = density.shape[0], density.shape[1], density.shape[2]
        self.kh, self.kf = hamilton.shape[1], filt.shape[1]
        self.nb = self.rows * n_row
        self.bc = self.nb // n_col
        self.wide = self.bc * self.bs
        self.groups = 2 if n_col % (2 * n_row) == 0 else 1
        self.chunks = n_col // self.groups
        chunk_bytes = self.rows * self.bs * self.groups * self.wide * 2
        self.dense_slots = self.chunks if chunk_bytes * self.chunks <= DENSE_LIMIT else 1


def density_col(z, idx, row, col, i, s):
    return idx[((row * z.n_col + col) * z.rows + i) * (z.ka + z.kh) + s]


def hamilton_col(z, idx, row, col, i, s):
    return idx[((row * z.n_col + col) * z.rows + i) * (z.ka + z.kh) + z.ka + s]


def lanes(z, block):
    return pl.ds(pl.multiple_of(block * z.bs, z.bs), z.bs)


def start_pieces(z, pos, left_in, right_in, left_buf, right_buf, left_sem, right_sem):
    copies = []
    for n, ref in enumerate(right_in):
        copies.append(pltpu.make_async_copy(ref, right_buf.at[pos[0] ^ n], right_sem.at[pos[0] ^ n]))
    n_chip = z.n_col // 2
    for n, ref in enumerate(left_in):
        chip = lax.rem(pos[1] // 2 + n_chip - n // 2, n_chip)
        col = chip * 2 + (lax.rem(pos[1], 2) ^ (n % 2))
        copies.append(pltpu.make_async_copy(ref, left_buf.at[col], left_sem.at[col]))
    for copy in copies:
        copy.start()


def fill_right(z, pos, idx, col_of, count, right_buf, right_sem, right_dense):
    right_dense[...] = jnp.zeros_like(right_dense)

    def one_row(row, _):
        pltpu.make_async_copy(right_buf.at[row], right_buf.at[row], right_sem.at[row]).wait()
        for i in range(z.rows):
            for s in range(count):
                j = col_of(z, idx, row, pos[1], i, s) - pos[1] * z.bc
                right_dense[row * z.rows + i, :, lanes(z, j)] = right_buf[row, i, s]
        return 0

    lax.fori_loop(0, z.n_row, one_row, 0)


def fill_left(z, pos, idx, chunk, left_buf, left_dense, left_sem):
    slot = chunk if z.dense_slots > 1 else 0
    left_dense[slot] = jnp.zeros(left_dense.shape[1:], left_dense.dtype)
    for g in range(z.groups):
        col = chunk * z.groups + g
        if left_sem is not None:
            pltpu.make_async_copy(left_buf.at[col], left_buf.at[col], left_sem.at[col]).wait()
        for i in range(z.rows):
            for s in range(z.ka):
                k = density_col(z, idx, pos[0], col, i, s) - col * z.bc
                left_dense[slot, i * z.bs:(i + 1) * z.bs, lanes(z, k + g * z.bc)] = left_buf[col, i, s]
    return slot


def multiply_panels(z, pos, idx, left_buf, left_sem, left_dense, right_dense, total):
    def one_chunk(chunk, _):
        slot = fill_left(z, pos, idx, chunk, left_buf, left_dense, left_sem)
        blocks = z.groups * z.bc
        right = right_dense[pl.ds(chunk * blocks, blocks)].reshape(blocks * z.bs, z.wide)
        term = jnp.dot(left_dense[slot], right, preferred_element_type=jnp.float32)

        @pl.when(chunk == 0)
        def _():
            total[...] = term

        @pl.when(chunk > 0)
        def _():
            total[...] += term
        return 0

    lax.fori_loop(0, z.chunks, one_chunk, 0)


def write_filtered(z, pos, total, filt, out):
    for i in range(z.rows):
        for s in range(z.kf):
            j = filt[i * z.kf + s] - pos[1] * z.bc
            out[i, s] = total[i * z.bs:(i + 1) * z.bs, lanes(z, j)].astype(out.dtype)


def mixed_kernel(z, *refs):
    pos, idx, filt = refs[:3]
    left_in = refs[3:3 + z.n_col]
    right_in = refs[3 + z.n_col:3 + z.n_col + z.n_row]
    rest = refs[3 + z.n_col + z.n_row:]
    mixed, direct = rest[:2]
    parts = rest[2:2 + z.n_row]
    left_buf, right_buf, left_dense, right_dense, total, turned, column, left_sem, right_sem = rest[2 + z.n_row:]
    start_pieces(z, pos, left_in, right_in, left_buf, right_buf, left_sem, right_sem)
    fill_right(z, pos, idx, hamilton_col, z.kh, right_buf, right_sem, right_dense)
    multiply_panels(z, pos, idx, left_buf, left_sem, left_dense, right_dense, total)

    for i in range(z.rows):
        rows = slice(i * z.bs, (i + 1) * z.bs)
        for j in range(z.bc):
            cols = slice(j * z.bs, (j + 1) * z.bs)
            turned[cols, rows] = total[rows, cols].T.astype(turned.dtype)

    step = 2
    for n in range(z.n_row):
        row = pos[0] ^ n
        first = row * (z.chunks // z.n_row)

        def one_chunk(chunk, _, n=n, row=row, first=first):
            if z.dense_slots > 1:
                slot = first + chunk
            else:
                slot = fill_left(z, pos, idx, first + chunk, left_buf, left_dense, None)

            def one_step(t, _):
                here = pl.ds(pl.multiple_of(t * step * z.bs, step * z.bs), step * z.bs)
                column[...] = jnp.dot(turned[...], left_dense[slot, :, here], preferred_element_type=jnp.float32)
                for b in range(step):
                    i = chunk * z.groups * z.bc + t * step + b
                    for s in range(z.ka):
                        j = density_col(z, idx, row, pos[1], i, s) - pos[1] * z.bc
                        parts[n][i, s] = column[lanes(z, j), b * z.bs:(b + 1) * z.bs].astype(parts[n].dtype)
                return 0

            lax.fori_loop(0, z.groups * z.bc // step, one_step, 0)
            return 0

        lax.fori_loop(0, z.chunks // z.n_row, one_chunk, 0)

    write_filtered(z, pos, total, filt, mixed)
    for i in range(z.rows):
        for s in range(z.ka):
            j = density_col(z, idx, pos[0], pos[1], i, s) - pos[1] * z.bc
            direct[i, s] = total[i * z.bs:(i + 1) * z.bs, lanes(z, j)]


def square_kernel(z, *refs):
    pos, idx, filt = refs[:3]
    left_in = refs[3:3 + z.n_col]
    right_in = refs[3 + z.n_col:3 + z.n_col + z.n_row]
    squared = refs[4 + z.n_col + z.n_row]
    left_buf, right_buf, left_dense, right_dense, total, left_sem, right_sem = refs[5 + z.n_col + z.n_row:]
    start_pieces(z, pos, left_in, right_in, left_buf, right_buf, left_sem, right_sem)
    fill_right(z, pos, idx, density_col, z.ka, right_buf, right_sem, right_dense)
    multiply_panels(z, pos, idx, left_buf, left_sem, left_dense, right_dense, total)
    write_filtered(z, pos, total, filt, squared)


def gradient_kernel(z, *refs):
    direct, parts, out = refs[0], refs[1:1 + z.n_row], refs[1 + z.n_row]
    for i in range(z.rows):
        for s in range(z.ka):
            cubic = parts[0][i, s].astype(jnp.float32)
            for n in range(1, z.n_row):
                cubic += parts[n][i, s].astype(jnp.float32)
            out[i, s] = (3.0 * direct[i, s] - 2.0 * cubic.T).astype(out.dtype)


def common_scratch(z, count):
    bf16, block = jnp.bfloat16, (z.bs, z.bs)
    return [
        pltpu.VMEM((z.n_col, z.rows, z.ka) + block, bf16),
        pltpu.VMEM((z.n_row, z.rows, count) + block, bf16),
        pltpu.VMEM((z.dense_slots, z.rows * z.bs, z.groups * z.wide), bf16),
        pltpu.VMEM((z.nb, z.bs, z.wide), bf16),
        pltpu.VMEM((z.rows * z.bs, z.wide), jnp.float32),
    ]


def local(n_row, n_col, density, density_cols, hamilton, hamilton_cols, filter_cols):
    z = Sizes(n_row, n_col, density, hamilton, filter_cols)
    n_chip = n_col // 2
    block = (z.bs, z.bs)

    def over_row(x, flip):
        return lax.ppermute(x, "row", [(r, r ^ flip) for r in range(n_row)])

    def next_chip(x):
        return lax.ppermute(x, "col", [(c, (c + 2) % n_col) for c in range(n_col)])

    def other_core(x):
        return lax.ppermute(x, "col", [(c, c ^ 1) for c in range(n_col)])

    left = []
    piece = density
    for step in range(n_chip):
        if step:
            piece = next_chip(piece)
        left += [piece, other_core(piece)]
    d_right, h_right = [density], [hamilton]
    for flip in range(1, n_row):
        high, low = 1 << (flip.bit_length() - 1), flip & -flip
        d_right.append(over_row(d_right[flip - high], high))
        h_right.append(over_row(h_right[flip - low], low))

    cols = jnp.concatenate([density_cols, hamilton_cols], axis=1).reshape(-1)
    idx = lax.all_gather(cols, ("row", "col"), axis=0, tiled=True)
    pos = jnp.stack([lax.axis_index("row"), lax.axis_index("col")]).astype(jnp.int32)
    filt = filter_cols.reshape(-1)

    smem = pl.BlockSpec(memory_space=pltpu.SMEM)
    vmem = pl.BlockSpec(memory_space=pltpu.VMEM)
    anywhere = pl.BlockSpec(memory_space=pl.ANY)
    params = pltpu.CompilerParams(vmem_limit_bytes=VMEM_LIMIT)
    flops = 2 * z.rows * z.bs * z.nb * z.bs * z.wide
    sems = [pltpu.SemaphoreType.DMA((n_col,)), pltpu.SemaphoreType.DMA((n_row,))]
    part = jax.ShapeDtypeStruct((z.rows, z.ka) + block, jnp.bfloat16)
    mixed, direct, *parts = pl.pallas_call(
        functools.partial(mixed_kernel, z),
        out_shape=[
            jax.ShapeDtypeStruct((z.rows, z.kf) + block, jnp.bfloat16),
            jax.ShapeDtypeStruct((z.rows, z.ka) + block, jnp.float32),
        ] + [part] * n_row,
        in_specs=[smem] * 3 + [anywhere] * (n_col + n_row),
        out_specs=[vmem] * (2 + n_row),
        scratch_shapes=common_scratch(z, z.kh) + [
            pltpu.VMEM((z.wide, z.rows * z.bs), jnp.bfloat16),
            pltpu.VMEM((z.wide, 2 * z.bs), jnp.float32),
        ] + sems,
        compiler_params=params,
        cost_estimate=pl.CostEstimate(flops=2 * flops, bytes_accessed=12 << 20, transcendentals=0),
        name="mixed",
    )(pos, idx, filt, *left, *h_right)
    received = [over_row(parts[n], n) for n in range(1, n_row)]
    squared = pl.pallas_call(
        functools.partial(square_kernel, z),
        out_shape=jax.ShapeDtypeStruct((z.rows, z.kf) + block, jnp.bfloat16),
        in_specs=[smem] * 3 + [anywhere] * (n_col + n_row + 1),
        out_specs=vmem,
        scratch_shapes=common_scratch(z, z.ka) + sems,
        compiler_params=params,
        cost_estimate=pl.CostEstimate(flops=flops, bytes_accessed=8 << 20, transcendentals=0),
        name="squared",
    )(pos, idx, filt, *left, *d_right, direct)
    gradient = pl.pallas_call(
        functools.partial(gradient_kernel, z),
        out_shape=jax.ShapeDtypeStruct((z.rows, z.ka) + block, jnp.bfloat16),
        in_specs=[vmem] * (1 + n_row),
        out_specs=vmem,
        compiler_params=params,
        name="gradient",
    )(direct, parts[0], *received)
    return squared, mixed, gradient


def solution(mesh):
    spec4 = P("row", "col", None, None)
    spec2 = P("row", "col")
    body = functools.partial(local, mesh.shape["row"], mesh.shape["col"])
    return jax.shard_map(
        body,
        mesh=mesh,
        in_specs=(spec4, spec2, spec4, spec2, spec2),
        out_specs=(spec4, spec4, spec4),
        check_vma=False,
    )
```

```python
import functools

import jax
import jax.numpy as jnp
from jax import lax
from jax.experimental import pallas as pl
from jax.experimental.pallas import tpu as pltpu
from jax.sharding import PartitionSpec as P

VMEM_LIMIT = 52 * 1024 * 1024
TAIL = 16
BF16, F32 = jnp.bfloat16, jnp.float32


class Sizes:
    def __init__(self, n_row, n_col, density, hamilton, filt):
        self.n_row, self.n_col, self.n_chip = n_row, n_col, n_col // 2
        self.rows, self.ka, self.bs = density.shape[0], density.shape[1], density.shape[2]
        self.kh, self.kf = hamilton.shape[1], filt.shape[1]
        self.nb = self.rows * n_row
        self.bc = self.nb // n_col
        self.tall, self.wide = self.rows * self.bs, self.bc * self.bs
        self.n_first = n_col - 2


def lanes(z, block):
    return pl.ds(pl.multiple_of(block * z.bs, z.bs), z.bs)


def block_rows(z, i, s, slots):
    return slice((i * slots + s) * z.bs, (i * slots + s + 1) * z.bs)


def piece_col(z, n):
    me = lax.axis_index("col")
    step, core = n // 2, lax.rem(me, 2) ^ (n % 2)
    up = lax.rem(me // 2 + step, z.n_chip)
    down = lax.rem(me // 2 + z.n_chip - step, z.n_chip)
    return jnp.where(core == 0, down, up) * 2 + core


def piece_of(z, col):
    me = lax.axis_index("col")
    chip, core = col // 2, lax.rem(col, 2)
    ahead = lax.rem(chip - me // 2 + z.n_chip, z.n_chip)
    behind = lax.rem(me // 2 - chip + z.n_chip, z.n_chip)
    return jnp.where(core == 0, behind, ahead) * 2 + (core ^ lax.rem(me, 2))


def pack_kernel(z, d_in, h_in, d_cols, h_cols, d_out, h_out, wide_tail, tail, sems):
    n = d_in.shape[0]
    m = h_in.shape[0]
    copies = [
        pltpu.make_async_copy(d_in, d_out.at[pl.ds(0, n)], sems.at[0]),
        pltpu.make_async_copy(h_in, h_out.at[pl.ds(0, m)], sems.at[1]),
    ]
    for copy in copies:
        copy.start()
    wide_tail[...] = jnp.zeros_like(wide_tail)
    wide_tail[0:z.ka, 0:z.rows] = d_cols[...].astype(F32)
    wide_tail[z.ka:z.ka + z.kh, 0:z.rows] = h_cols[...].astype(F32)
    tail[...] = wide_tail[...].astype(BF16)
    tails = [
        pltpu.make_async_copy(tail, d_out.at[pl.ds(n, TAIL)], sems.at[2]),
        pltpu.make_async_copy(tail, h_out.at[pl.ds(m, TAIL)], sems.at[3]),
    ]
    for copy in tails:
        copy.start()
    for copy in copies + tails:
        copy.wait()


def read_tails(ins, blocks, tails, ints, idx, sems, int_sem):
    copies = [
        pltpu.make_async_copy(ref.at[pl.ds(rows, TAIL)], tails.at[n], sems.at[n])
        for n, (ref, rows) in enumerate(zip(ins, blocks))
    ]
    for copy in copies:
        copy.start()
    for copy in copies:
        copy.wait()
    ints[...] = tails[:, 0:8, :].astype(F32).astype(jnp.int32)
    copy = pltpu.make_async_copy(ints, idx, int_sem)
    copy.start()
    copy.wait()


def fill_left(z, idx, n, col, buf, dense):
    zero = jnp.zeros((z.bs, z.wide), BF16)
    for i in range(z.rows):
        rows = slice(i * z.bs, (i + 1) * z.bs)
        dense[rows, :] = zero
        for s in range(z.ka):
            k = idx[n, s, i] - col * z.bc
            dense[rows, lanes(z, k)] = buf[block_rows(z, i, s, z.ka), :]


def fill_right(z, first_slot, slots, idx, row_of, buf, dense):
    dense[...] = jnp.zeros_like(dense)
    me = lax.axis_index("col")

    def one(p, _):
        for i in range(z.rows):
            k = row_of(p) * z.rows + i
            n = piece_of(z, k // z.bc)
            at = pl.ds(pl.multiple_of((n * z.bc + lax.rem(k, z.bc)) * z.bs, z.bs), z.bs)
            for s in range(slots):
                j = idx[p, first_slot + s, i] - me * z.bc
                dense[at, lanes(z, j)] = buf[p, block_rows(z, i, s, slots), :]
        return 0

    lax.fori_loop(0, z.n_row, one, 0)


def first_kernel(z, *refs):
    left_in, right_in, rest = refs[:z.n_first], refs[z.n_first:z.n_first + z.n_row], refs[z.n_first + z.n_row:]
    total, panel, right_last, table = rest[:4]
    left_buf, right_buf, dense, right, tails, ints, idx, left_sem, right_sem, tail_sem, out_sem, int_sem = rest[4:]
    d_rows, h_rows = z.rows * z.ka * z.bs, z.rows * z.kh * z.bs
    copies = [
        pltpu.make_async_copy(ref.at[pl.ds(0, h_rows)], right_buf.at[n], right_sem.at[n])
        for n, ref in enumerate(right_in)
    ] + [
        pltpu.make_async_copy(ref.at[pl.ds(0, d_rows)], left_buf.at[n], left_sem.at[n])
        for n, ref in enumerate(left_in)
    ]
    for copy in copies:
        copy.start()
    read_tails(right_in + left_in, [h_rows] * z.n_row + [d_rows] * z.n_first, tails, ints, idx, tail_sem, int_sem)
    table[...] = ints[0:z.n_row]
    for copy in copies[:z.n_row]:
        copy.wait()
    fill_right(z, z.ka, z.kh, idx, lambda p: lax.axis_index("row") ^ p, right_buf, right)
    outs = []
    for n in range(z.n_first):
        copies[z.n_row + n].wait()
        here = dense.at[:, n * z.wide:(n + 1) * z.wide]
        fill_left(z, idx, z.n_row + n, piece_col(z, n), left_buf.at[n], here)
        outs.append(pltpu.make_async_copy(here, panel.at[n], out_sem.at[n]))
        outs[-1].start()
    deep = z.n_first * z.wide
    half = z.tall // 2
    for m in range(2):
        rows = slice(m * half, (m + 1) * half)
        total[rows, :] = jnp.dot(dense[rows, :], right[0:deep, :], preferred_element_type=F32)
    right_last[...] = right[deep:, :]
    for copy in outs:
        copy.wait()


def parts_kernel(z, *refs):
    table, left_in, right_in, total_in, panel = refs[0], refs[1:3], refs[3], refs[4], refs[5]
    total_out, turned_out, panel_last = refs[6:9]
    parts = refs[9:9 + z.n_row - 1]
    (left_buf, last, right, total, dense, turned, columns, part_buf, tails, ints, idx,
     sems, dense_sem, tail_sem, out_sem, part_sem, int_sem) = refs[9 + z.n_row - 1:]
    d_rows = z.rows * z.ka * z.bs
    copies = [
        pltpu.make_async_copy(left_in[0].at[pl.ds(0, d_rows)], left_buf.at[0], sems.at[0]),
        pltpu.make_async_copy(left_in[1].at[pl.ds(0, d_rows)], left_buf.at[1], sems.at[1]),
        pltpu.make_async_copy(right_in, right, sems.at[2]),
        pltpu.make_async_copy(total_in, total, sems.at[3]),
    ]
    for copy in copies:
        copy.start()
    loads = [pltpu.make_async_copy(panel.at[n], dense.at[n], dense_sem.at[n]) for n in range(z.n_first)]
    for copy in loads:
        copy.start()
    read_tails(left_in, [d_rows] * 2, tails, ints, idx, tail_sem, int_sem)
    outs = []
    for n in range(2):
        copies[n].wait()
        here = last.at[:, n * z.wide:(n + 1) * z.wide]
        fill_left(z, idx, n, piece_col(z, z.n_first + n), left_buf.at[n], here)
        outs.append(pltpu.make_async_copy(here, panel_last.at[n], out_sem.at[n]))
        outs[-1].start()
        dense[z.n_first + n] = here[...]
    copies[2].wait()
    copies[3].wait()
    half = z.tall // 2
    for m in range(2):
        rows = slice(m * half, (m + 1) * half)
        total[rows, :] += jnp.dot(last[rows, :], right[...], preferred_element_type=F32)
    outs.append(pltpu.make_async_copy(total, total_out, out_sem.at[2]))
    outs[-1].start()
    for i in range(z.rows):
        rows = slice(i * z.bs, (i + 1) * z.bs)
        for j in range(z.bc):
            cols = slice(j * z.bs, (j + 1) * z.bs)
            turned[cols, rows] = total[rows, cols].T.astype(BF16)
    outs.append(pltpu.make_async_copy(turned, turned_out, out_sem.at[3]))
    outs[-1].start()
    for copy in loads:
        copy.wait()
    for n in reversed(range(1, z.n_row)):
        one_part(z, table, n, turned, dense, columns, part_buf.at[n - 1])
        outs.append(pltpu.make_async_copy(part_buf.at[n - 1], parts[n - 1], part_sem.at[n - 1]))
        outs[-1].start()
    for copy in outs:
        copy.wait()


def one_part(z, table, n, turned, dense, columns, out):
    row = lax.axis_index("row") ^ n
    per = z.n_col // z.n_row
    for t in range(per):
        column = columns.at[t % 2]
        column[...] = jnp.dot(turned[...], dense[piece_of(z, row * per + t)], preferred_element_type=F32)
        for b in range(z.bc):
            i = t * z.bc + b
            for s in range(z.ka):
                j = table[n, s, i] - lax.axis_index("col") * z.bc
                out[i, s] = column[lanes(z, j), b * z.bs:(b + 1) * z.bs].astype(out.dtype)


def square_kernel(z, *refs):
    table, filt = refs[:2]
    right_in, panel, panel_last, total_in, turned_in = refs[2:2 + z.n_row], *refs[2 + z.n_row:6 + z.n_row]
    squared, mixed, base = refs[6 + z.n_row:9 + z.n_row]
    right_buf, right, dense, total, turned, columns, own, right_sem, sems, dense_sem = refs[9 + z.n_row:]
    copies = [pltpu.make_async_copy(ref, right_buf.at[n], right_sem.at[n]) for n, ref in enumerate(right_in)]
    small = [
        pltpu.make_async_copy(total_in, total, sems.at[0]),
        pltpu.make_async_copy(turned_in, turned, sems.at[1]),
    ]
    loads = [pltpu.make_async_copy(panel.at[n], dense.at[n], dense_sem.at[n]) for n in range(z.n_first)]
    loads += [
        pltpu.make_async_copy(panel_last.at[n], dense.at[z.n_first + n], dense_sem.at[z.n_first + n]) for n in range(2)
    ]
    for copy in small + copies + loads:
        copy.start()
    me = lax.axis_index("col")
    small[0].wait()
    for i in range(z.rows):
        rows = slice(i * z.bs, (i + 1) * z.bs)
        for s in range(z.kf):
            mixed[i, s] = total[rows, lanes(z, filt[s, i] - me * z.bc)].astype(mixed.dtype)
    small[1].wait()
    for copy in loads:
        copy.wait()
    one_part(z, table, 0, turned, dense, columns, own)
    for i in range(z.rows):
        rows = slice(i * z.bs, (i + 1) * z.bs)
        for s in range(z.ka):
            direct = total[rows, lanes(z, table[0, s, i] - me * z.bc)]
            base[i, s] = 3.0 * direct - 2.0 * own[i, s].T
    for copy in copies:
        copy.wait()
    fill_right(z, 0, z.ka, table, lambda p: lax.axis_index("row") ^ p, right_buf, right)
    half = z.tall // 2
    for m in range(2):
        rows = slice(m * half, (m + 1) * half)
        left = jnp.concatenate([dense[n, rows, :] for n in range(z.n_col)], axis=1)
        total[rows, :] = jnp.dot(left, right[...], preferred_element_type=F32)
    for i in range(z.rows):
        rows = slice(i * z.bs, (i + 1) * z.bs)
        for s in range(z.kf):
            squared[i, s] = total[rows, lanes(z, filt[s, i] - me * z.bc)].astype(squared.dtype)


def gradient_kernel(z, base, *refs):
    parts, out = refs[:z.n_row - 1], refs[z.n_row - 1]
    for i in range(z.rows):
        for s in range(z.ka):
            cubic = parts[0][i, s].astype(F32)
            for n in range(1, z.n_row - 1):
                cubic += parts[n][i, s].astype(F32)
            out[i, s] = (base[i, s] - 2.0 * cubic.T).astype(out.dtype)


def local(n_row, n_col, density, density_cols, hamilton, hamilton_cols, filter_cols):
    z = Sizes(n_row, n_col, density, hamilton, filter_cols)
    block = (z.bs, z.bs)
    shape = jax.ShapeDtypeStruct
    smem = pl.BlockSpec(memory_space=pltpu.SMEM)
    vmem = pl.BlockSpec(memory_space=pltpu.VMEM)
    anywhere = pl.BlockSpec(memory_space=pl.ANY)
    params = pltpu.CompilerParams(vmem_limit_bytes=VMEM_LIMIT)
    dma = pltpu.SemaphoreType.DMA
    d_rows, h_rows = z.rows * z.ka * z.bs, z.rows * z.kh * z.bs
    panel_flops = 2 * z.tall * z.wide * z.nb * z.bs

    def over_row(x, flip):
        return lax.ppermute(x, "row", [(r, r ^ flip) for r in range(n_row)])

    def next_chip(x):
        pairs = [(2 * p, 2 * ((p + 1) % z.n_chip)) for p in range(z.n_chip)]
        pairs += [(2 * p + 1, 2 * ((p - 1) % z.n_chip) + 1) for p in range(z.n_chip)]
        return lax.ppermute(x, "col", pairs)

    def other_core(x):
        return lax.ppermute(x, "col", [(c, c ^ 1) for c in range(n_col)])

    flat = density.reshape(d_rows, z.bs)
    d_pay, h_pay = pl.pallas_call(
        functools.partial(pack_kernel, z),
        out_shape=[shape((d_rows + TAIL, z.bs), BF16), shape((h_rows + TAIL, z.bs), BF16)],
        in_specs=[anywhere, anywhere, vmem, vmem],
        out_specs=[anywhere, anywhere],
        scratch_shapes=[pltpu.VMEM((TAIL, z.bs), F32), pltpu.VMEM((TAIL, z.bs), BF16), dma((4,))],
        name="pack",
    )(flat, hamilton.reshape(h_rows, z.bs), density_cols.T, hamilton_cols.T)

    pieces, d_right, h_right = [d_pay], {0: flat}, {0: h_pay}
    left = [d_pay]
    for step in range(1, z.n_chip):
        pieces.append(next_chip(pieces[-1]))
        for flip in range(1, n_row):
            bits, low = flip.bit_count(), flip & -flip
            if bits == step:
                h_right[flip] = over_row(h_right[flip - low], low)
            if (step == 2 and flip == 1) or (step == 3 and bits == 1 and flip > 1):
                d_right[flip] = over_row(d_right[flip - low], low)
        left.append(other_core(left[-1]))
        if step < z.n_chip - 1:
            pieces[-1], left, d_right, h_right = lax.optimization_barrier((pieces[-1], left, d_right, h_right))
        left.append(pieces[-1])
    h_right = [h_right[flip] for flip in range(n_row)]

    total, panel, right_last, table = pl.pallas_call(
        functools.partial(first_kernel, z),
        out_shape=[
            shape((z.tall, z.wide), F32),
            shape((z.n_first, z.tall, z.wide), BF16),
            shape((2 * z.wide, z.wide), BF16),
            shape((n_row, 8, z.bs), jnp.int32),
        ],
        in_specs=[anywhere] * (z.n_first + n_row),
        out_specs=[vmem, anywhere, vmem, vmem],
        scratch_shapes=[
            pltpu.VMEM((z.n_first, d_rows, z.bs), BF16),
            pltpu.VMEM((n_row, h_rows, z.bs), BF16),
            pltpu.VMEM((z.tall, z.n_first * z.wide), BF16),
            pltpu.VMEM((z.nb * z.bs, z.wide), BF16),
            pltpu.VMEM((z.n_first + n_row, TAIL, z.bs), BF16),
            pltpu.VMEM((z.n_first + n_row, 8, z.bs), jnp.int32),
            pltpu.SMEM((z.n_first + n_row, 8, z.bs), jnp.int32),
            dma((z.n_first,)), dma((n_row,)), dma((z.n_first + n_row,)), dma((z.n_first,)), dma,
        ],
        compiler_params=params,
        cost_estimate=pl.CostEstimate(flops=panel_flops, bytes_accessed=16 << 20, transcendentals=0),
        name="first",
    )(*left[:z.n_first], *h_right)
    last, total, d_right = lax.optimization_barrier((left[-1], total, d_right))
    for flip in range(1, n_row):
        if flip not in d_right:
            d_right[flip] = over_row(d_right[flip & (flip - 1)], flip & -flip)
    d_right = [d_right[flip] for flip in range(n_row)]
    left = [last, other_core(last)]
    part = shape((z.rows, z.ka) + block, BF16)
    total, turned, panel_last, *parts = pl.pallas_call(
        functools.partial(parts_kernel, z),
        out_shape=[
            shape((z.tall, z.wide), F32),
            shape((z.wide, z.tall), BF16),
            shape((2, z.tall, z.wide), BF16),
        ] + [part] * (n_row - 1),
        in_specs=[smem] + [anywhere] * 5,
        out_specs=[anywhere] * (2 + n_row),
        scratch_shapes=[
            pltpu.VMEM((2, d_rows, z.bs), BF16),
            pltpu.VMEM((z.tall, 2 * z.wide), BF16),
            pltpu.VMEM((2 * z.wide, z.wide), BF16),
            pltpu.VMEM((z.tall, z.wide), F32),
            pltpu.VMEM((n_col, z.tall, z.wide), BF16),
            pltpu.VMEM((z.wide, z.tall), BF16),
            pltpu.VMEM((2, z.wide, z.wide), F32),
            pltpu.VMEM((n_row - 1, z.rows, z.ka) + block, BF16),
            pltpu.VMEM((2, TAIL, z.bs), BF16),
            pltpu.VMEM((2, 8, z.bs), jnp.int32),
            pltpu.SMEM((2, 8, z.bs), jnp.int32),
            dma((4,)), dma((z.n_first,)), dma((2,)), dma((4,)), dma((n_row - 1,)), dma,
        ],
        compiler_params=params,
        cost_estimate=pl.CostEstimate(flops=panel_flops, bytes_accessed=16 << 20, transcendentals=0),
        name="parts",
    )(table, *left, right_last, total, panel)
    received = [over_row(parts[n - 1], n) for n in range(1, n_row)]
    squared, mixed, base = pl.pallas_call(
        functools.partial(square_kernel, z),
        out_shape=[
            shape((z.rows, z.kf) + block, BF16),
            shape((z.rows, z.kf) + block, BF16),
            shape((z.rows, z.ka) + block, F32),
        ],
        in_specs=[smem] * 2 + [anywhere] * (n_row + 4),
        out_specs=[vmem] * 3,
        scratch_shapes=[
            pltpu.VMEM((n_row, d_rows, z.bs), BF16),
            pltpu.VMEM((z.nb * z.bs, z.wide), BF16),
            pltpu.VMEM((n_col, z.tall, z.wide), BF16),
            pltpu.VMEM((z.tall, z.wide), F32),
            pltpu.VMEM((z.wide, z.tall), BF16),
            pltpu.VMEM((2, z.wide, z.wide), F32),
            pltpu.VMEM((z.rows, z.ka) + block, F32),
            dma((n_row,)), dma((2,)), dma((n_col,)),
        ],
        compiler_params=params,
        cost_estimate=pl.CostEstimate(flops=2 * panel_flops, bytes_accessed=16 << 20, transcendentals=0),
        name="squared",
    )(table, filter_cols.T, *d_right, panel, panel_last, total, turned)
    gradient = pl.pallas_call(
        functools.partial(gradient_kernel, z),
        out_shape=part,
        in_specs=[vmem] * n_row,
        out_specs=vmem,
        name="gradient",
    )(base, *received)
    return squared, mixed, gradient


def solution(mesh):
    spec4 = P("row", "col", None, None)
    spec2 = P("row", "col")
    body = functools.partial(local, mesh.shape["row"], mesh.shape["col"])
    return jax.shard_map(
        body,
        mesh=mesh,
        in_specs=(spec4, spec2, spec4, spec2, spec2),
        out_specs=(spec4, spec4, spec4),
        check_vma=False,
    )
```

```python
import functools
import math

import jax
import jax.numpy as jnp
from jax import lax
from jax.experimental import pallas as pl
from jax.experimental.pallas import tpu as pltpu
from jax.sharding import PartitionSpec as P

VMEM_ROOM = 6 * 1024 * 1024
TAIL = 16
BF16, F32 = jnp.bfloat16, jnp.float32


class Sizes:
    def __init__(self, n_row, n_col, density, hamilton, filt):
        self.n_row, self.n_col, self.n_chip = n_row, n_col, n_col // 2
        self.rows, self.ka, self.bs = density.shape[0], density.shape[1], density.shape[2]
        self.kh, self.kf = hamilton.shape[1], filt.shape[1]
        self.nb = self.rows * n_row
        self.bc = self.nb // n_col
        self.tall, self.wide = self.rows * self.bs, self.bc * self.bs
        self.n_first = n_col - 2


def call(kernel, z, ins, outs, scratch, in_specs, out_specs, flops, name):
    held = [x for x in scratch if getattr(x, "memory_space", None) == pltpu.VMEM]
    held += [x for x, spec in zip(list(ins) + outs, in_specs + out_specs) if spec.memory_space == pltpu.VMEM]
    size = sum(math.prod(x.shape) * jnp.dtype(x.dtype).itemsize for x in held)
    return pl.pallas_call(
        functools.partial(kernel, z),
        out_shape=outs,
        in_specs=in_specs,
        out_specs=out_specs,
        scratch_shapes=scratch,
        compiler_params=pltpu.CompilerParams(vmem_limit_bytes=size + VMEM_ROOM),
        cost_estimate=pl.CostEstimate(flops=flops, bytes_accessed=16 << 20, transcendentals=0),
        name=name,
    )(*ins)


def lanes(z, block):
    return pl.ds(pl.multiple_of(block * z.bs, z.bs), z.bs)


def block_rows(z, i, s, slots):
    return slice((i * slots + s) * z.bs, (i * slots + s + 1) * z.bs)


def piece_col(z, n):
    me = lax.axis_index("col")
    step, core = n // 2, lax.rem(me, 2) ^ (n % 2)
    up = lax.rem(me // 2 + step, z.n_chip)
    down = lax.rem(me // 2 + z.n_chip - step, z.n_chip)
    return jnp.where(core == 0, down, up) * 2 + core


def piece_of(z, col):
    me = lax.axis_index("col")
    chip, core = col // 2, lax.rem(col, 2)
    ahead = lax.rem(chip - me // 2 + z.n_chip, z.n_chip)
    behind = lax.rem(me // 2 - chip + z.n_chip, z.n_chip)
    return jnp.where(core == 0, behind, ahead) * 2 + (core ^ lax.rem(me, 2))


def pack_kernel(z, d_in, h_in, d_cols, h_cols, d_out, h_out, tail):
    tail[...] = jnp.zeros_like(tail)
    tail[0:z.ka, 0:z.rows] = d_cols[...].astype(F32)
    tail[z.ka:z.ka + z.kh, 0:z.rows] = h_cols[...].astype(F32)
    for ref, out in ((d_in, d_out), (h_in, h_out)):
        rows = ref.shape[0]
        out[0:rows, :] = ref[...]
        out[rows:rows + TAIL, :] = tail[...].astype(BF16)


def read_tails(ins, blocks, tails, ints, idx, sems, int_sem):
    copies = [
        pltpu.make_async_copy(ref.at[pl.ds(rows, TAIL)], tails.at[n], sems.at[n])
        for n, (ref, rows) in enumerate(zip(ins, blocks))
    ]
    for copy in copies:
        copy.start()
    for copy in copies:
        copy.wait()
    ints[...] = tails[:, 0:8, :].astype(F32).astype(jnp.int32)
    copy = pltpu.make_async_copy(ints, idx, int_sem)
    copy.start()
    copy.wait()


def fill_left(z, idx, n, col, buf, dense):
    zero = jnp.zeros((z.bs, z.wide), BF16)
    for i in range(z.rows):
        rows = slice(i * z.bs, (i + 1) * z.bs)
        dense[rows, :] = zero
        for s in range(z.ka):
            k = idx[n, s, i] - col * z.bc
            dense[rows, lanes(z, k)] = buf[block_rows(z, i, s, z.ka), :]


def fill_right(z, first_slot, slots, idx, row_of, buf, dense):
    dense[...] = jnp.zeros_like(dense)
    me = lax.axis_index("col")

    def one(p, _):
        for i in range(z.rows):
            k = row_of(p) * z.rows + i
            n = piece_of(z, k // z.bc)
            at = pl.ds(pl.multiple_of((n * z.bc + lax.rem(k, z.bc)) * z.bs, z.bs), z.bs)
            for s in range(slots):
                j = idx[p, first_slot + s, i] - me * z.bc
                dense[at, lanes(z, j)] = buf[p, block_rows(z, i, s, slots), :]
        return 0

    lax.fori_loop(0, z.n_row, one, 0)


def first_kernel(z, *refs):
    left_in, right_in, rest = refs[:z.n_first], refs[z.n_first:z.n_first + z.n_row], refs[z.n_first + z.n_row:]
    total, panel, right_last, table = rest[:4]
    left_buf, right_buf, dense, right, tails, ints, idx, left_sem, right_sem, tail_sem, out_sem, int_sem = rest[4:]
    d_rows, h_rows = z.rows * z.ka * z.bs, z.rows * z.kh * z.bs
    copies = [
        pltpu.make_async_copy(ref.at[pl.ds(0, h_rows)], right_buf.at[n], right_sem.at[n])
        for n, ref in enumerate(right_in)
    ] + [
        pltpu.make_async_copy(ref.at[pl.ds(0, d_rows)], left_buf.at[n], left_sem.at[n])
        for n, ref in enumerate(left_in)
    ]
    for copy in copies:
        copy.start()
    read_tails(right_in + left_in, [h_rows] * z.n_row + [d_rows] * z.n_first, tails, ints, idx, tail_sem, int_sem)
    table[...] = ints[0:z.n_row]
    for copy in copies[:z.n_row]:
        copy.wait()
    fill_right(z, z.ka, z.kh, idx, lambda p: lax.axis_index("row") ^ p, right_buf, right)
    outs = []
    for n in range(z.n_first):
        copies[z.n_row + n].wait()
        here = dense.at[:, n * z.wide:(n + 1) * z.wide]
        fill_left(z, idx, z.n_row + n, piece_col(z, n), left_buf.at[n], here)
        outs.append(pltpu.make_async_copy(here, panel.at[n], out_sem.at[n]))
        outs[-1].start()
    deep = z.n_first * z.wide
    half = z.tall // 2
    for m in range(2):
        rows = slice(m * half, (m + 1) * half)
        total[rows, :] = jnp.dot(dense[rows, :], right[0:deep, :], preferred_element_type=F32)
    right_last[...] = right[deep:, :]
    for copy in outs:
        copy.wait()


def parts_kernel(z, *refs):
    table, left_in, right_in, total_in, panel = refs[0], refs[1:3], refs[3], refs[4], refs[5]
    total_out, turned_out, panel_last = refs[6:9]
    parts = refs[9:9 + z.n_row - 1]
    (left_buf, last, right, total, dense, turned, columns, part_buf, tails, ints, idx,
     sems, dense_sem, tail_sem, out_sem, part_sem, int_sem) = refs[9 + z.n_row - 1:]
    d_rows = z.rows * z.ka * z.bs
    copies = [
        pltpu.make_async_copy(left_in[0].at[pl.ds(0, d_rows)], left_buf.at[0], sems.at[0]),
        pltpu.make_async_copy(left_in[1].at[pl.ds(0, d_rows)], left_buf.at[1], sems.at[1]),
        pltpu.make_async_copy(right_in, right, sems.at[2]),
        pltpu.make_async_copy(total_in, total, sems.at[3]),
    ]
    for copy in copies:
        copy.start()
    loads = [pltpu.make_async_copy(panel.at[n], dense.at[n], dense_sem.at[n]) for n in range(z.n_first)]
    for copy in loads:
        copy.start()
    read_tails(left_in, [d_rows] * 2, tails, ints, idx, tail_sem, int_sem)
    outs = []
    for n in range(2):
        copies[n].wait()
        here = last.at[:, n * z.wide:(n + 1) * z.wide]
        fill_left(z, idx, n, piece_col(z, z.n_first + n), left_buf.at[n], here)
        outs.append(pltpu.make_async_copy(here, panel_last.at[n], out_sem.at[n]))
        outs[-1].start()
        dense[z.n_first + n] = here[...]
    copies[2].wait()
    copies[3].wait()
    half = z.tall // 2
    for m in range(2):
        rows = slice(m * half, (m + 1) * half)
        total[rows, :] += jnp.dot(last[rows, :], right[...], preferred_element_type=F32)
    outs.append(pltpu.make_async_copy(total, total_out, out_sem.at[2]))
    outs[-1].start()
    for i in range(z.rows):
        rows = slice(i * z.bs, (i + 1) * z.bs)
        for j in range(z.bc):
            cols = slice(j * z.bs, (j + 1) * z.bs)
            turned[cols, rows] = total[rows, cols].T.astype(BF16)
    outs.append(pltpu.make_async_copy(turned, turned_out, out_sem.at[3]))
    outs[-1].start()
    for copy in loads:
        copy.wait()
    for n in reversed(range(1, z.n_row)):
        one_part(z, table, n, turned, dense, columns, part_buf.at[n - 1])
        outs.append(pltpu.make_async_copy(part_buf.at[n - 1], parts[n - 1], part_sem.at[n - 1]))
        outs[-1].start()
    for copy in outs:
        copy.wait()


def one_part(z, table, n, turned, dense, columns, out):
    row = lax.axis_index("row") ^ n
    per = z.n_col // z.n_row
    for t in range(per):
        column = columns.at[t % 2]
        column[...] = jnp.dot(turned[...], dense[piece_of(z, row * per + t)], preferred_element_type=F32)
        for b in range(z.bc):
            i = t * z.bc + b
            for s in range(z.ka):
                j = table[n, s, i] - lax.axis_index("col") * z.bc
                out[i, s] = column[lanes(z, j), b * z.bs:(b + 1) * z.bs].astype(out.dtype)


def square_kernel(z, *refs):
    table, filt = refs[:2]
    right_in, panel, panel_last, total_in, turned_in = refs[2:2 + z.n_row], *refs[2 + z.n_row:6 + z.n_row]
    squared, mixed, base = refs[6 + z.n_row:9 + z.n_row]
    right_buf, right, dense, total, turned, columns, own, right_sem, sems, dense_sem = refs[9 + z.n_row:]
    copies = [pltpu.make_async_copy(ref, right_buf.at[n], right_sem.at[n]) for n, ref in enumerate(right_in)]
    small = [
        pltpu.make_async_copy(total_in, total, sems.at[0]),
        pltpu.make_async_copy(turned_in, turned, sems.at[1]),
    ]
    loads = [pltpu.make_async_copy(panel.at[n], dense.at[n], dense_sem.at[n]) for n in range(z.n_first)]
    loads += [
        pltpu.make_async_copy(panel_last.at[n], dense.at[z.n_first + n], dense_sem.at[z.n_first + n]) for n in range(2)
    ]
    for copy in small + copies + loads:
        copy.start()
    me = lax.axis_index("col")
    small[0].wait()
    for i in range(z.rows):
        rows = slice(i * z.bs, (i + 1) * z.bs)
        for s in range(z.kf):
            mixed[i, s] = total[rows, lanes(z, filt[s, i] - me * z.bc)].astype(mixed.dtype)
    small[1].wait()
    for copy in loads:
        copy.wait()
    one_part(z, table, 0, turned, dense, columns, own)
    for i in range(z.rows):
        rows = slice(i * z.bs, (i + 1) * z.bs)
        for s in range(z.ka):
            direct = total[rows, lanes(z, table[0, s, i] - me * z.bc)]
            base[i, s] = 3.0 * direct - 2.0 * own[i, s].T
    for copy in copies:
        copy.wait()
    fill_right(z, 0, z.ka, table, lambda p: lax.axis_index("row") ^ p, right_buf, right)
    half = z.tall // 2
    for m in range(2):
        rows = slice(m * half, (m + 1) * half)
        left = jnp.concatenate([dense[n, rows, :] for n in range(z.n_col)], axis=1)
        total[rows, :] = jnp.dot(left, right[...], preferred_element_type=F32)
    for i in range(z.rows):
        rows = slice(i * z.bs, (i + 1) * z.bs)
        for s in range(z.kf):
            squared[i, s] = total[rows, lanes(z, filt[s, i] - me * z.bc)].astype(squared.dtype)


def gradient_kernel(z, base, *refs):
    parts, out = refs[:z.n_row - 1], refs[z.n_row - 1]
    for i in range(z.rows):
        for s in range(z.ka):
            cubic = parts[0][i, s].astype(F32)
            for n in range(1, z.n_row - 1):
                cubic += parts[n][i, s].astype(F32)
            out[i, s] = (base[i, s] - 2.0 * cubic.T).astype(out.dtype)


def local(n_row, n_col, density, density_cols, hamilton, hamilton_cols, filter_cols):
    z = Sizes(n_row, n_col, density, hamilton, filter_cols)
    block = (z.bs, z.bs)
    shape = jax.ShapeDtypeStruct
    smem = pl.BlockSpec(memory_space=pltpu.SMEM)
    vmem = pl.BlockSpec(memory_space=pltpu.VMEM)
    anywhere = pl.BlockSpec(memory_space=pl.ANY)
    dma = pltpu.SemaphoreType.DMA
    d_rows, h_rows = z.rows * z.ka * z.bs, z.rows * z.kh * z.bs
    panel_flops = 2 * z.tall * z.wide * z.nb * z.bs

    def over_row(x, flip):
        return lax.ppermute(x, "row", [(r, r ^ flip) for r in range(n_row)])

    def next_chip(x):
        pairs = [(2 * p, 2 * ((p + 1) % z.n_chip)) for p in range(z.n_chip)]
        pairs += [(2 * p + 1, 2 * ((p - 1) % z.n_chip) + 1) for p in range(z.n_chip)]
        return lax.ppermute(x, "col", pairs)

    def other_core(x):
        return lax.ppermute(x, "col", [(c, c ^ 1) for c in range(n_col)])

    flat = density.reshape(d_rows, z.bs)
    d_pay, h_pay = call(
        pack_kernel, z,
        [flat, hamilton.reshape(h_rows, z.bs), density_cols.T, hamilton_cols.T],
        [shape((d_rows + TAIL, z.bs), BF16), shape((h_rows + TAIL, z.bs), BF16)],
        [pltpu.VMEM((TAIL, z.bs), F32)],
        [vmem] * 4, [vmem] * 2, 0, "pack",
    )

    pieces, d_right, h_right = [d_pay], {0: flat}, {0: h_pay}
    left = [d_pay]
    for step in range(1, z.n_chip):
        pieces.append(next_chip(pieces[-1]))
        for flip in range(1, n_row):
            bits, low, high = flip.bit_count(), flip & -flip, 1 << (flip.bit_length() - 1)
            if bits == step:
                h_right[flip] = over_row(h_right[flip - high], high)
            if (step == 2 and flip == 1) or (step == 3 and bits == 1 and flip > 1):
                d_right[flip] = over_row(d_right[flip - low], low)
        left.append(other_core(left[-1]))
        if step < z.n_chip - 1:
            pieces[-1], left, d_right, h_right = lax.optimization_barrier((pieces[-1], left, d_right, h_right))
        left.append(pieces[-1])
    h_right = [h_right[flip] for flip in range(n_row)]

    n_pay = z.n_first + n_row
    total, panel, right_last, table = call(
        first_kernel, z,
        [*left[:z.n_first], *h_right],
        [
            shape((z.tall, z.wide), F32),
            shape((z.n_first, z.tall, z.wide), BF16),
            shape((2 * z.wide, z.wide), BF16),
            shape((n_row, 8, z.bs), jnp.int32),
        ],
        [
            pltpu.VMEM((z.n_first, d_rows, z.bs), BF16),
            pltpu.VMEM((n_row, h_rows, z.bs), BF16),
            pltpu.VMEM((z.tall, z.n_first * z.wide), BF16),
            pltpu.VMEM((z.nb * z.bs, z.wide), BF16),
            pltpu.VMEM((n_pay, TAIL, z.bs), BF16),
            pltpu.VMEM((n_pay, 8, z.bs), jnp.int32),
            pltpu.SMEM((n_pay, 8, z.bs), jnp.int32),
            dma((z.n_first,)), dma((n_row,)), dma((n_pay,)), dma((z.n_first,)), dma,
        ],
        [anywhere] * n_pay, [vmem, anywhere, vmem, vmem], panel_flops, "first",
    )
    last, total, d_right = lax.optimization_barrier((left[-1], total, d_right))
    for flip in range(1, n_row):
        if flip not in d_right:
            d_right[flip] = over_row(d_right[flip & (flip - 1)], flip & -flip)
    d_right = [d_right[flip] for flip in range(n_row)]
    part = shape((z.rows, z.ka) + block, BF16)
    total, turned, panel_last, *parts = call(
        parts_kernel, z,
        [table, last, other_core(last), right_last, total, panel],
        [
            shape((z.tall, z.wide), F32),
            shape((z.wide, z.tall), BF16),
            shape((2, z.tall, z.wide), BF16),
        ] + [part] * (n_row - 1),
        [
            pltpu.VMEM((2, d_rows, z.bs), BF16),
            pltpu.VMEM((z.tall, 2 * z.wide), BF16),
            pltpu.VMEM((2 * z.wide, z.wide), BF16),
            pltpu.VMEM((z.tall, z.wide), F32),
            pltpu.VMEM((n_col, z.tall, z.wide), BF16),
            pltpu.VMEM((z.wide, z.tall), BF16),
            pltpu.VMEM((2, z.wide, z.wide), F32),
            pltpu.VMEM((n_row - 1, z.rows, z.ka) + block, BF16),
            pltpu.VMEM((2, TAIL, z.bs), BF16),
            pltpu.VMEM((2, 8, z.bs), jnp.int32),
            pltpu.SMEM((2, 8, z.bs), jnp.int32),
            dma((4,)), dma((z.n_first,)), dma((2,)), dma((4,)), dma((n_row - 1,)), dma,
        ],
        [smem] + [anywhere] * 5, [anywhere] * (2 + n_row), panel_flops, "parts",
    )
    received = [over_row(parts[n - 1], n) for n in range(1, n_row)]
    squared, mixed, base = call(
        square_kernel, z,
        [table, filter_cols.T, *d_right, panel, panel_last, total, turned],
        [
            shape((z.rows, z.kf) + block, BF16),
            shape((z.rows, z.kf) + block, BF16),
            shape((z.rows, z.ka) + block, F32),
        ],
        [
            pltpu.VMEM((n_row, d_rows, z.bs), BF16),
            pltpu.VMEM((z.nb * z.bs, z.wide), BF16),
            pltpu.VMEM((n_col, z.tall, z.wide), BF16),
            pltpu.VMEM((z.tall, z.wide), F32),
            pltpu.VMEM((z.wide, z.tall), BF16),
            pltpu.VMEM((2, z.wide, z.wide), F32),
            pltpu.VMEM((z.rows, z.ka) + block, F32),
            dma((n_row,)), dma((2,)), dma((n_col,)),
        ],
        [smem] * 2 + [anywhere] * (n_row + 4), [vmem] * 3, 2 * panel_flops, "squared",
    )
    gradient, = call(gradient_kernel, z, [base, *received], [part], [], [vmem] * n_row, [vmem], 0, "gradient")
    return squared, mixed, gradient


def solution(mesh):
    spec4 = P("row", "col", None, None)
    spec2 = P("row", "col")
    body = functools.partial(local, mesh.shape["row"], mesh.shape["col"])
    return jax.shard_map(
        body,
        mesh=mesh,
        in_specs=(spec4, spec2, spec4, spec2, spec2),
        out_specs=(spec4, spec4, spec4),
        check_vma=False,
    )
```

```python
import functools
import math

import jax
import jax.numpy as jnp
from jax import lax
from jax.experimental import pallas as pl
from jax.experimental.pallas import tpu as pltpu
from jax.sharding import PartitionSpec as P

VMEM_ROOM = 6 * 1024 * 1024
TAIL = 16
BF16, F32 = jnp.bfloat16, jnp.float32


class Sizes:
    def __init__(self, n_row, n_col, density, hamilton, filt):
        self.n_row, self.n_col, self.n_chip = n_row, n_col, n_col // 2
        self.rows, self.ka, self.bs = density.shape[0], density.shape[1], density.shape[2]
        self.kh, self.kf = hamilton.shape[1], filt.shape[1]
        self.nb = self.rows * n_row
        self.bc = self.nb // n_col
        self.tall, self.wide = self.rows * self.bs, self.bc * self.bs
        self.n_first = n_col - 2


def call(kernel, z, ins, outs, scratch, in_specs, out_specs, flops, name):
    held = [x for x in scratch if getattr(x, "memory_space", None) == pltpu.VMEM]
    held += [x for x, spec in zip(list(ins) + outs, in_specs + out_specs) if spec.memory_space == pltpu.VMEM]
    size = sum(math.prod(x.shape) * jnp.dtype(x.dtype).itemsize for x in held)
    return pl.pallas_call(
        functools.partial(kernel, z),
        out_shape=outs,
        in_specs=in_specs,
        out_specs=out_specs,
        scratch_shapes=scratch,
        compiler_params=pltpu.CompilerParams(vmem_limit_bytes=size + VMEM_ROOM),
        cost_estimate=pl.CostEstimate(flops=flops, bytes_accessed=16 << 20, transcendentals=0),
        name=name,
    )(*ins)


def lanes(z, block):
    return pl.ds(pl.multiple_of(block * z.bs, z.bs), z.bs)


def block_rows(z, i, s, slots):
    return slice((i * slots + s) * z.bs, (i * slots + s + 1) * z.bs)


def piece_col(z, n):
    me = lax.axis_index("col")
    step, core = n // 2, lax.rem(me, 2) ^ (n % 2)
    up = lax.rem(me // 2 + step, z.n_chip)
    down = lax.rem(me // 2 + z.n_chip - step, z.n_chip)
    return jnp.where(core == 0, down, up) * 2 + core


def piece_of(z, col):
    me = lax.axis_index("col")
    chip, core = col // 2, lax.rem(col, 2)
    ahead = lax.rem(chip - me // 2 + z.n_chip, z.n_chip)
    behind = lax.rem(me // 2 - chip + z.n_chip, z.n_chip)
    return jnp.where(core == 0, behind, ahead) * 2 + (core ^ lax.rem(me, 2))


def pack_kernel(z, vals_in, *refs):
    cols_in, (out, tail) = refs[:-2], refs[-2:]
    tail[...] = jnp.zeros_like(tail)
    first = 0
    for cols in cols_in:
        count = cols.shape[0]
        tail[first:first + count, 0:z.rows] = cols[...].astype(F32)
        first += count
    rows = vals_in.shape[0]
    out[rows:rows + TAIL, :] = tail[...].astype(BF16)
    out[0:rows, :] = vals_in[...]


def read_tails(payloads, ints, idx, sem):
    for n, ref in enumerate(payloads):
        rows = ref.shape[0] - TAIL
        ints[n] = ref[rows:rows + TAIL, :].astype(F32).astype(jnp.int32)[0:8, :]
    copy = pltpu.make_async_copy(ints, idx, sem)
    copy.start()
    copy.wait()


def fill_left(z, idx, n, col, blocks, dense, first):
    zero = jnp.zeros((z.bs, z.wide), BF16)
    for i in range(z.rows):
        rows = slice(i * z.bs, (i + 1) * z.bs)
        dense[rows, first:first + z.wide] = zero
        for s in range(z.ka):
            k = idx[n, s, i] - col * z.bc
            at = pl.ds(pl.multiple_of(first + k * z.bs, z.bs), z.bs)
            dense[rows, at] = blocks[block_rows(z, i, s, z.ka), :]


def fill_right(z, first_slot, slots, idx, payloads, dense):
    dense[...] = jnp.zeros_like(dense)
    me = lax.axis_index("col")
    for p, payload in enumerate(payloads):
        for i in range(z.rows):
            k = (lax.axis_index("row") ^ p) * z.rows + i
            n = piece_of(z, k // z.bc)
            at = pl.ds(pl.multiple_of((n * z.bc + lax.rem(k, z.bc)) * z.bs, z.bs), z.bs)
            for s in range(slots):
                j = idx[p, first_slot + s, i] - me * z.bc
                dense[at, lanes(z, j)] = payload[block_rows(z, i, s, slots), :]


def halves(n):
    return [slice(0, n // 2), slice(n // 2, n)]


def first_kernel(z, *refs):
    left_in, right_in = refs[:z.n_first], refs[z.n_first:z.n_first + z.n_row]
    total, panel, right_last, table, right, ints, idx, sem = refs[z.n_first + z.n_row:]
    read_tails(right_in + left_in, ints, idx, sem)
    table[...] = ints[0:z.n_row]
    fill_right(z, z.ka, z.kh, idx, right_in, right)
    for n in range(z.n_first):
        fill_left(z, idx, z.n_row + n, piece_col(z, n), left_in[n], panel, n * z.wide)
    deep = z.n_first * z.wide
    for rows in halves(z.tall):
        total[rows, :] = jnp.dot(panel[rows, :], right[0:deep, :], preferred_element_type=F32)
    right_last[...] = right[deep:, :]


def last_kernel(z, table, last_0, last_1, right, total_in, panel, *refs):
    total, turned, panel_last, *part, columns, ints, idx, sem = refs
    read_tails([last_0, last_1], ints, idx, sem)
    for n, payload in enumerate((last_0, last_1)):
        fill_left(z, idx, n, piece_col(z, z.n_first + n), payload, panel_last, n * z.wide)
    for rows in halves(z.tall):
        total[rows, :] = total_in[rows, :] + jnp.dot(panel_last[rows, :], right[...], preferred_element_type=F32)
    for i in range(z.rows):
        rows = slice(i * z.bs, (i + 1) * z.bs)
        for j in range(z.bc):
            cols = slice(j * z.bs, (j + 1) * z.bs)
            turned[cols, rows] = total[rows, cols].T.astype(BF16)
    one_part(z, table, z.n_row - 1, turned, panel, panel_last, columns, part)


def parts_kernel(z, table, turned, panel, panel_last, *refs):
    cuts = (len(refs) - 1) // (z.n_row - 2)
    for n in range(1, z.n_row - 1):
        one_part(z, table, n, turned, panel, panel_last, refs[-1], refs[(n - 1) * cuts:n * cuts])


def one_part(z, table, n, turned, panel, panel_last, columns, out):
    per_out = z.rows // len(out)
    row = lax.axis_index("row") ^ n
    per = z.n_col // z.n_row
    for t in range(per):
        column = columns.at[t % 2]
        piece = piece_of(z, row * per + t)

        @pl.when(piece < z.n_first)
        def _():
            at = pl.ds(pl.multiple_of(piece * z.wide, z.wide), z.wide)
            column[...] = jnp.dot(turned[...], panel[:, at], preferred_element_type=F32)

        @pl.when(piece >= z.n_first)
        def _():
            at = pl.ds(pl.multiple_of((piece - z.n_first) * z.wide, z.wide), z.wide)
            column[...] = jnp.dot(turned[...], panel_last[:, at], preferred_element_type=F32)

        for b in range(z.bc):
            i = t * z.bc + b
            for s in range(z.ka):
                j = table[n, s, i] - lax.axis_index("col") * z.bc
                out[i // per_out][i % per_out, s] = column[lanes(z, j), b * z.bs:(b + 1) * z.bs].astype(out[0].dtype)


def base_kernel(z, table, filt, total, turned, panel, panel_last, mixed, base, columns, own):
    me = lax.axis_index("col")
    one_part(z, table, 0, turned, panel, panel_last, columns, [own])
    for i in range(z.rows):
        rows = slice(i * z.bs, (i + 1) * z.bs)
        for s in range(z.kf):
            mixed[i, s] = total[rows, lanes(z, filt[s, i] - me * z.bc)].astype(mixed.dtype)
        for s in range(z.ka):
            direct = total[rows, lanes(z, table[0, s, i] - me * z.bc)]
            base[i, s] = 3.0 * direct - 2.0 * own[i, s].T


def square_kernel(z, *refs):
    table, filt, panel, panel_last = refs[:4]
    squared, right, total = refs[4 + z.n_row:]
    me = lax.axis_index("col")
    fill_right(z, 0, z.ka, table, refs[4:4 + z.n_row], right)
    deep = z.n_first * z.wide
    for rows in halves(z.tall):
        total[rows, :] = jnp.dot(panel[rows, :], right[0:deep, :], preferred_element_type=F32)
        total[rows, :] += jnp.dot(panel_last[rows, :], right[deep:, :], preferred_element_type=F32)
    for i in range(z.rows):
        rows = slice(i * z.bs, (i + 1) * z.bs)
        for s in range(z.kf):
            squared[i, s] = total[rows, lanes(z, filt[s, i] - me * z.bc)].astype(squared.dtype)


def add_kernel(z, x_0, x_1, y_0, y_1, x_out, y_out):
    x_out[...] = (x_0[...].astype(F32) + x_1[...].astype(F32)).astype(x_out.dtype)
    y_out[...] = (y_0[...].astype(F32) + y_1[...].astype(F32)).astype(y_out.dtype)


def gradient_kernel(z, base, *refs):
    terms, out = refs[:-1], refs[-1]
    for i in range(z.rows):
        for s in range(z.ka):
            here = [t for t in terms if t.shape[0] == z.rows]
            cut = [t for t in terms if t.shape[0] < z.rows]
            half = z.rows // 2
            blocks = [t[i, s] for t in here] + [t[i % half, s] for t in cut[i // half::2]]
            cubic = blocks[0].astype(F32)
            for other in blocks[1:]:
                cubic += other.astype(F32)
            out[i, s] = (base[i, s] - 2.0 * cubic.T).astype(out.dtype)


def local(n_row, n_col, density, density_cols, hamilton, hamilton_cols, filter_cols):
    z = Sizes(n_row, n_col, density, hamilton, filter_cols)
    block = (z.bs, z.bs)
    shape = jax.ShapeDtypeStruct
    smem = pl.BlockSpec(memory_space=pltpu.SMEM)
    vmem = pl.BlockSpec(memory_space=pltpu.VMEM)
    dma = pltpu.SemaphoreType.DMA
    d_rows, h_rows = z.rows * z.ka * z.bs, z.rows * z.kh * z.bs
    panel_flops = 2 * z.tall * z.wide * z.nb * z.bs
    part_flops = panel_flops // n_row

    def over_row(x, flip):
        return lax.ppermute(x, "row", [(r, r ^ flip) for r in range(n_row)])

    def next_chip(x):
        pairs = [(2 * p, 2 * ((p + 1) % z.n_chip)) for p in range(z.n_chip)]
        pairs += [(2 * p + 1, 2 * ((p - 1) % z.n_chip) + 1) for p in range(z.n_chip)]
        return lax.ppermute(x, "col", pairs)

    def other_core(x):
        return lax.ppermute(x, "col", [(c, c ^ 1) for c in range(n_col)])

    flat = density.reshape(d_rows, z.bs)

    def pack(vals, cols, name):
        rows = vals.shape[0]
        outs = [shape((rows + TAIL, z.bs), BF16)]
        scratch = [pltpu.VMEM((TAIL, z.bs), F32)]
        return call(pack_kernel, z, [vals, *cols], outs, scratch, [vmem] * (1 + len(cols)), [vmem], 0, name)[0]

    d_pay = pack(flat, [density_cols.T], "pack_d")
    h_pay = pack(hamilton.reshape(h_rows, z.bs), [density_cols.T, hamilton_cols.T], "pack_h")

    def high(flip):
        return 1 << (flip.bit_length() - 1)

    def low(flip):
        return flip & -flip

    d_right, h_right = {0: flat}, {0: h_pay}
    for flip in range(1, n_row):
        if flip.bit_count() == 1:
            h_right[flip] = over_row(h_pay, flip)
    d_right, h_right = lax.optimization_barrier((d_right, h_right))
    d_right[1] = over_row(d_right[0], 1)
    for flip in sorted(range(1, n_row), key=int.bit_count):
        if flip not in h_right:
            h_right[flip] = over_row(h_right[flip - high(flip)], high(flip))
    d_right, h_right = lax.optimization_barrier((d_right, h_right))
    for flip in range(2, n_row):
        if flip.bit_count() == 1:
            d_right[flip] = over_row(d_right[0], flip)
    h_right = [h_right[flip] for flip in range(n_row)]

    left, piece = [], d_pay
    for step in range(z.n_chip):
        if step:
            piece = next_chip(piece)
        left.append(piece)
        if step < z.n_chip - 1:
            left.append(other_core(piece))

    n_pay = z.n_first + n_row
    total, panel, right_last, table = call(
        first_kernel, z,
        [*left[:z.n_first], *h_right],
        [
            shape((z.tall, z.wide), F32),
            shape((z.tall, z.n_first * z.wide), BF16),
            shape((2 * z.wide, z.wide), BF16),
            shape((n_row, 8, z.bs), jnp.int32),
        ],
        [
            pltpu.VMEM((z.nb * z.bs, z.wide), BF16),
            pltpu.VMEM((n_pay, 8, z.bs), jnp.int32),
            pltpu.SMEM((n_pay, 8, z.bs), jnp.int32),
            dma,
        ],
        [vmem] * n_pay, [vmem] * 4, panel_flops, "first",
    )
    last, total, d_right = lax.optimization_barrier((left[-1], total, d_right))
    for flip in range(1, n_row):
        if flip not in d_right:
            d_right[flip] = over_row(d_right[flip - low(flip)], low(flip))
    d_right = [d_right[flip] for flip in range(n_row)]

    part = shape((z.rows, z.ka) + block, BF16)
    columns = pltpu.VMEM((2, z.wide, z.wide), F32)
    cuts = 2 if n_row == 4 and z.rows % 2 == 0 else 1
    cut_part = shape((z.rows // cuts, z.ka) + block, BF16)
    total, turned, panel_last, *far = call(
        last_kernel, z,
        [table, last, other_core(last), right_last, total, panel],
        [shape((z.tall, z.wide), F32), shape((z.wide, z.tall), BF16), shape((z.tall, 2 * z.wide), BF16)]
        + [cut_part] * cuts,
        [
            columns,
            pltpu.VMEM((2, 8, z.bs), jnp.int32),
            pltpu.SMEM((2, 8, z.bs), jnp.int32),
            dma,
        ],
        [smem] + [vmem] * 5, [vmem] * (3 + cuts), panel_flops // 4 + part_flops, "last",
    )
    near = call(
        parts_kernel, z, [table, turned, panel, panel_last], [cut_part] * (cuts * (n_row - 2)), [columns],
        [smem] + [vmem] * 3, [vmem] * (cuts * (n_row - 2)), part_flops * (n_row - 2), "parts",
    )
    if cuts == 2:
        far = over_row(far[0], 1), over_row(far[1], 2)
        x_0, y_1 = over_row(near[0], 1), over_row(near[3], 2)
    else:
        received = [over_row(term, n + 1) for n, term in enumerate([*near, *far])]
    mixed, base = call(
        base_kernel, z,
        [table, filter_cols.T, total, turned, panel, panel_last],
        [shape((z.rows, z.kf) + block, BF16), shape((z.rows, z.ka) + block, F32)],
        [columns, pltpu.VMEM((z.rows, z.ka) + block, F32)],
        [smem] * 2 + [vmem] * 4, [vmem] * 2, part_flops, "base",
    )
    if cuts == 2:
        y_0, x_1 = call(
            add_kernel, z, [near[2], far[0], near[1], far[1]], [cut_part] * 2, [],
            [vmem] * 4, [vmem] * 2, 0, "add",
        )
        received = [x_0, over_row(x_1, 1), over_row(y_0, 2), y_1]
    squared, = call(
        square_kernel, z,
        [table, filter_cols.T, panel, panel_last, *d_right],
        [shape((z.rows, z.kf) + block, BF16)],
        [pltpu.VMEM((z.nb * z.bs, z.wide), BF16), pltpu.VMEM((z.tall, z.wide), F32)],
        [smem] * 2 + [vmem] * (n_row + 2), [vmem], panel_flops, "squared",
    )
    gradient, = call(
        gradient_kernel, z, [base, *received], [part], [],
        [vmem] * (1 + len(received)), [vmem], 0, "gradient",
    )
    return squared, mixed, gradient


def solution(mesh):
    spec4 = P("row", "col", None, None)
    spec2 = P("row", "col")
    body = functools.partial(local, mesh.shape["row"], mesh.shape["col"])
    return jax.shard_map(
        body,
        mesh=mesh,
        in_specs=(spec4, spec2, spec4, spec2, spec2),
        out_specs=(spec4, spec4, spec4),
        check_vma=False,
    )
```

```python
import functools
import math

import jax
import jax.numpy as jnp
from jax import lax
from jax.experimental import pallas as pl
from jax.experimental.pallas import tpu as pltpu
from jax.sharding import PartitionSpec as P

VMEM_ROOM = 6 * 1024 * 1024
TAIL = 16
BF16, F32 = jnp.bfloat16, jnp.float32


class Sizes:
    def __init__(self, n_row, n_col, density, hamilton, filt):
        self.n_row, self.n_col, self.n_chip = n_row, n_col, n_col // 2
        self.rows, self.ka, self.bs = density.shape[0], density.shape[1], density.shape[2]
        self.kh, self.kf = hamilton.shape[1], filt.shape[1]
        self.nb = self.rows * n_row
        self.bc = self.nb // n_col
        self.tall, self.wide = self.rows * self.bs, self.bc * self.bs
        self.n_first, self.n_last = n_col - 3, 3


def call(kernel, ins, outs, scratch, in_specs, out_specs, flops, name):
    held = [x for x in scratch if getattr(x, "memory_space", None) == pltpu.VMEM]
    held += [x for x, spec in zip(list(ins) + outs, in_specs + out_specs) if spec.memory_space == pltpu.VMEM]
    size = sum(math.prod(x.shape) * jnp.dtype(x.dtype).itemsize for x in held)
    return pl.pallas_call(
        kernel,
        out_shape=outs,
        in_specs=in_specs,
        out_specs=out_specs,
        scratch_shapes=scratch,
        compiler_params=pltpu.CompilerParams(vmem_limit_bytes=size + VMEM_ROOM),
        cost_estimate=pl.CostEstimate(flops=flops, bytes_accessed=1024, transcendentals=0),
        name=name,
    )(*ins)


def lanes(z, block):
    return pl.ds(pl.multiple_of(block * z.bs, z.bs), z.bs)


def block_rows(z, i, s, slots):
    return slice((i * slots + s) * z.bs, (i * slots + s + 1) * z.bs)


def piece_col(z, n):
    me = lax.axis_index("col")
    step, core = n // 2, lax.rem(me, 2) ^ (n % 2)
    up = lax.rem(me // 2 + step, z.n_chip)
    down = lax.rem(me // 2 + z.n_chip - step, z.n_chip)
    return jnp.where(core == 0, down, up) * 2 + core


def piece_of(z, col):
    me = lax.axis_index("col")
    chip, core = col // 2, lax.rem(col, 2)
    ahead = lax.rem(chip - me // 2 + z.n_chip, z.n_chip)
    behind = lax.rem(me // 2 - chip + z.n_chip, z.n_chip)
    return jnp.where(core == 0, behind, ahead) * 2 + (core ^ lax.rem(me, 2))


def pack_kernel(z, vals_in, *refs):
    cols_in, (out, tail) = refs[:-2], refs[-2:]
    tail[...] = jnp.zeros_like(tail)
    first = 0
    for cols in cols_in:
        count = cols.shape[0]
        tail[first:first + count, 0:z.rows] = cols[...].astype(F32)
        first += count
    rows = vals_in.shape[0]
    out[rows:rows + TAIL, :] = tail[...].astype(BF16)
    out[0:rows, :] = vals_in[...]


def read_tails(payloads, ints, idx, sem):
    for n, ref in enumerate(payloads):
        rows = ref.shape[0] - TAIL
        ints[n] = ref[rows:rows + TAIL, :].astype(F32).astype(jnp.int32)[0:8, :]
    copy = pltpu.make_async_copy(ints, idx, sem)
    copy.start()
    copy.wait()


def fill_left(z, idx, n, col, blocks, dense, first):
    zero = jnp.zeros((z.bs, z.wide), BF16)
    for i in range(z.rows):
        rows = slice(i * z.bs, (i + 1) * z.bs)
        dense[rows, first:first + z.wide] = zero
        for s in range(z.ka):
            k = idx[n, s, i] - col * z.bc
            at = pl.ds(pl.multiple_of(first + k * z.bs, z.bs), z.bs)
            dense[rows, at] = blocks[block_rows(z, i, s, z.ka), :]


def fill_right(z, first_slot, slots, idx, payloads, flips, place, dense):
    dense[...] = jnp.zeros_like(dense)
    me = lax.axis_index("col")
    for flip, payload in zip(flips, payloads):
        for i in range(z.rows):
            at = pl.ds(pl.multiple_of(place(flip, i) * z.bs, z.bs), z.bs)
            for s in range(slots):
                j = idx[flip, first_slot + s, i] - me * z.bc
                row, part = (i * slots + s) * z.bs, 0
                while row >= payload[part].shape[0]:
                    row -= payload[part].shape[0]
                    part += 1
                dense[at, lanes(z, j)] = payload[part][row:row + z.bs, :]


def by_piece(z, flip, i):
    k = (lax.axis_index("row") ^ flip) * z.rows + i
    return piece_of(z, k // z.bc) * z.bc + lax.rem(k, z.bc)


def group(refs, counts):
    refs = iter(refs)
    return [[next(refs) for _ in range(count)] for count in counts]


def halves(n):
    return [slice(0, n // 2), slice(n // 2, n)]


def first_kernel(z, counts, *refs):
    left_in, right_in = refs[:z.n_first], group(refs[z.n_first:], counts)
    total, panel, right_last, table, right, ints, idx, sem = refs[z.n_first + sum(counts):]
    read_tails([x[-1] for x in right_in] + list(left_in), ints, idx, sem)
    table[...] = ints[0:z.n_row]
    fill_right(z, z.ka, z.kh, idx, right_in, range(z.n_row), functools.partial(by_piece, z), right)
    for n in range(z.n_first):
        fill_left(z, idx, z.n_row + n, piece_col(z, n), left_in[n], panel, n * z.wide)
    deep = z.n_first * z.wide
    for rows in halves(z.tall):
        total[rows, :] = jnp.dot(panel[rows, :], right[0:deep, :], preferred_element_type=F32)
    right_last[...] = right[deep:, :]


def last_kernel(z, table, right, total_in, panel, *refs):
    payloads, (total, turned, panel_last, *part, columns, ints, idx, sem) = refs[:z.n_last], refs[z.n_last:]
    read_tails(payloads, ints, idx, sem)
    for n, payload in enumerate(payloads):
        fill_left(z, idx, n, piece_col(z, z.n_first + n), payload, panel_last, n * z.wide)
    for rows in halves(z.tall):
        total[rows, :] = total_in[rows, :] + jnp.dot(panel_last[rows, :], right[...], preferred_element_type=F32)
    for i in range(z.rows):
        rows = slice(i * z.bs, (i + 1) * z.bs)
        for j in range(z.bc):
            cols = slice(j * z.bs, (j + 1) * z.bs)
            turned[cols, rows] = total[rows, cols].T.astype(BF16)
    one_part(z, table, z.n_row - 1, turned, panel, panel_last, columns, part)


def parts_kernel(z, table, turned, panel, panel_last, *refs):
    cuts = (len(refs) - 1) // (z.n_row - 2)
    for n in range(1, z.n_row - 1):
        one_part(z, table, n, turned, panel, panel_last, refs[-1], refs[(n - 1) * cuts:n * cuts])


def one_part(z, table, n, turned, panel, panel_last, columns, out):
    per_out = z.rows // len(out)
    row = lax.axis_index("row") ^ n
    per = z.n_col // z.n_row
    for t in range(per):
        column = columns.at[t % 2]
        piece = piece_of(z, row * per + t)

        @pl.when(piece < z.n_first)
        def _():
            at = pl.ds(pl.multiple_of(piece * z.wide, z.wide), z.wide)
            column[...] = jnp.dot(turned[...], panel[:, at], preferred_element_type=F32)

        @pl.when(piece >= z.n_first)
        def _():
            at = pl.ds(pl.multiple_of((piece - z.n_first) * z.wide, z.wide), z.wide)
            column[...] = jnp.dot(turned[...], panel_last[:, at], preferred_element_type=F32)

        for b in range(z.bc):
            i = t * z.bc + b
            for s in range(z.ka):
                j = table[n, s, i] - lax.axis_index("col") * z.bc
                out[i // per_out][i % per_out, s] = column[lanes(z, j), b * z.bs:(b + 1) * z.bs].astype(out[0].dtype)


def base_kernel(z, table, filt, total, turned, panel, panel_last, mixed, base, columns, own):
    me = lax.axis_index("col")
    one_part(z, table, 0, turned, panel, panel_last, columns, [own])
    for i in range(z.rows):
        rows = slice(i * z.bs, (i + 1) * z.bs)
        for s in range(z.kf):
            mixed[i, s] = total[rows, lanes(z, filt[s, i] - me * z.bc)].astype(mixed.dtype)
        for s in range(z.ka):
            direct = total[rows, lanes(z, table[0, s, i] - me * z.bc)]
            base[i, s] = 3.0 * direct - 2.0 * own[i, s].T


def square_kernel(z, counts, table, filt, panel, panel_last, *refs):
    squared, right, total = refs[sum(counts):]
    me = lax.axis_index("col")
    fill_right(z, 0, z.ka, table, group(refs, counts), range(z.n_row), functools.partial(by_piece, z), right)
    deep = z.n_first * z.wide
    for rows in halves(z.tall):
        total[rows, :] = jnp.dot(panel[rows, :], right[0:deep, :], preferred_element_type=F32)
        total[rows, :] += jnp.dot(panel_last[rows, :], right[deep:, :], preferred_element_type=F32)
    for i in range(z.rows):
        rows = slice(i * z.bs, (i + 1) * z.bs)
        for s in range(z.kf):
            squared[i, s] = total[rows, lanes(z, filt[s, i] - me * z.bc)].astype(squared.dtype)


def add_kernel(z, x_0, x_1, y_0, y_1, x_out, y_out):
    x_out[...] = (x_0[...].astype(F32) + x_1[...].astype(F32)).astype(x_out.dtype)
    y_out[...] = (y_0[...].astype(F32) + y_1[...].astype(F32)).astype(y_out.dtype)


def gradient_kernel(z, base, *refs):
    terms, out = refs[:-1], refs[-1]
    for i in range(z.rows):
        for s in range(z.ka):
            here = [t for t in terms if t.shape[0] == z.rows]
            cut = [t for t in terms if t.shape[0] < z.rows]
            half = z.rows // 2
            blocks = [t[i, s] for t in here] + [t[i % half, s] for t in cut[i // half::2]]
            cubic = blocks[0].astype(F32)
            for other in blocks[1:]:
                cubic += other.astype(F32)
            out[i, s] = (base[i, s] - 2.0 * cubic.T).astype(out.dtype)


def local(n_row, n_col, density, density_cols, hamilton, hamilton_cols, filter_cols):
    z = Sizes(n_row, n_col, density, hamilton, filter_cols)
    block = (z.bs, z.bs)
    shape = jax.ShapeDtypeStruct
    smem = pl.BlockSpec(memory_space=pltpu.SMEM)
    vmem = pl.BlockSpec(memory_space=pltpu.VMEM)
    dma = pltpu.SemaphoreType.DMA
    d_rows, h_rows = z.rows * z.ka * z.bs, z.rows * z.kh * z.bs
    panel_flops = 2 * z.tall * z.wide * z.nb * z.bs
    part_flops = panel_flops // n_row

    def over_row(x, flip):
        return lax.ppermute(x, "row", [(r, r ^ flip) for r in range(n_row)])

    def next_chip(x):
        pairs = [(2 * p, 2 * ((p + 1) % z.n_chip)) for p in range(z.n_chip)]
        pairs += [(2 * p + 1, 2 * ((p - 1) % z.n_chip) + 1) for p in range(z.n_chip)]
        return lax.ppermute(x, "col", pairs)

    def other_core(x):
        return lax.ppermute(x, "col", [(c, c ^ 1) for c in range(n_col)])

    flat = density.reshape(d_rows, z.bs)

    def pack(vals, cols, name):
        rows = vals.shape[0]
        outs = [shape((rows + TAIL, z.bs), BF16)]
        scratch = [pltpu.VMEM((TAIL, z.bs), F32)]
        return call(functools.partial(pack_kernel, z), [vals, *cols], outs, scratch, [vmem] * (1 + len(cols)), [vmem], 0, name)[0]

    d_pay = pack(flat, [density_cols.T], "pack_d")
    h_pay = pack(hamilton.reshape(h_rows, z.bs), [density_cols.T, hamilton_cols.T], "pack_h")

    flips = sorted(range(1, n_row), key=int.bit_count)
    single = [flip for flip in flips if flip.bit_count() == 1]
    h_half, d_half = h_rows // 2, d_rows // 2

    def forward(blocks):
        for flip in flips:
            if flip not in blocks:
                blocks[flip] = [over_row(blocks[flip & (flip - 1)][0], flip & -flip)]

    left, piece = [d_pay, other_core(d_pay)], d_pay
    h_right, d_0 = {0: [h_pay]}, d_pay
    for step in range(1, z.n_chip):
        piece = next_chip(piece)
        if step == 1:
            for flip in single:
                h_right[flip] = [over_row(h_pay, flip)]
        if step == 2:
            if n_row == 4:
                h_right[3] = [over_row(h_right[1][0][:h_half], 2), over_row(h_right[2][0][h_half:], 1)]
            forward(h_right)
            piece, h_right, d_0 = lax.optimization_barrier((piece, h_right, d_0))
            d_right = {0: [d_0]}
            for flip in single:
                d_right[flip] = [over_row(d_0, flip)]
        left.append(piece)
        if step < z.n_chip - 1:
            left.append(other_core(piece))
    h_right = [h_right[flip] for flip in range(n_row)]

    n_pay = z.n_first + n_row
    total, panel, right_last, table = call(
        functools.partial(first_kernel, z, [len(x) for x in h_right]),
        [*left[:z.n_first], *sum(h_right, [])],
        [
            shape((z.tall, z.wide), F32),
            shape((z.tall, z.n_first * z.wide), BF16),
            shape((z.n_last * z.wide, z.wide), BF16),
            shape((n_row, 8, z.bs), jnp.int32),
        ],
        [
            pltpu.VMEM((z.nb * z.bs, z.wide), BF16),
            pltpu.VMEM((n_pay, 8, z.bs), jnp.int32),
            pltpu.SMEM((n_pay, 8, z.bs), jnp.int32),
            dma,
        ],
        [vmem] * (z.n_first + sum(map(len, h_right))), [vmem] * 4, 0, "first",
    )
    last, total, d_right = lax.optimization_barrier((left[-1], total, d_right))
    if n_row == 4:
        d_right[3] = [over_row(d_right[1][0][:d_half], 2), over_row(d_right[2][0][d_half:d_rows], 1)]
    forward(d_right)
    d_right = [d_right[flip] for flip in range(n_row)]
    part = shape((z.rows, z.ka) + block, BF16)
    columns = pltpu.VMEM((2, z.wide, z.wide), F32)
    cuts = 2 if n_row == 4 and z.rows % 2 == 0 else 1
    cut_part = shape((z.rows // cuts, z.ka) + block, BF16)
    total, turned, panel_last, *far = call(
        functools.partial(last_kernel, z),
        [table, right_last, total, panel, *left[z.n_first:-1], last, other_core(last)],
        [shape((z.tall, z.wide), F32), shape((z.wide, z.tall), BF16), shape((z.tall, z.n_last * z.wide), BF16)]
        + [cut_part] * cuts,
        [
            columns,
            pltpu.VMEM((z.n_last, 8, z.bs), jnp.int32),
            pltpu.SMEM((z.n_last, 8, z.bs), jnp.int32),
            dma,
        ],
        [smem] + [vmem] * (3 + z.n_last), [vmem] * (3 + cuts), panel_flops // 4 + part_flops, "last",
    )
    far, d_right = lax.optimization_barrier((far, d_right))
    near = call(
        functools.partial(parts_kernel, z), [table, turned, panel, panel_last], [cut_part] * (cuts * (n_row - 2)), [columns],
        [smem] + [vmem] * 3, [vmem] * (cuts * (n_row - 2)), part_flops * (n_row - 2), "parts",
    )
    if cuts == 2:
        far = over_row(far[0], 1), over_row(far[1], 2)
        x_0, y_1 = over_row(near[0], 1), over_row(near[3], 2)
    else:
        received = [over_row(term, n + 1) for n, term in enumerate([*near, *far])]
    mixed, base = call(
        functools.partial(base_kernel, z),
        [table, filter_cols.T, total, turned, panel, panel_last],
        [shape((z.rows, z.kf) + block, BF16), shape((z.rows, z.ka) + block, F32)],
        [columns, pltpu.VMEM((z.rows, z.ka) + block, F32)],
        [smem] * 2 + [vmem] * 4, [vmem] * 2, part_flops, "base",
    )
    if cuts == 2:
        y_0, x_1 = call(
            functools.partial(add_kernel, z), [near[2], far[0], near[1], far[1]], [cut_part] * 2, [],
            [vmem] * 4, [vmem] * 2, 0, "add",
        )
        received = [x_0, over_row(x_1, 1), over_row(y_0, 2), y_1]
    squared, = call(
        functools.partial(square_kernel, z, [len(x) for x in d_right]),
        [table, filter_cols.T, panel, panel_last, *sum(d_right, [])],
        [shape((z.rows, z.kf) + block, BF16)],
        [pltpu.VMEM((z.nb * z.bs, z.wide), BF16), pltpu.VMEM((z.tall, z.wide), F32)],
        [smem] * 2 + [vmem] * (2 + sum(map(len, d_right))), [vmem], panel_flops, "squared",
    )
    gradient, = call(
        functools.partial(gradient_kernel, z), [base, *received], [part], [],
        [vmem] * (1 + len(received)), [vmem], 0, "gradient",
    )
    return squared, mixed, gradient


def solution(mesh):
    spec4 = P("row", "col", None, None)
    spec2 = P("row", "col")
    body = functools.partial(local, mesh.shape["row"], mesh.shape["col"])
    return jax.shard_map(
        body,
        mesh=mesh,
        in_specs=(spec4, spec2, spec4, spec2, spec2),
        out_specs=(spec4, spec4, spec4),
        check_vma=False,
    )
```

```python
import functools
import math

import jax
import jax.numpy as jnp
from jax import lax
from jax.experimental import pallas as pl
from jax.experimental.pallas import tpu as pltpu
from jax.sharding import PartitionSpec as P

VMEM_ROOM = 6 * 1024 * 1024
TAIL = 16
BF16, F32 = jnp.bfloat16, jnp.float32


class Sizes:
    def __init__(self, n_row, n_col, density, hamilton, filt):
        self.n_row, self.n_col, self.n_chip = n_row, n_col, n_col // 2
        self.rows, self.ka, self.bs = density.shape[0], density.shape[1], density.shape[2]
        self.kh, self.kf = hamilton.shape[1], filt.shape[1]
        self.nb = self.rows * n_row
        self.bc = self.nb // n_col
        self.tall, self.wide = self.rows * self.bs, self.bc * self.bs
        self.n_first, self.n_last = n_col - 3, 3


def call(kernel, ins, outs, scratch, in_specs, out_specs, flops, name):
    held = [x for x in scratch if getattr(x, "memory_space", None) == pltpu.VMEM]
    held += [x for x, spec in zip(list(ins) + outs, in_specs + out_specs) if spec.memory_space == pltpu.VMEM]
    size = sum(math.prod(x.shape) * jnp.dtype(x.dtype).itemsize for x in held)
    return pl.pallas_call(
        kernel,
        out_shape=outs,
        in_specs=in_specs,
        out_specs=out_specs,
        scratch_shapes=scratch,
        compiler_params=pltpu.CompilerParams(vmem_limit_bytes=size + VMEM_ROOM),
        cost_estimate=pl.CostEstimate(flops=flops, bytes_accessed=1024, transcendentals=0),
        name=name,
    )(*ins)


def lanes(z, block):
    return pl.ds(pl.multiple_of(block * z.bs, z.bs), z.bs)


def block_rows(z, i, s, slots):
    return slice((i * slots + s) * z.bs, (i * slots + s + 1) * z.bs)


def piece_col(z, n):
    me = lax.axis_index("col")
    step, core = n // 2, lax.rem(me, 2) ^ (n % 2)
    up = lax.rem(me // 2 + step, z.n_chip)
    down = lax.rem(me // 2 + z.n_chip - step, z.n_chip)
    return jnp.where(core == 0, down, up) * 2 + core


def piece_of(z, col):
    me = lax.axis_index("col")
    chip, core = col // 2, lax.rem(col, 2)
    ahead = lax.rem(chip - me // 2 + z.n_chip, z.n_chip)
    behind = lax.rem(me // 2 - chip + z.n_chip, z.n_chip)
    return jnp.where(core == 0, behind, ahead) * 2 + (core ^ lax.rem(me, 2))


def pack_kernel(z, vals_in, *refs):
    cols_in, (out, tail) = refs[:-2], refs[-2:]
    tail[...] = jnp.zeros_like(tail)
    first = 0
    for cols in cols_in:
        count = cols.shape[0]
        tail[first:first + count, 0:z.rows] = cols[...].astype(F32)
        first += count
    rows = vals_in.shape[0]
    out[rows:rows + TAIL, :] = tail[...].astype(BF16)
    out[0:rows, :] = vals_in[...]


def read_tails(payloads, ints, idx, sem):
    for n, ref in enumerate(payloads):
        rows = ref.shape[0] - TAIL
        ints[n] = ref[rows:rows + TAIL, :].astype(F32).astype(jnp.int32)[0:8, :]
    copy = pltpu.make_async_copy(ints, idx, sem)
    copy.start()
    copy.wait()


def fill_left(z, idx, n, col, blocks, dense, first):
    zero = jnp.zeros((z.bs, z.wide), BF16)
    for i in range(z.rows):
        rows = slice(i * z.bs, (i + 1) * z.bs)
        dense[rows, first:first + z.wide] = zero
        for s in range(z.ka):
            k = idx[n, s, i] - col * z.bc
            at = pl.ds(pl.multiple_of(first + k * z.bs, z.bs), z.bs)
            dense[rows, at] = blocks[block_rows(z, i, s, z.ka), :]


def fill_right(z, first_slot, slots, idx, payloads, flips, place, dense):
    dense[...] = jnp.zeros_like(dense)
    me = lax.axis_index("col")
    for flip, payload in zip(flips, payloads):
        for i in range(z.rows):
            at = pl.ds(pl.multiple_of(place(flip, i) * z.bs, z.bs), z.bs)
            for s in range(slots):
                j = idx[flip, first_slot + s, i] - me * z.bc
                row, part = (i * slots + s) * z.bs, 0
                while row >= payload[part].shape[0]:
                    row -= payload[part].shape[0]
                    part += 1
                dense[at, lanes(z, j)] = payload[part][row:row + z.bs, :]


def by_piece(z, flip, i):
    k = (lax.axis_index("row") ^ flip) * z.rows + i
    return piece_of(z, k // z.bc) * z.bc + lax.rem(k, z.bc)


def group(refs, counts):
    refs = iter(refs)
    return [[next(refs) for _ in range(count)] for count in counts]


def halves(n):
    return [slice(0, n // 2), slice(n // 2, n)]


def first_kernel(z, counts, *refs):
    left_in, right_in = refs[:z.n_first], group(refs[z.n_first:], counts)
    total, panel, right_last, table, right, ints, idx, sem = refs[z.n_first + sum(counts):]
    read_tails([x[-1] for x in right_in] + list(left_in), ints, idx, sem)
    table[...] = ints[0:z.n_row]
    fill_right(z, z.ka, z.kh, idx, right_in, range(z.n_row), functools.partial(by_piece, z), right)
    for n in range(z.n_first):
        fill_left(z, idx, z.n_row + n, piece_col(z, n), left_in[n], panel, n * z.wide)
    deep = z.n_first * z.wide
    for rows in halves(z.tall):
        total[rows, :] = jnp.dot(panel[rows, :], right[0:deep, :], preferred_element_type=F32)
    right_last[...] = right[deep:, :]


def last_kernel(z, table, right, total_in, panel, *refs):
    payloads, (total, turned, panel_last, *part, ints, idx, sem) = refs[:z.n_last], refs[z.n_last:]
    read_tails(payloads, ints, idx, sem)
    for n, payload in enumerate(payloads):
        fill_left(z, idx, n, piece_col(z, z.n_first + n), payload, panel_last, n * z.wide)
    for rows in halves(z.tall):
        total[rows, :] = total_in[rows, :] + jnp.dot(panel_last[rows, :], right[...], preferred_element_type=F32)
    for i in range(z.rows):
        rows = slice(i * z.bs, (i + 1) * z.bs)
        for j in range(z.bc):
            cols = slice(j * z.bs, (j + 1) * z.bs)
            turned[cols, rows] = total[rows, cols].T.astype(BF16)
    one_part(z, table, z.n_row - 1, turned, panel, panel_last, part)


def parts_kernel(z, table, turned, panel, panel_last, *refs):
    cuts = len(refs) // (z.n_row - 2)
    for n in range(1, z.n_row - 1):
        one_part(z, table, n, turned, panel, panel_last, refs[(n - 1) * cuts:n * cuts])


def one_part(z, table, n, turned, panel, panel_last, out):
    row = lax.axis_index("row") ^ n
    per, per_out = z.n_col // z.n_row, z.rows // len(out)
    me = lax.axis_index("col")

    def blocks(t, source, first):
        for b in range(z.bc):
            i = t * z.bc + b
            wanted = [turned[lanes(z, table[n, s, i] - me * z.bc), :] for s in range(z.ka)]
            column = source[:, lanes(z, first * z.bc + b)]
            terms = jnp.dot(jnp.concatenate(wanted, axis=0), column, preferred_element_type=F32)
            for s in range(z.ka):
                ref = out[i // per_out]
                ref[i % per_out, s] = terms[s * z.bs:(s + 1) * z.bs, :].astype(ref.dtype)

    for t in range(per):
        piece = piece_of(z, row * per + t)
        pl.when(piece < z.n_first)(functools.partial(blocks, t, panel, piece))
        pl.when(piece >= z.n_first)(functools.partial(blocks, t, panel_last, piece - z.n_first))


def filtered(z, filt, total, i, s):
    me = lax.axis_index("col")
    return total[i * z.bs:(i + 1) * z.bs, lanes(z, filt[s, i] - me * z.bc)].astype(BF16)


def base_kernel(z, table, filt, total, turned, panel, panel_last, mixed, direct, own, held, sem):
    me = lax.axis_index("col")
    for i in range(z.rows):
        for s in range(z.kf):
            held[i, s] = filtered(z, filt, total, i, s)
    copy = pltpu.make_async_copy(held, mixed, sem)
    copy.start()
    for i in range(z.rows):
        for s in range(z.ka):
            direct[i, s] = 3.0 * total[i * z.bs:(i + 1) * z.bs, lanes(z, table[0, s, i] - me * z.bc)]
    one_part(z, table, 0, turned, panel, panel_last, [own])
    copy.wait()


def square_kernel(z, counts, table, filt, panel, panel_last, *refs):
    squared, right, total, held, sems = refs[sum(counts):]
    fill_right(z, 0, z.ka, table, group(refs, counts), range(z.n_row), functools.partial(by_piece, z), right)
    deep = z.n_first * z.wide
    copies = []
    for n, rows in enumerate(halves(z.tall)):
        total[rows, :] = jnp.dot(panel[rows, :], right[0:deep, :], preferred_element_type=F32)
        total[rows, :] += jnp.dot(panel_last[rows, :], right[deep:, :], preferred_element_type=F32)
        here = halves(z.rows)[n]
        for i in range(here.start, here.stop):
            for s in range(z.kf):
                held[i, s] = filtered(z, filt, total, i, s)
        copies.append(pltpu.make_async_copy(held.at[here], squared.at[here], sems.at[n]))
        copies[-1].start()
    for copy in copies:
        copy.wait()


def add_kernel(z, x_0, x_1, y_0, y_1, x_out, y_out):
    x_out[...] = (x_0[...].astype(F32) + x_1[...].astype(F32)).astype(x_out.dtype)
    y_out[...] = (y_0[...].astype(F32) + y_1[...].astype(F32)).astype(y_out.dtype)


def gradient_kernel(z, direct, own, *refs):
    terms, out = refs[:-1], refs[-1]
    half = z.rows // 2
    here = [t for t in terms if t.shape[0] == z.rows]
    cut = [t for t in terms if t.shape[0] < z.rows]
    for i in range(z.rows):
        for s in range(z.ka):
            cubic = own[i, s]
            for block in [t[i, s] for t in here] + [t[i % half, s] for t in cut[i // half::2]]:
                cubic += block.astype(F32)
            out[i, s] = (direct[i, s] - 2.0 * cubic.T).astype(out.dtype)


def local(n_row, n_col, density, density_cols, hamilton, hamilton_cols, filter_cols):
    z = Sizes(n_row, n_col, density, hamilton, filter_cols)
    block = (z.bs, z.bs)
    shape = jax.ShapeDtypeStruct
    smem = pl.BlockSpec(memory_space=pltpu.SMEM)
    vmem = pl.BlockSpec(memory_space=pltpu.VMEM)
    anywhere = pl.BlockSpec(memory_space=pl.ANY)
    dma = pltpu.SemaphoreType.DMA
    d_rows, h_rows = z.rows * z.ka * z.bs, z.rows * z.kh * z.bs
    panel_flops = 2 * z.tall * z.wide * z.nb * z.bs
    part_flops = panel_flops // n_row

    def over_row(x, flip):
        return lax.ppermute(x, "row", [(r, r ^ flip) for r in range(n_row)])

    def next_chip(x):
        pairs = [(2 * p, 2 * ((p + 1) % z.n_chip)) for p in range(z.n_chip)]
        pairs += [(2 * p + 1, 2 * ((p - 1) % z.n_chip) + 1) for p in range(z.n_chip)]
        return lax.ppermute(x, "col", pairs)

    def other_core(x):
        return lax.ppermute(x, "col", [(c, c ^ 1) for c in range(n_col)])

    flat = density.reshape(d_rows, z.bs)

    def pack(vals, cols, name):
        rows = vals.shape[0]
        outs = [shape((rows + TAIL, z.bs), BF16)]
        scratch = [pltpu.VMEM((TAIL, z.bs), F32)]
        return call(functools.partial(pack_kernel, z), [vals, *cols], outs, scratch, [vmem] * (1 + len(cols)), [vmem], 0, name)[0]

    d_pay = pack(flat, [density_cols.T], "pack_d")
    h_pay = pack(hamilton.reshape(h_rows, z.bs), [density_cols.T, hamilton_cols.T], "pack_h")

    flips = sorted(range(1, n_row), key=int.bit_count)
    single = [flip for flip in flips if flip.bit_count() == 1]
    h_half, d_half = h_rows // 2, d_rows // 2

    def forward(blocks):
        for flip in flips:
            if flip not in blocks:
                blocks[flip] = [over_row(blocks[flip & (flip - 1)][0], flip & -flip)]

    left, piece = [d_pay, other_core(d_pay)], d_pay
    h_right, d_0 = {0: [h_pay]}, d_pay
    for step in range(1, z.n_chip):
        piece = next_chip(piece)
        if step == 1:
            for flip in single:
                h_right[flip] = [over_row(h_pay, flip)]
        if step == 2:
            if n_row == 4:
                h_right[3] = [over_row(h_right[1][0][:h_half], 2), over_row(h_right[2][0][h_half:], 1)]
            forward(h_right)
            piece, h_right, d_0 = lax.optimization_barrier((piece, h_right, d_0))
            d_right = {0: [d_0]}
            for flip in single:
                d_right[flip] = [over_row(d_0, flip)]
        left.append(piece)
        if step < z.n_chip - 1:
            left.append(other_core(piece))
    h_right = [h_right[flip] for flip in range(n_row)]

    n_pay = z.n_first + n_row
    total, panel, right_last, table = call(
        functools.partial(first_kernel, z, [len(x) for x in h_right]),
        [*left[:z.n_first], *sum(h_right, [])],
        [
            shape((z.tall, z.wide), F32),
            shape((z.tall, z.n_first * z.wide), BF16),
            shape((z.n_last * z.wide, z.wide), BF16),
            shape((n_row, 8, z.bs), jnp.int32),
        ],
        [
            pltpu.VMEM((z.nb * z.bs, z.wide), BF16),
            pltpu.VMEM((n_pay, 8, z.bs), jnp.int32),
            pltpu.SMEM((n_pay, 8, z.bs), jnp.int32),
            dma,
        ],
        [vmem] * (z.n_first + sum(map(len, h_right))), [vmem] * 4, 0, "first",
    )
    last, total, d_right = lax.optimization_barrier((left[-1], total, d_right))
    if n_row == 4:
        d_right[3] = [over_row(d_right[1][0][:d_half], 2), over_row(d_right[2][0][d_half:d_rows], 1)]
    forward(d_right)
    d_right = [d_right[flip] for flip in range(n_row)]
    part = shape((z.rows, z.ka) + block, BF16)
    cuts = 2 if n_row == 4 and z.rows % 2 == 0 else 1
    cut_part = shape((z.rows // cuts, z.ka) + block, BF16)
    total, turned, panel_last, *far = call(
        functools.partial(last_kernel, z),
        [table, right_last, total, panel, *left[z.n_first:-1], last, other_core(last)],
        [shape((z.tall, z.wide), F32), shape((z.wide, z.tall), BF16), shape((z.tall, z.n_last * z.wide), BF16)]
        + [cut_part] * cuts,
        [
            pltpu.VMEM((z.n_last, 8, z.bs), jnp.int32),
            pltpu.SMEM((z.n_last, 8, z.bs), jnp.int32),
            dma,
        ],
        [smem] + [vmem] * (3 + z.n_last), [vmem] * (3 + cuts), panel_flops // 4 + part_flops, "last",
    )
    near = call(
        functools.partial(parts_kernel, z), [table, turned, panel, panel_last], [cut_part] * (cuts * (n_row - 2)), [],
        [smem] + [vmem] * 3, [vmem] * (cuts * (n_row - 2)), part_flops * (n_row - 2), "parts",
    )
    near, d_right = lax.optimization_barrier((near, d_right))
    if cuts == 2:
        far = over_row(far[0], 1), over_row(far[1], 2)
        x_0, y_1 = over_row(near[0], 1), over_row(near[3], 2)
    else:
        received = [over_row(term, n + 1) for n, term in enumerate([*near, *far])]
    whole_part = shape((z.rows, z.ka) + block, F32)
    mixed, direct, own = call(
        functools.partial(base_kernel, z),
        [table, filter_cols.T, total, turned, panel, panel_last],
        [shape((z.rows, z.kf) + block, BF16), whole_part, whole_part],
        [pltpu.VMEM((z.rows, z.kf) + block, BF16), dma],
        [smem] * 2 + [vmem] * 4, [anywhere, vmem, vmem], part_flops, "base",
    )
    if cuts == 2:
        y_0, x_1 = call(
            functools.partial(add_kernel, z), [near[2], far[0], near[1], far[1]], [cut_part] * 2, [],
            [vmem] * 4, [vmem] * 2, 0, "add",
        )
        received = [x_0, over_row(x_1, 1), over_row(y_0, 2), y_1]
    squared, = call(
        functools.partial(square_kernel, z, [len(x) for x in d_right]),
        [table, filter_cols.T, panel, panel_last, *sum(d_right, [])],
        [shape((z.rows, z.kf) + block, BF16)],
        [
            pltpu.VMEM((z.nb * z.bs, z.wide), BF16), pltpu.VMEM((z.tall, z.wide), F32),
            pltpu.VMEM((z.rows, z.kf) + block, BF16), dma((2,)),
        ],
        [smem] * 2 + [vmem] * (2 + sum(map(len, d_right))), [anywhere], panel_flops, "squared",
    )
    gradient, = call(
        functools.partial(gradient_kernel, z), [direct, own, *received], [part], [],
        [vmem] * (2 + len(received)), [vmem], 0, "gradient",
    )
    return squared, mixed, gradient


def solution(mesh):
    spec4 = P("row", "col", None, None)
    spec2 = P("row", "col")
    body = functools.partial(local, mesh.shape["row"], mesh.shape["col"])
    return jax.shard_map(
        body,
        mesh=mesh,
        in_specs=(spec4, spec2, spec4, spec2, spec2),
        out_specs=(spec4, spec4, spec4),
        check_vma=False,
    )
```

```python
import functools
import math

import jax
import jax.numpy as jnp
from jax import lax
from jax.experimental import pallas as pl
from jax.experimental.pallas import tpu as pltpu
from jax.sharding import PartitionSpec as P

VMEM_ROOM = 6 * 1024 * 1024
N_LAST = 3
TAIL = 16
BF16, F32 = jnp.bfloat16, jnp.float32


class Sizes:
    def __init__(self, n_row, n_col, density, hamilton, filt):
        self.n_row, self.n_col, self.n_chip = n_row, n_col, n_col // 2
        self.rows, self.ka, self.bs = density.shape[0], density.shape[1], density.shape[2]
        self.kh, self.kf = hamilton.shape[1], filt.shape[1]
        self.nb = self.rows * n_row
        self.bc = self.nb // n_col
        self.tall, self.wide = self.rows * self.bs, self.bc * self.bs
        self.n_first, self.n_last = n_col - N_LAST, N_LAST


def call(kernel, ins, outs, scratch, in_specs, out_specs, flops, name):
    held = [x for x in scratch if getattr(x, "memory_space", None) == pltpu.VMEM]
    held += [x for x, spec in zip(list(ins) + outs, in_specs + out_specs) if spec.memory_space == pltpu.VMEM]
    size = sum(math.prod(x.shape) * jnp.dtype(x.dtype).itemsize for x in held)
    return pl.pallas_call(
        kernel,
        out_shape=outs,
        in_specs=in_specs,
        out_specs=out_specs,
        scratch_shapes=scratch,
        compiler_params=pltpu.CompilerParams(vmem_limit_bytes=size + VMEM_ROOM),
        cost_estimate=pl.CostEstimate(flops=flops, bytes_accessed=1024, transcendentals=0),
        name=name,
    )(*ins)


def lanes(z, block):
    return pl.ds(pl.multiple_of(block * z.bs, z.bs), z.bs)


def block_rows(z, i, s, slots):
    return slice((i * slots + s) * z.bs, (i * slots + s + 1) * z.bs)


def piece_col(z, n):
    me = lax.axis_index("col")
    hops, core = (n // 2 + 1) // 2, lax.rem(me, 2) ^ (n % 2)
    up = lax.rem(me // 2 + hops, z.n_chip)
    down = lax.rem(me // 2 + z.n_chip - hops, z.n_chip)
    behind = 0 if n // 2 % 2 else 1
    return jnp.where(core == behind, down, up) * 2 + core


def piece_of(z, col):
    me = lax.axis_index("col")
    chip, core = col // 2, lax.rem(col, 2)
    up = lax.rem(chip - me // 2 + z.n_chip, z.n_chip)
    down = lax.rem(me // 2 - chip + z.n_chip, z.n_chip)
    hops = jnp.where(core == 0, down, up)
    step = jnp.where(2 * hops <= z.n_chip, jnp.maximum(2 * hops - 1, 0), 2 * (z.n_chip - hops))
    return step * 2 + (core ^ lax.rem(me, 2))


def pack_kernel(z, vals_in, *refs):
    cols_in, (out, tail) = refs[:-2], refs[-2:]
    tail[...] = jnp.zeros_like(tail)
    first = 0
    for cols in cols_in:
        count = cols.shape[0]
        tail[first:first + count, 0:z.rows] = cols[...].astype(F32)
        first += count
    rows = vals_in.shape[0]
    out[rows:rows + TAIL, :] = tail[...].astype(BF16)
    out[0:rows, :] = vals_in[...]


def read_tails(payloads, ints, idx, sem):
    for n, ref in enumerate(payloads):
        rows = ref.shape[0] - TAIL
        ints[n] = ref[rows:rows + TAIL, :].astype(F32).astype(jnp.int32)[0:8, :]
    copy = pltpu.make_async_copy(ints, idx, sem)
    copy.start()
    copy.wait()


def fill_left(z, idx, n, col, blocks, dense, first):
    zero = jnp.zeros((z.bs, z.wide), BF16)
    for i in range(z.rows):
        rows = slice(i * z.bs, (i + 1) * z.bs)
        dense[rows, first:first + z.wide] = zero
        for s in range(z.ka):
            k = idx[n, s, i] - col * z.bc
            at = pl.ds(pl.multiple_of(first + k * z.bs, z.bs), z.bs)
            dense[rows, at] = blocks[block_rows(z, i, s, z.ka), :]


def fill_right(z, first_slot, slots, idx, payloads, flips, place, dense):
    dense[...] = jnp.zeros_like(dense)
    me = lax.axis_index("col")
    for flip, payload in zip(flips, payloads):
        for i in range(z.rows):
            at = pl.ds(pl.multiple_of(place(flip, i) * z.bs, z.bs), z.bs)
            for s in range(slots):
                j = idx[flip, first_slot + s, i] - me * z.bc
                row, part = (i * slots + s) * z.bs, 0
                while row >= payload[part].shape[0]:
                    row -= payload[part].shape[0]
                    part += 1
                dense[at, lanes(z, j)] = payload[part][row:row + z.bs, :]


def by_piece(z, flip, i):
    k = (lax.axis_index("row") ^ flip) * z.rows + i
    return piece_of(z, k // z.bc) * z.bc + lax.rem(k, z.bc)


def group(refs, counts):
    refs = iter(refs)
    return [[next(refs) for _ in range(count)] for count in counts]


def halves(n):
    return [slice(0, n // 2), slice(n // 2, n)]


def first_kernel(z, counts, *refs):
    left_in, right_in = refs[:z.n_first], group(refs[z.n_first:], counts)
    total, panel, right_last, table, right, ints, idx, sem = refs[z.n_first + sum(counts):]
    read_tails([x[-1] for x in right_in] + list(left_in), ints, idx, sem)
    table[...] = ints[0:z.n_row]
    fill_right(z, z.ka, z.kh, idx, right_in, range(z.n_row), functools.partial(by_piece, z), right)
    for n in range(z.n_first):
        fill_left(z, idx, z.n_row + n, piece_col(z, n), left_in[n], panel, n * z.wide)
    deep = z.n_first * z.wide
    for rows in halves(z.tall):
        total[rows, :] = jnp.dot(panel[rows, :], right[0:deep, :], preferred_element_type=F32)
    right_last[...] = right[deep:, :]


def last_kernel(z, table, right, total_in, panel, *refs):
    payloads, (total, turned, panel_last, *part, ints, idx, sem) = refs[:z.n_last], refs[z.n_last:]
    read_tails(payloads, ints, idx, sem)
    for n, payload in enumerate(payloads):
        fill_left(z, idx, n, piece_col(z, z.n_first + n), payload, panel_last, n * z.wide)
    for rows in halves(z.tall):
        total[rows, :] = total_in[rows, :] + jnp.dot(panel_last[rows, :], right[...], preferred_element_type=F32)
    for i in range(z.rows):
        rows = slice(i * z.bs, (i + 1) * z.bs)
        for j in range(z.bc):
            cols = slice(j * z.bs, (j + 1) * z.bs)
            turned[cols, rows] = total[rows, cols].T.astype(BF16)
    one_part(z, table, z.n_row - 1, turned, panel, panel_last, part)


def parts_kernel(z, table, turned, panel, panel_last, *refs):
    cuts = len(refs) // (z.n_row - 2)
    for n in range(1, z.n_row - 1):
        one_part(z, table, n, turned, panel, panel_last, refs[(n - 1) * cuts:n * cuts])


def one_part(z, table, n, turned, panel, panel_last, out):
    row = lax.axis_index("row") ^ n
    per, per_out = z.n_col // z.n_row, z.rows // len(out)
    me = lax.axis_index("col")

    def blocks(t, source, first):
        for b in range(z.bc):
            i = t * z.bc + b
            wanted = [turned[lanes(z, table[n, s, i] - me * z.bc), :] for s in range(z.ka)]
            column = source[:, lanes(z, first * z.bc + b)]
            terms = jnp.dot(jnp.concatenate(wanted, axis=0), column, preferred_element_type=F32)
            for s in range(z.ka):
                ref = out[i // per_out]
                ref[i % per_out, s] = terms[s * z.bs:(s + 1) * z.bs, :].astype(ref.dtype)

    for t in range(per):
        piece = piece_of(z, row * per + t)
        pl.when(piece < z.n_first)(functools.partial(blocks, t, panel, piece))
        pl.when(piece >= z.n_first)(functools.partial(blocks, t, panel_last, piece - z.n_first))


def filtered(z, filt, total, i, s):
    me = lax.axis_index("col")
    return total[i * z.bs:(i + 1) * z.bs, lanes(z, filt[s, i] - me * z.bc)].astype(BF16)


def base_kernel(z, table, filt, total, turned, panel, panel_last, mixed, direct, own, held, sem):
    me = lax.axis_index("col")
    for i in range(z.rows):
        for s in range(z.kf):
            held[i, s] = filtered(z, filt, total, i, s)
    copy = pltpu.make_async_copy(held, mixed, sem)
    copy.start()
    for i in range(z.rows):
        for s in range(z.ka):
            direct[i, s] = 3.0 * total[i * z.bs:(i + 1) * z.bs, lanes(z, table[0, s, i] - me * z.bc)]
    one_part(z, table, 0, turned, panel, panel_last, [own])
    copy.wait()


def square_kernel(z, counts, table, filt, panel, panel_last, *refs):
    squared, right, total, held, sems = refs[sum(counts):]
    fill_right(z, 0, z.ka, table, group(refs, counts), range(z.n_row), functools.partial(by_piece, z), right)
    deep = z.n_first * z.wide
    copies = []
    for n, rows in enumerate(halves(z.tall)):
        total[rows, :] = jnp.dot(panel[rows, :], right[0:deep, :], preferred_element_type=F32)
        total[rows, :] += jnp.dot(panel_last[rows, :], right[deep:, :], preferred_element_type=F32)
        here = halves(z.rows)[n]
        for i in range(here.start, here.stop):
            for s in range(z.kf):
                held[i, s] = filtered(z, filt, total, i, s)
        copies.append(pltpu.make_async_copy(held.at[here], squared.at[here], sems.at[n]))
        copies[-1].start()
    for copy in copies:
        copy.wait()


def add_kernel(z, x_0, x_1, y_0, y_1, x_out, y_out):
    x_out[...] = (x_0[...].astype(F32) + x_1[...].astype(F32)).astype(x_out.dtype)
    y_out[...] = (y_0[...].astype(F32) + y_1[...].astype(F32)).astype(y_out.dtype)


def gradient_kernel(z, direct, own, *refs):
    terms, out = refs[:-1], refs[-1]
    half = z.rows // 2
    here = [t for t in terms if t.shape[0] == z.rows]
    cut = [t for t in terms if t.shape[0] < z.rows]
    for i in range(z.rows):
        for s in range(z.ka):
            cubic = own[i, s]
            for block in [t[i, s] for t in here] + [t[i % half, s] for t in cut[i // half::2]]:
                cubic += block.astype(F32)
            out[i, s] = (direct[i, s] - 2.0 * cubic.T).astype(out.dtype)


def local(n_row, n_col, density, density_cols, hamilton, hamilton_cols, filter_cols):
    z = Sizes(n_row, n_col, density, hamilton, filter_cols)
    block = (z.bs, z.bs)
    shape = jax.ShapeDtypeStruct
    smem = pl.BlockSpec(memory_space=pltpu.SMEM)
    vmem = pl.BlockSpec(memory_space=pltpu.VMEM)
    anywhere = pl.BlockSpec(memory_space=pl.ANY)
    dma = pltpu.SemaphoreType.DMA
    d_rows, h_rows = z.rows * z.ka * z.bs, z.rows * z.kh * z.bs
    panel_flops = 2 * z.tall * z.wide * z.nb * z.bs
    part_flops = panel_flops // n_row

    def over_row(x, flip):
        return lax.ppermute(x, "row", [(r, r ^ flip) for r in range(n_row)])

    def next_chip(x, up):
        move = {0: up, 1: -up}
        return lax.ppermute(x, "col", [(c, (c // 2 + move[c % 2]) % z.n_chip * 2 + c % 2) for c in range(n_col)])

    def other_core(x):
        return lax.ppermute(x, "col", [(c, c ^ 1) for c in range(n_col)])

    flat = density.reshape(d_rows, z.bs)

    def pack(vals, cols, name):
        rows = vals.shape[0]
        outs = [shape((rows + TAIL, z.bs), BF16)]
        scratch = [pltpu.VMEM((TAIL, z.bs), F32)]
        return call(functools.partial(pack_kernel, z), [vals, *cols], outs, scratch, [vmem] * (1 + len(cols)), [vmem], 0, name)[0]

    d_pay = pack(flat, [density_cols.T], "pack_d")
    h_pay = pack(hamilton.reshape(h_rows, z.bs), [density_cols.T, hamilton_cols.T], "pack_h")

    flips = sorted(range(1, n_row), key=int.bit_count)
    single = [flip for flip in flips if flip.bit_count() == 1]
    h_half, d_half = h_rows // 2, d_rows // 2

    def forward(blocks):
        for flip in flips:
            if flip not in blocks:
                blocks[flip] = [over_row(blocks[flip & (flip - 1)][0], flip & -flip)]

    pieces = [d_pay, next_chip(d_pay, 1)]
    h_right = {0: [h_pay]}
    for flip in single:
        h_right[flip] = [over_row(h_pay, flip)]
    pieces.append(next_chip(d_pay, -1))
    pieces[1], h_right, twin = lax.optimization_barrier((pieces[1], h_right, other_core(d_pay)))
    if n_row == 4:
        h_right[3] = [over_row(h_right[1][0][:h_half], 2), over_row(h_right[2][0][h_half:], 1)]
    forward(h_right)
    d_0, pieces[2] = lax.optimization_barrier((d_pay, pieces[2]))
    for step in range(3, z.n_chip):
        pieces.append(next_chip(pieces[step - 2], 1 if step % 2 else -1))
    d_right = {0: [d_0]}
    for flip in single:
        d_right[flip] = [over_row(d_0, flip)]
    left = []
    for step, piece in enumerate(pieces):
        left.append(piece)
        if step < z.n_chip - 1:
            left.append(other_core(piece) if step else twin)
    h_right = [h_right[flip] for flip in range(n_row)]

    n_pay = z.n_first + n_row
    total, panel, right_last, table = call(
        functools.partial(first_kernel, z, [len(x) for x in h_right]),
        [*left[:z.n_first], *sum(h_right, [])],
        [
            shape((z.tall, z.wide), F32),
            shape((z.tall, z.n_first * z.wide), BF16),
            shape((z.n_last * z.wide, z.wide), BF16),
            shape((n_row, 8, z.bs), jnp.int32),
        ],
        [
            pltpu.VMEM((z.nb * z.bs, z.wide), BF16),
            pltpu.VMEM((n_pay, 8, z.bs), jnp.int32),
            pltpu.SMEM((n_pay, 8, z.bs), jnp.int32),
            dma,
        ],
        [vmem] * (z.n_first + sum(map(len, h_right))), [vmem] * 4, 0, "first",
    )
    last, total = lax.optimization_barrier((left[-1], total))
    if n_row == 4:
        d_right[3] = [over_row(d_right[1][0][:d_half], 2), over_row(d_right[2][0][d_half:d_rows], 1)]
    forward(d_right)
    d_right = [d_right[flip] for flip in range(n_row)]
    part = shape((z.rows, z.ka) + block, BF16)
    cuts = 2 if n_row == 4 and z.rows % 2 == 0 else 1
    cut_part = shape((z.rows // cuts, z.ka) + block, BF16)
    total, turned, panel_last, *far = call(
        functools.partial(last_kernel, z),
        [table, right_last, total, panel, *left[z.n_first:-1], last, other_core(last)],
        [shape((z.tall, z.wide), F32), shape((z.wide, z.tall), BF16), shape((z.tall, z.n_last * z.wide), BF16)]
        + [cut_part] * cuts,
        [
            pltpu.VMEM((z.n_last, 8, z.bs), jnp.int32),
            pltpu.SMEM((z.n_last, 8, z.bs), jnp.int32),
            dma,
        ],
        [smem] + [vmem] * (3 + z.n_last), [vmem] * (3 + cuts), panel_flops // 4 + part_flops, "last",
    )
    near = call(
        functools.partial(parts_kernel, z), [table, turned, panel, panel_last], [cut_part] * (cuts * (n_row - 2)), [],
        [smem] + [vmem] * 3, [vmem] * (cuts * (n_row - 2)), part_flops * (n_row - 2), "parts",
    )
    near, d_right = lax.optimization_barrier((near, d_right))
    if cuts == 2:
        far = over_row(far[0], 1), over_row(far[1], 2)
        x_0, y_1 = over_row(near[0], 1), over_row(near[3], 2)
    else:
        received = [over_row(term, n + 1) for n, term in enumerate([*near, *far])]
    whole_part = shape((z.rows, z.ka) + block, F32)
    mixed, direct, own = call(
        functools.partial(base_kernel, z),
        [table, filter_cols.T, total, turned, panel, panel_last],
        [shape((z.rows, z.kf) + block, BF16), whole_part, whole_part],
        [pltpu.VMEM((z.rows, z.kf) + block, BF16), dma],
        [smem] * 2 + [vmem] * 4, [anywhere, vmem, vmem], part_flops, "base",
    )
    if cuts == 2:
        y_0, x_1 = call(
            functools.partial(add_kernel, z), [near[2], far[0], near[1], far[1]], [cut_part] * 2, [],
            [vmem] * 4, [vmem] * 2, 0, "add",
        )
        received = [x_0, over_row(x_1, 1), over_row(y_0, 2), y_1]
    squared, = call(
        functools.partial(square_kernel, z, [len(x) for x in d_right]),
        [table, filter_cols.T, panel, panel_last, *sum(d_right, [])],
        [shape((z.rows, z.kf) + block, BF16)],
        [
            pltpu.VMEM((z.nb * z.bs, z.wide), BF16), pltpu.VMEM((z.tall, z.wide), F32),
            pltpu.VMEM((z.rows, z.kf) + block, BF16), dma((2,)),
        ],
        [smem] * 2 + [vmem] * (2 + sum(map(len, d_right))), [anywhere], panel_flops, "squared",
    )
    gradient, = call(
        functools.partial(gradient_kernel, z), [direct, own, *received], [part], [],
        [vmem] * (2 + len(received)), [vmem], 0, "gradient",
    )
    return squared, mixed, gradient


def solution(mesh):
    spec4 = P("row", "col", None, None)
    spec2 = P("row", "col")
    body = functools.partial(local, mesh.shape["row"], mesh.shape["col"])
    return jax.shard_map(
        body,
        mesh=mesh,
        in_specs=(spec4, spec2, spec4, spec2, spec2),
        out_specs=(spec4, spec4, spec4),
        check_vma=False,
    )
```

```python
import functools
import math

import jax
import jax.numpy as jnp
from jax import lax
from jax.experimental import pallas as pl
from jax.experimental.pallas import tpu as pltpu
from jax.sharding import PartitionSpec as P

VMEM_ROOM = 6 * 1024 * 1024
N_LAST = 2
TAIL = 16
BF16, F32 = jnp.bfloat16, jnp.float32


class Sizes:
    def __init__(self, n_row, n_col, density, hamilton, filt):
        self.n_row, self.n_col, self.n_chip = n_row, n_col, n_col // 2
        self.rows, self.ka, self.bs = density.shape[0], density.shape[1], density.shape[2]
        self.kh, self.kf = hamilton.shape[1], filt.shape[1]
        self.nb = self.rows * n_row
        self.bc = self.nb // n_col
        self.tall, self.wide = self.rows * self.bs, self.bc * self.bs
        self.n_first, self.n_last = n_col - N_LAST, N_LAST


def call(kernel, ins, outs, scratch, in_specs, out_specs, flops, name):
    held = [x for x in scratch if getattr(x, "memory_space", None) == pltpu.VMEM]
    held += [x for x, spec in zip(list(ins) + outs, in_specs + out_specs) if spec.memory_space == pltpu.VMEM]
    size = sum(math.prod(x.shape) * jnp.dtype(x.dtype).itemsize for x in held)
    return pl.pallas_call(
        kernel,
        out_shape=outs,
        in_specs=in_specs,
        out_specs=out_specs,
        scratch_shapes=scratch,
        compiler_params=pltpu.CompilerParams(vmem_limit_bytes=size + VMEM_ROOM),
        cost_estimate=pl.CostEstimate(flops=flops, bytes_accessed=1024, transcendentals=0),
        name=name,
    )(*ins)


def lanes(z, block):
    return pl.ds(pl.multiple_of(block * z.bs, z.bs), z.bs)


def block_rows(z, i, s, slots):
    return slice((i * slots + s) * z.bs, (i * slots + s + 1) * z.bs)


def piece_col(z, n):
    me = lax.axis_index("col")
    hops, core = (n // 2 + 1) // 2, lax.rem(me, 2) ^ (n % 2)
    up = lax.rem(me // 2 + hops, z.n_chip)
    down = lax.rem(me // 2 + z.n_chip - hops, z.n_chip)
    behind = 0 if n // 2 % 2 else 1
    return jnp.where(core == behind, down, up) * 2 + core


def piece_of(z, col):
    me = lax.axis_index("col")
    chip, core = col // 2, lax.rem(col, 2)
    up = lax.rem(chip - me // 2 + z.n_chip, z.n_chip)
    down = lax.rem(me // 2 - chip + z.n_chip, z.n_chip)
    hops = jnp.where(core == 0, down, up)
    step = jnp.where(2 * hops <= z.n_chip, jnp.maximum(2 * hops - 1, 0), 2 * (z.n_chip - hops))
    return step * 2 + (core ^ lax.rem(me, 2))


def pack_kernel(z, slots, first, last, *refs):
    cols_in, vals_in, (out, tail) = refs[:len(slots)], refs[len(slots):-2], refs[-2:]
    tail[...] = jnp.zeros_like(tail)
    at = 0
    for cols, count in zip(cols_in, slots):
        tail[at:at + count, 0:z.rows] = cols[...].astype(F32)
        at += count
    out[0:first, :] = vals_in[0][...]
    out[first:first + TAIL, :] = tail[...].astype(BF16)
    if last:
        out[first + TAIL:, :] = vals_in[1][...]


def read_tails(payloads, ints, idx, sem):
    for n, (ref, row) in enumerate(payloads):
        ints[n] = ref[row:row + TAIL, :].astype(F32).astype(jnp.int32)[0:8, :]
    copy = pltpu.make_async_copy(ints, idx, sem)
    copy.start()
    copy.wait()


def fill_left(z, idx, n, col, blocks, dense, first):
    zero = jnp.zeros((z.bs, z.wide), BF16)
    for i in range(z.rows):
        rows = slice(i * z.bs, (i + 1) * z.bs)
        dense[rows, first:first + z.wide] = zero
        for s in range(z.ka):
            k = idx[n, s, i] - col * z.bc
            at = pl.ds(pl.multiple_of(first + k * z.bs, z.bs), z.bs)
            dense[rows, at] = blocks[block_rows(z, i, s, z.ka), :]


def fill_right(z, first_slot, slots, idx, payloads, place, dense):
    dense[...] = jnp.zeros_like(dense)
    me = lax.axis_index("col")
    for flip, n, ref, row in payloads:
        for i in range(z.rows):
            at = pl.ds(pl.multiple_of(place(flip, i) * z.bs, z.bs), z.bs)
            for s in range(slots):
                j = idx[n, first_slot + s, i] - me * z.bc
                here = row + (i * slots + s) * z.bs
                dense[at, lanes(z, j)] = ref[here:here + z.bs, :]


def by_piece(z, flip, i):
    k = (lax.axis_index("row") ^ flip) * z.rows + i
    return piece_of(z, k // z.bc) * z.bc + lax.rem(k, z.bc)


def panel_at(z, piece):
    return pl.ds(pl.multiple_of(piece * z.wide, z.wide), z.wide)


def each_group(z, flips):
    per = z.n_col // z.n_row
    for n, flip in enumerate(flips):
        for t in range(per):
            rows = slice((n * per + t) * z.wide, (n * per + t + 1) * z.wide)
            yield piece_of(z, (lax.axis_index("row") ^ flip) * per + t), rows


def in_order(z, flips):
    return lambda flip, i: flips.index(flip) * z.rows + i


def halves(n):
    return [slice(0, n // 2), slice(n // 2, n)]


def first_kernel(z, near, *refs):
    left_in, right_in = refs[:z.n_first], refs[z.n_first:z.n_first + len(near)]
    total, panel, right_last, table, right, ints, idx, sem = refs[z.n_first + len(near):]
    h_rows, d_rows = z.rows * z.kh * z.bs, z.rows * z.ka * z.bs
    read_tails([(x, h_rows) for x in right_in] + [(x, d_rows) for x in left_in], ints, idx, sem)
    for n, flip in enumerate(near):
        table[flip] = ints[n]
    payloads = [(flip, n, x, 0) for n, (flip, x) in enumerate(zip(near, right_in))]
    fill_right(z, z.ka, z.kh, idx, payloads, functools.partial(by_piece, z), right)
    for n in range(z.n_first):
        fill_left(z, idx, len(near) + n, piece_col(z, n), left_in[n], panel, n * z.wide)
    deep = z.n_first * z.wide
    for rows in halves(z.tall):
        total[rows, :] = jnp.dot(panel[rows, :], right[0:deep, :], preferred_element_type=F32)
    right_last[...] = right[deep:, :]


def mid_kernel(z, near, far, table_in, total_in, panel, right_in, *refs):
    payloads, (table, total, right_last, right, ints, idx, sem) = refs[:len(far)], refs[len(far):]
    read_tails([(x, z.rows * z.kh * z.bs) for x in payloads], ints, idx, sem)
    for flip in near:
        table[flip] = table_in[flip]
    for n, flip in enumerate(far):
        table[flip] = ints[n]
    payloads = [(flip, n, x, 0) for n, (flip, x) in enumerate(zip(far, payloads))]
    fill_right(z, z.ka, z.kh, idx, payloads, in_order(z, far), right)
    total[...] = total_in[...]
    right_last[...] = right_in[...]
    for piece, rows in each_group(z, far):
        @pl.when(piece < z.n_first)
        def _():
            total[...] += jnp.dot(panel[:, panel_at(z, piece)], right[rows, :], preferred_element_type=F32)

        @pl.when(piece >= z.n_first)
        def _():
            right_last[panel_at(z, piece - z.n_first), :] = right[rows, :]


def last_kernel(z, table, right, total_in, panel, *refs):
    payloads, (total, turned, panel_last, *part, ints, idx, sem) = refs[:z.n_last], refs[z.n_last:]
    read_tails([(x, z.rows * z.ka * z.bs) for x in payloads], ints, idx, sem)
    for n, payload in enumerate(payloads):
        fill_left(z, idx, n, piece_col(z, z.n_first + n), payload, panel_last, n * z.wide)
    for rows in halves(z.tall):
        total[rows, :] = total_in[rows, :] + jnp.dot(panel_last[rows, :], right[...], preferred_element_type=F32)
    for i in range(z.rows):
        rows = slice(i * z.bs, (i + 1) * z.bs)
        for j in range(z.bc):
            cols = slice(j * z.bs, (j + 1) * z.bs)
            turned[cols, rows] = total[rows, cols].T.astype(BF16)
    one_part(z, table, z.n_row - 1, turned, panel, panel_last, part)


def parts_kernel(z, table, turned, panel, panel_last, *refs):
    cuts = len(refs) // (z.n_row - 2)
    for n in range(1, z.n_row - 1):
        one_part(z, table, n, turned, panel, panel_last, refs[(n - 1) * cuts:n * cuts])


def one_part(z, table, n, turned, panel, panel_last, out):
    row = lax.axis_index("row") ^ n
    per, per_out = z.n_col // z.n_row, z.rows // len(out)
    me = lax.axis_index("col")

    def blocks(t, source, first):
        for b in range(z.bc):
            i = t * z.bc + b
            wanted = [turned[lanes(z, table[n, s, i] - me * z.bc), :] for s in range(z.ka)]
            column = source[:, lanes(z, first * z.bc + b)]
            terms = jnp.dot(jnp.concatenate(wanted, axis=0), column, preferred_element_type=F32)
            for s in range(z.ka):
                ref = out[i // per_out]
                ref[i % per_out, s] = terms[s * z.bs:(s + 1) * z.bs, :].astype(ref.dtype)

    for t in range(per):
        piece = piece_of(z, row * per + t)
        pl.when(piece < z.n_first)(functools.partial(blocks, t, panel, piece))
        pl.when(piece >= z.n_first)(functools.partial(blocks, t, panel_last, piece - z.n_first))


def filtered(z, filt, total, i, s):
    me = lax.axis_index("col")
    return total[i * z.bs:(i + 1) * z.bs, lanes(z, filt[s, i] - me * z.bc)].astype(BF16)


def base_kernel(z, table, filt, total, turned, panel, panel_last, mixed, direct, own, held, sem):
    me = lax.axis_index("col")
    for i in range(z.rows):
        for s in range(z.kf):
            held[i, s] = filtered(z, filt, total, i, s)
    copy = pltpu.make_async_copy(held, mixed, sem)
    copy.start()
    for i in range(z.rows):
        for s in range(z.ka):
            direct[i, s] = 3.0 * total[i * z.bs:(i + 1) * z.bs, lanes(z, table[0, s, i] - me * z.bc)]
    one_part(z, table, 0, turned, panel, panel_last, [own])
    copy.wait()


def early_kernel(z, near, table, panel, *refs):
    payloads, (total, right) = refs[:-2], refs[-2:]
    payloads = [(flip, flip, x, z.rows * z.kh * z.bs + TAIL) for flip, x in zip(near, payloads)]
    fill_right(z, 0, z.ka, table, payloads, in_order(z, near), right)
    total[...] = jnp.zeros_like(total)
    for piece, rows in each_group(z, near):
        @pl.when(piece < z.n_first)
        def _():
            total[...] += jnp.dot(panel[:, panel_at(z, piece)], right[rows, :], preferred_element_type=F32)


def square_kernel(z, near, far, starts, table, filt, panel, panel_last, total_in, right_near, *refs):
    payloads, (squared, right, total, held, sem) = refs[:len(far)], refs[len(far):]
    payloads = [(flip, flip, x, start) for flip, x, start in zip(far, payloads, starts)]
    fill_right(z, 0, z.ka, table, payloads, in_order(z, far), right)
    total[...] = total_in[...]
    for piece, rows in each_group(z, near):
        @pl.when(piece >= z.n_first)
        def _():
            at = panel_at(z, piece - z.n_first)
            total[...] += jnp.dot(panel_last[:, at], right_near[rows, :], preferred_element_type=F32)
    for piece, rows in each_group(z, far):
        @pl.when(piece < z.n_first)
        def _():
            total[...] += jnp.dot(panel[:, panel_at(z, piece)], right[rows, :], preferred_element_type=F32)

        @pl.when(piece >= z.n_first)
        def _():
            at = panel_at(z, piece - z.n_first)
            total[...] += jnp.dot(panel_last[:, at], right[rows, :], preferred_element_type=F32)
    for i in range(z.rows):
        for s in range(z.kf):
            held[i, s] = filtered(z, filt, total, i, s)
    copy = pltpu.make_async_copy(held, squared, sem)
    copy.start()
    copy.wait()


def add_kernel(z, x_0, x_1, y_0, y_1, x_out, y_out):
    x_out[...] = (x_0[...].astype(F32) + x_1[...].astype(F32)).astype(x_out.dtype)
    y_out[...] = (y_0[...].astype(F32) + y_1[...].astype(F32)).astype(y_out.dtype)


def gradient_kernel(z, direct, own, *refs):
    terms, out = refs[:-1], refs[-1]
    half = z.rows // 2
    here = [t for t in terms if t.shape[0] == z.rows]
    cut = [t for t in terms if t.shape[0] < z.rows]
    for i in range(z.rows):
        for s in range(z.ka):
            cubic = own[i, s]
            for block in [t[i, s] for t in here] + [t[i % half, s] for t in cut[i // half::2]]:
                cubic += block.astype(F32)
            out[i, s] = (direct[i, s] - 2.0 * cubic.T).astype(out.dtype)


def local(n_row, n_col, density, density_cols, hamilton, hamilton_cols, filter_cols):
    z = Sizes(n_row, n_col, density, hamilton, filter_cols)
    block = (z.bs, z.bs)
    shape = jax.ShapeDtypeStruct
    smem = pl.BlockSpec(memory_space=pltpu.SMEM)
    vmem = pl.BlockSpec(memory_space=pltpu.VMEM)
    anywhere = pl.BlockSpec(memory_space=pl.ANY)
    dma = pltpu.SemaphoreType.DMA
    d_rows, h_rows = z.rows * z.ka * z.bs, z.rows * z.kh * z.bs
    panel_flops = 2 * z.tall * z.wide * z.nb * z.bs
    part_flops = panel_flops // n_row

    def over_row(x, flip):
        return lax.ppermute(x, "row", [(r, r ^ flip) for r in range(n_row)])

    def next_chip(x, up):
        move = {0: up, 1: -up}
        return lax.ppermute(x, "col", [(c, (c // 2 + move[c % 2]) % z.n_chip * 2 + c % 2) for c in range(n_col)])

    def other_core(x):
        return lax.ppermute(x, "col", [(c, c ^ 1) for c in range(n_col)])

    flat_d, flat_h = density.reshape(d_rows, z.bs), hamilton.reshape(h_rows, z.bs)

    def pack(vals, cols, name):
        first, last = vals[0].shape[0], sum(x.shape[0] for x in vals[1:])
        outs = [shape((first + TAIL + last, z.bs), BF16)]
        kernel = functools.partial(pack_kernel, z, [x.shape[0] for x in cols], first, last)
        ins = [*cols, *vals]
        return call(kernel, ins, outs, [pltpu.VMEM((TAIL, z.bs), F32)], [vmem] * len(ins), [vmem], 0, name)[0]

    d_pay = pack([flat_d], [density_cols.T], "pack_d")
    dh_pay = pack([flat_h, flat_d], [density_cols.T, hamilton_cols.T], "pack_dh")

    near = [0] + [1 << bit for bit in range(n_row.bit_length() - 1)]
    far = sorted(set(range(n_row)) - set(near), key=int.bit_count)
    pieces = [d_pay, next_chip(d_pay, 1)]
    dh = {0: dh_pay}
    for flip in near[1:]:
        dh[flip] = over_row(dh_pay, flip)
    later, dh_pay = lax.optimization_barrier((d_pay, dh_pay))
    pieces.append(next_chip(later, -1))
    for step in range(3, z.n_chip):
        pieces.append(next_chip(pieces[step - 2], 1 if step % 2 else -1))
    if n_row == 4:
        h_far, d_far = [over_row(dh[2][:h_rows + TAIL], 1)], [over_row(dh[1][h_rows + TAIL:], 2)]
        d_starts = [0]
    else:
        for flip in far:
            dh[flip] = over_row(dh[flip & (flip - 1)], flip & -flip)
        h_far = d_far = [dh[flip] for flip in far]
        d_starts = [h_rows + TAIL] * len(far)
    dh_near = [dh[flip] for flip in near]
    left = []
    for step, piece in enumerate(pieces):
        left.append(piece)
        if step < z.n_chip - 1:
            left.append(other_core(piece))

    table_shape = shape((n_row, 8, z.bs), jnp.int32)
    total_shape = shape((z.tall, z.wide), F32)
    last_shape = shape((z.n_last * z.wide, z.wide), BF16)

    def scalars(count):
        return [pltpu.VMEM((count, 8, z.bs), jnp.int32), pltpu.SMEM((count, 8, z.bs), jnp.int32), dma]

    n_pay = z.n_first + len(near)
    total, panel, right_last, table = call(
        functools.partial(first_kernel, z, near),
        [*left[:z.n_first], *dh_near],
        [total_shape, shape((z.tall, z.n_first * z.wide), BF16), last_shape, table_shape],
        [pltpu.VMEM((z.nb * z.bs, z.wide), BF16)] + scalars(n_pay),
        [vmem] * n_pay, [vmem] * 4, 0, "first",
    )
    total_early, right_near = call(
        functools.partial(early_kernel, z, near),
        [table, panel, *dh_near],
        [total_shape, shape((len(near) * z.tall, z.wide), BF16)],
        [], [smem] + [vmem] * (1 + len(near)), [vmem] * 2, 0, "early",
    )
    last, total, total_early = lax.optimization_barrier((left[-1], total, total_early))
    h_far, d_far = lax.optimization_barrier((h_far, d_far))
    table, total, right_last = call(
        functools.partial(mid_kernel, z, near, far),
        [table, total, panel, right_last, *h_far],
        [table_shape, total_shape, last_shape],
        [pltpu.VMEM((len(far) * z.tall, z.wide), BF16)] + scalars(len(far)),
        [vmem] * (4 + len(far)), [vmem] * 3, 1 * panel_flops, "mid",
    )
    part = shape((z.rows, z.ka) + block, BF16)
    cuts = 2 if n_row == 4 and z.rows % 2 == 0 else 1
    cut_part = shape((z.rows // cuts, z.ka) + block, BF16)
    total, turned, panel_last, *ends = call(
        functools.partial(last_kernel, z),
        [table, right_last, total, panel, *left[z.n_first:-1], last, other_core(last)],
        [shape((z.tall, z.wide), F32), shape((z.wide, z.tall), BF16), shape((z.tall, z.n_last * z.wide), BF16)]
        + [cut_part] * cuts,
        [
            pltpu.VMEM((z.n_last, 8, z.bs), jnp.int32),
            pltpu.SMEM((z.n_last, 8, z.bs), jnp.int32),
            dma,
        ],
        [smem] + [vmem] * (3 + z.n_last), [vmem] * (3 + cuts), panel_flops // 4 + part_flops, "last",
    )
    sums = call(
        functools.partial(parts_kernel, z), [table, turned, panel, panel_last], [cut_part] * (cuts * (n_row - 2)), [],
        [smem] + [vmem] * 3, [vmem] * (cuts * (n_row - 2)), part_flops * (n_row - 2), "parts",
    )
    if cuts == 2:
        ends = over_row(ends[0], 1), over_row(ends[1], 2)
        x_0, y_1 = over_row(sums[0], 1), over_row(sums[3], 2)
    else:
        received = [over_row(term, n + 1) for n, term in enumerate([*sums, *ends])]
    whole_part = shape((z.rows, z.ka) + block, F32)
    mixed, direct, own = call(
        functools.partial(base_kernel, z),
        [table, filter_cols.T, total, turned, panel, panel_last],
        [shape((z.rows, z.kf) + block, BF16), whole_part, whole_part],
        [pltpu.VMEM((z.rows, z.kf) + block, BF16), dma],
        [smem] * 2 + [vmem] * 4, [anywhere, vmem, vmem], part_flops, "base",
    )
    if cuts == 2:
        y_0, x_1 = call(
            functools.partial(add_kernel, z), [sums[2], ends[0], sums[1], ends[1]], [cut_part] * 2, [],
            [vmem] * 4, [vmem] * 2, 0, "add",
        )
        received = [x_0, over_row(x_1, 1), over_row(y_0, 2), y_1]
    squared, = call(
        functools.partial(square_kernel, z, near, far, d_starts),
        [table, filter_cols.T, panel, panel_last, total_early, right_near, *d_far],
        [shape((z.rows, z.kf) + block, BF16)],
        [
            pltpu.VMEM((len(far) * z.tall, z.wide), BF16), pltpu.VMEM((z.tall, z.wide), F32),
            pltpu.VMEM((z.rows, z.kf) + block, BF16), dma,
        ],
        [smem] * 2 + [vmem] * (4 + len(far)), [anywhere], panel_flops, "squared",
    )
    gradient, = call(
        functools.partial(gradient_kernel, z), [direct, own, *received], [part], [],
        [vmem] * (2 + len(received)), [vmem], 0, "gradient",
    )
    return squared, mixed, gradient


def solution(mesh):
    spec4 = P("row", "col", None, None)
    spec2 = P("row", "col")
    body = functools.partial(local, mesh.shape["row"], mesh.shape["col"])
    return jax.shard_map(
        body,
        mesh=mesh,
        in_specs=(spec4, spec2, spec4, spec2, spec2),
        out_specs=(spec4, spec4, spec4),
        check_vma=False,
    )
```

```python
import functools
import math

import jax
import jax.numpy as jnp
from jax import lax
from jax.experimental import pallas as pl
from jax.experimental.pallas import tpu as pltpu
from jax.sharding import PartitionSpec as P

VMEM_ROOM = 6 * 1024 * 1024
N_LAST = 3
TAIL = 16
BF16, F32 = jnp.bfloat16, jnp.float32


class Sizes:
    def __init__(self, n_row, n_col, density, hamilton, filt):
        self.n_row, self.n_col, self.n_chip = n_row, n_col, n_col // 2
        self.rows, self.ka, self.bs = density.shape[0], density.shape[1], density.shape[2]
        self.kh, self.kf = hamilton.shape[1], filt.shape[1]
        self.nb = self.rows * n_row
        self.bc = self.nb // n_col
        self.tall, self.wide = self.rows * self.bs, self.bc * self.bs
        self.n_first, self.n_last = n_col - N_LAST, N_LAST


def call(kernel, ins, outs, scratch, in_specs, out_specs, flops, name):
    held = [x for x in scratch if getattr(x, "memory_space", None) == pltpu.VMEM]
    held += [x for x, spec in zip(list(ins) + outs, in_specs + out_specs) if spec.memory_space == pltpu.VMEM]
    size = sum(math.prod(x.shape) * jnp.dtype(x.dtype).itemsize for x in held)
    return pl.pallas_call(
        kernel,
        out_shape=outs,
        in_specs=in_specs,
        out_specs=out_specs,
        scratch_shapes=scratch,
        compiler_params=pltpu.CompilerParams(vmem_limit_bytes=size + VMEM_ROOM),
        cost_estimate=pl.CostEstimate(flops=flops, bytes_accessed=1024, transcendentals=0),
        name=name,
    )(*ins)


def lanes(z, block):
    return pl.ds(pl.multiple_of(block * z.bs, z.bs), z.bs)


def block_rows(z, i, s, slots):
    return slice((i * slots + s) * z.bs, (i * slots + s + 1) * z.bs)


def piece_col(z, n):
    me = lax.axis_index("col")
    hops, core = (n // 2 + 1) // 2, lax.rem(me, 2) ^ (n % 2)
    up = lax.rem(me // 2 + hops, z.n_chip)
    down = lax.rem(me // 2 + z.n_chip - hops, z.n_chip)
    behind = 0 if n // 2 % 2 else 1
    return jnp.where(core == behind, down, up) * 2 + core


def piece_of(z, col):
    me = lax.axis_index("col")
    chip, core = col // 2, lax.rem(col, 2)
    up = lax.rem(chip - me // 2 + z.n_chip, z.n_chip)
    down = lax.rem(me // 2 - chip + z.n_chip, z.n_chip)
    hops = jnp.where(core == 0, down, up)
    step = jnp.where(2 * hops <= z.n_chip, jnp.maximum(2 * hops - 1, 0), 2 * (z.n_chip - hops))
    return step * 2 + (core ^ lax.rem(me, 2))


def pack_kernel(z, vals_in, *refs):
    cols_in, (out, tail) = refs[:-2], refs[-2:]
    tail[...] = jnp.zeros_like(tail)
    first = 0
    for cols in cols_in:
        count = cols.shape[0]
        tail[first:first + count, 0:z.rows] = cols[...].astype(F32)
        first += count
    rows = vals_in.shape[0]
    out[rows:rows + TAIL, :] = tail[...].astype(BF16)
    out[0:rows, :] = vals_in[...]


def read_tails(payloads, ints, idx, sem):
    for n, ref in enumerate(payloads):
        rows = ref.shape[0] - TAIL
        ints[n] = ref[rows:rows + TAIL, :].astype(F32).astype(jnp.int32)[0:8, :]
    copy = pltpu.make_async_copy(ints, idx, sem)
    copy.start()
    copy.wait()


def fill_left(z, idx, n, col, blocks, dense, dense_t, first):
    zero, zero_t = jnp.zeros((z.bs, z.wide), BF16), jnp.zeros((z.wide, z.bs), BF16)
    for i in range(z.rows):
        rows = slice(i * z.bs, (i + 1) * z.bs)
        dense[rows, first:first + z.wide] = zero
        if dense_t is not None:
            dense_t[first:first + z.wide, rows] = zero_t
        for s in range(z.ka):
            k = idx[n, s, i] - col * z.bc
            at = pl.ds(pl.multiple_of(first + k * z.bs, z.bs), z.bs)
            block = blocks[block_rows(z, i, s, z.ka), :]
            dense[rows, at] = block
            if dense_t is not None:
                dense_t[at, rows] = block.T


def fill_right(z, first_slot, slots, idx, payloads, flips, place, dense):
    dense[...] = jnp.zeros_like(dense)
    me = lax.axis_index("col")
    for flip, payload in zip(flips, payloads):
        for i in range(z.rows):
            at = pl.ds(pl.multiple_of(place(flip, i) * z.bs, z.bs), z.bs)
            for s in range(slots):
                j = idx[flip, first_slot + s, i] - me * z.bc
                row, part = (i * slots + s) * z.bs, 0
                while row >= payload[part].shape[0]:
                    row -= payload[part].shape[0]
                    part += 1
                dense[at, lanes(z, j)] = payload[part][row:row + z.bs, :]


def by_piece(z, flip, i):
    k = (lax.axis_index("row") ^ flip) * z.rows + i
    return piece_of(z, k // z.bc) * z.bc + lax.rem(k, z.bc)


def group(refs, counts):
    refs = iter(refs)
    return [[next(refs) for _ in range(count)] for count in counts]


def halves(n):
    return [slice(0, n // 2), slice(n // 2, n)]


def first_kernel(z, counts, *refs):
    left_in, right_in = refs[:z.n_first], group(refs[z.n_first:], counts)
    total, panel, panel_t, right_last, table, right, ints, idx, sem = refs[z.n_first + sum(counts):]
    read_tails([x[-1] for x in right_in] + list(left_in), ints, idx, sem)
    table[...] = ints[0:z.n_row]
    fill_right(z, z.ka, z.kh, idx, right_in, range(z.n_row), functools.partial(by_piece, z), right)
    for n in range(z.n_first):
        fill_left(z, idx, z.n_row + n, piece_col(z, n), left_in[n], panel, None, n * z.wide)
    deep = z.n_first * z.wide
    for rows in halves(z.tall):
        total[rows, :] = jnp.dot(panel[rows, :], right[0:deep, :], preferred_element_type=F32)

    def turn(n, _):
        for i in range(z.rows):
            rows = slice(i * z.bs, (i + 1) * z.bs)
            at = pl.ds(pl.multiple_of(n * z.wide, z.wide), z.wide)
            panel_t[at, rows] = panel[rows, at].T
        return 0

    lax.fori_loop(0, z.n_first, turn, 0)
    right_last[...] = right[deep:, :]


def last_kernel(z, table, right, total_in, panel_t, *refs):
    payloads, (total, m16, panel_last, panel_last_t, *part, ints, idx, sem) = refs[:z.n_last], refs[z.n_last:]
    read_tails(payloads, ints, idx, sem)
    for n, payload in enumerate(payloads):
        fill_left(z, idx, n, piece_col(z, z.n_first + n), payload, panel_last, panel_last_t, n * z.wide)
    for rows in halves(z.tall):
        total[rows, :] = total_in[rows, :] + jnp.dot(panel_last[rows, :], right[...], preferred_element_type=F32)
        m16[rows, :] = total[rows, :].astype(BF16)
    one_part(z, table, z.n_row - 1, m16, panel_t, panel_last_t, part)


def parts_kernel(z, table, m16, panel_t, panel_last_t, *refs):
    cuts = len(refs) // (z.n_row - 2)
    for n in range(1, z.n_row - 1):
        one_part(z, table, n, m16, panel_t, panel_last_t, refs[(n - 1) * cuts:n * cuts])


def one_part(z, table, n, m16, panel_t, panel_last_t, out):
    row = lax.axis_index("row") ^ n
    per, per_out = z.n_col // z.n_row, z.rows // len(out)
    me = lax.axis_index("col")

    def blocks(t, source, first):
        for b in range(z.bc):
            i = t * z.bc + b
            wanted = [m16[:, lanes(z, table[n, s, i] - me * z.bc)] for s in range(z.ka)]
            terms = jnp.dot(
                source[lanes(z, first * z.bc + b), :], jnp.concatenate(wanted, axis=1), preferred_element_type=F32
            )
            for s in range(z.ka):
                ref = out[i // per_out]
                ref[i % per_out, s] = terms[:, s * z.bs:(s + 1) * z.bs].astype(ref.dtype)

    for t in range(per):
        piece = piece_of(z, row * per + t)
        pl.when(piece < z.n_first)(functools.partial(blocks, t, panel_t, piece))
        pl.when(piece >= z.n_first)(functools.partial(blocks, t, panel_last_t, piece - z.n_first))


def filtered(z, filt, total, i, s):
    me = lax.axis_index("col")
    return total[i * z.bs:(i + 1) * z.bs, lanes(z, filt[s, i] - me * z.bc)].astype(BF16)


def base_kernel(z, table, filt, total, m16, panel_t, panel_last_t, mixed, base, held, sem):
    me = lax.axis_index("col")
    for i in range(z.rows):
        for s in range(z.kf):
            held[i, s] = filtered(z, filt, total, i, s)
    copy = pltpu.make_async_copy(held, mixed, sem)
    copy.start()
    one_part(z, table, 0, m16, panel_t, panel_last_t, [base])
    for i in range(z.rows):
        for s in range(z.ka):
            direct = total[i * z.bs:(i + 1) * z.bs, lanes(z, table[0, s, i] - me * z.bc)]
            base[i, s] = 3.0 * direct - 2.0 * base[i, s]
    copy.wait()


def square_kernel(z, counts, table, filt, panel, panel_last, *refs):
    squared, right, total, held, sems = refs[sum(counts):]
    fill_right(z, 0, z.ka, table, group(refs, counts), range(z.n_row), functools.partial(by_piece, z), right)
    deep = z.n_first * z.wide
    copies = []
    for n, rows in enumerate(halves(z.tall)):
        total[rows, :] = jnp.dot(panel[rows, :], right[0:deep, :], preferred_element_type=F32)
        total[rows, :] += jnp.dot(panel_last[rows, :], right[deep:, :], preferred_element_type=F32)
        here = halves(z.rows)[n]
        for i in range(here.start, here.stop):
            for s in range(z.kf):
                held[i, s] = filtered(z, filt, total, i, s)
        copies.append(pltpu.make_async_copy(held.at[here], squared.at[here], sems.at[n]))
        copies[-1].start()
    for copy in copies:
        copy.wait()


def add_kernel(z, x_0, x_1, y_0, y_1, x_out, y_out):
    x_out[...] = (x_0[...].astype(F32) + x_1[...].astype(F32)).astype(x_out.dtype)
    y_out[...] = (y_0[...].astype(F32) + y_1[...].astype(F32)).astype(y_out.dtype)


def gradient_kernel(z, base, *refs):
    terms, out = refs[:-1], refs[-1]
    half = z.rows // 2
    here = [t for t in terms if t.shape[0] == z.rows]
    cut = [t for t in terms if t.shape[0] < z.rows]
    for i in range(z.rows):
        for s in range(z.ka):
            blocks = [t[i, s] for t in here] + [t[i % half, s] for t in cut[i // half::2]]
            cubic = sum(block.astype(F32) for block in blocks)
            out[i, s] = (base[i, s] - 2.0 * cubic).astype(out.dtype)


def local(n_row, n_col, density, density_cols, hamilton, hamilton_cols, filter_cols):
    z = Sizes(n_row, n_col, density, hamilton, filter_cols)
    block = (z.bs, z.bs)
    shape = jax.ShapeDtypeStruct
    smem = pl.BlockSpec(memory_space=pltpu.SMEM)
    vmem = pl.BlockSpec(memory_space=pltpu.VMEM)
    anywhere = pl.BlockSpec(memory_space=pl.ANY)
    dma = pltpu.SemaphoreType.DMA
    d_rows, h_rows = z.rows * z.ka * z.bs, z.rows * z.kh * z.bs
    panel_flops = 2 * z.tall * z.wide * z.nb * z.bs
    part_flops = panel_flops // n_row

    def over_row(x, flip):
        return lax.ppermute(x, "row", [(r, r ^ flip) for r in range(n_row)])

    def next_chip(x, up):
        move = {0: up, 1: -up}
        return lax.ppermute(x, "col", [(c, (c // 2 + move[c % 2]) % z.n_chip * 2 + c % 2) for c in range(n_col)])

    def other_core(x):
        return lax.ppermute(x, "col", [(c, c ^ 1) for c in range(n_col)])

    flat = density.reshape(d_rows, z.bs)

    def pack(vals, cols, name):
        rows = vals.shape[0]
        outs = [shape((rows + TAIL, z.bs), BF16)]
        scratch = [pltpu.VMEM((TAIL, z.bs), F32)]
        return call(functools.partial(pack_kernel, z), [vals, *cols], outs, scratch, [vmem] * (1 + len(cols)), [vmem], 0, name)[0]

    d_pay = pack(flat, [density_cols.T], "pack_d")
    h_pay = pack(hamilton.reshape(h_rows, z.bs), [density_cols.T, hamilton_cols.T], "pack_h")

    flips = sorted(range(1, n_row), key=int.bit_count)
    single = [flip for flip in flips if flip.bit_count() == 1]
    h_half, d_half = h_rows // 2, d_rows // 2

    def forward(blocks):
        for flip in flips:
            if flip not in blocks:
                blocks[flip] = [over_row(blocks[flip & (flip - 1)][0], flip & -flip)]

    pieces = [d_pay, next_chip(d_pay, 1)]
    h_right = {0: [h_pay]}
    for flip in single:
        h_right[flip] = [over_row(h_pay, flip)]
    pieces.append(next_chip(d_pay, -1))
    pieces[1], h_right, twin = lax.optimization_barrier((pieces[1], h_right, other_core(d_pay)))
    if n_row == 4:
        h_right[3] = [over_row(h_right[1][0][:h_half], 2), over_row(h_right[2][0][h_half:], 1)]
    forward(h_right)
    d_0, pieces[2] = lax.optimization_barrier((d_pay, pieces[2]))
    for step in range(3, z.n_chip):
        pieces.append(next_chip(pieces[step - 2], 1 if step % 2 else -1))
    d_right = {0: [d_0]}
    for flip in single:
        d_right[flip] = [over_row(d_0, flip)]
    left = []
    for step, piece in enumerate(pieces):
        left.append(piece)
        if step < z.n_chip - 1:
            left.append(other_core(piece) if step else twin)
    h_right = [h_right[flip] for flip in range(n_row)]

    n_pay = z.n_first + n_row
    total, panel, panel_t, right_last, table = call(
        functools.partial(first_kernel, z, [len(x) for x in h_right]),
        [*left[:z.n_first], *sum(h_right, [])],
        [
            shape((z.tall, z.wide), F32),
            shape((z.tall, z.n_first * z.wide), BF16),
            shape((z.n_first * z.wide, z.tall), BF16),
            shape((z.n_last * z.wide, z.wide), BF16),
            shape((n_row, 8, z.bs), jnp.int32),
        ],
        [
            pltpu.VMEM((z.nb * z.bs, z.wide), BF16),
            pltpu.VMEM((n_pay, 8, z.bs), jnp.int32),
            pltpu.SMEM((n_pay, 8, z.bs), jnp.int32),
            dma,
        ],
        [vmem] * (z.n_first + sum(map(len, h_right))), [vmem] * 5, 0, "first",
    )
    last, total = lax.optimization_barrier((left[-1], total))
    if n_row == 4:
        d_right[3] = [over_row(d_right[1][0][:d_half], 2), over_row(d_right[2][0][d_half:d_rows], 1)]
    forward(d_right)
    d_right = [d_right[flip] for flip in range(n_row)]
    part = shape((z.rows, z.ka) + block, BF16)
    cuts = 2 if n_row == 4 and z.rows % 2 == 0 else 1
    cut_part = shape((z.rows // cuts, z.ka) + block, BF16)
    total, m16, panel_last, panel_last_t, *far = call(
        functools.partial(last_kernel, z),
        [table, right_last, total, panel_t, *left[z.n_first:-1], last, other_core(last)],
        [
            shape((z.tall, z.wide), F32), shape((z.tall, z.wide), BF16),
            shape((z.tall, z.n_last * z.wide), BF16), shape((z.n_last * z.wide, z.tall), BF16),
        ] + [cut_part] * cuts,
        [
            pltpu.VMEM((z.n_last, 8, z.bs), jnp.int32),
            pltpu.SMEM((z.n_last, 8, z.bs), jnp.int32),
            dma,
        ],
        [smem] + [vmem] * (3 + z.n_last), [vmem] * (4 + cuts), panel_flops // 4 + part_flops, "last",
    )
    near = call(
        functools.partial(parts_kernel, z), [table, m16, panel_t, panel_last_t], [cut_part] * (cuts * (n_row - 2)), [],
        [smem] + [vmem] * 3, [vmem] * (cuts * (n_row - 2)), part_flops * (n_row - 2), "parts",
    )
    near, d_right = lax.optimization_barrier((near, d_right))
    if cuts == 2:
        far = over_row(far[0], 1), over_row(far[1], 2)
        x_0, y_1 = over_row(near[0], 1), over_row(near[3], 2)
    else:
        received = [over_row(term, n + 1) for n, term in enumerate([*near, *far])]
    mixed, base = call(
        functools.partial(base_kernel, z),
        [table, filter_cols.T, total, m16, panel_t, panel_last_t],
        [shape((z.rows, z.kf) + block, BF16), shape((z.rows, z.ka) + block, F32)],
        [pltpu.VMEM((z.rows, z.kf) + block, BF16), dma],
        [smem] * 2 + [vmem] * 4, [anywhere, vmem], part_flops, "base",
    )
    if cuts == 2:
        y_0, x_1 = call(
            functools.partial(add_kernel, z), [near[2], far[0], near[1], far[1]], [cut_part] * 2, [],
            [vmem] * 4, [vmem] * 2, 0, "add",
        )
        received = [x_0, over_row(x_1, 1), over_row(y_0, 2), y_1]
    squared, = call(
        functools.partial(square_kernel, z, [len(x) for x in d_right]),
        [table, filter_cols.T, panel, panel_last, *sum(d_right, [])],
        [shape((z.rows, z.kf) + block, BF16)],
        [
            pltpu.VMEM((z.nb * z.bs, z.wide), BF16), pltpu.VMEM((z.tall, z.wide), F32),
            pltpu.VMEM((z.rows, z.kf) + block, BF16), dma((2,)),
        ],
        [smem] * 2 + [vmem] * (2 + sum(map(len, d_right))), [anywhere], panel_flops, "squared",
    )
    gradient, = call(
        functools.partial(gradient_kernel, z), [base, *received], [part], [],
        [vmem] * (1 + len(received)), [vmem], 0, "gradient",
    )
    return squared, mixed, gradient


def solution(mesh):
    spec4 = P("row", "col", None, None)
    spec2 = P("row", "col")
    body = functools.partial(local, mesh.shape["row"], mesh.shape["col"])
    return jax.shard_map(
        body,
        mesh=mesh,
        in_specs=(spec4, spec2, spec4, spec2, spec2),
        out_specs=(spec4, spec4, spec4),
        check_vma=False,
    )
```

```python
import functools
import math

import jax
import jax.numpy as jnp
from jax import lax
from jax.experimental import pallas as pl
from jax.experimental.pallas import tpu as pltpu
from jax.sharding import PartitionSpec as P

VMEM_ROOM = 6 * 1024 * 1024
N_LAST = 3
TAIL = 16
BF16, F32 = jnp.bfloat16, jnp.float32


class Sizes:
    def __init__(self, n_row, n_col, density, hamilton, filt):
        self.n_row, self.n_col, self.n_chip = n_row, n_col, n_col // 2
        self.rows, self.ka, self.bs = density.shape[0], density.shape[1], density.shape[2]
        self.kh, self.kf = hamilton.shape[1], filt.shape[1]
        self.nb = self.rows * n_row
        self.bc = self.nb // n_col
        self.tall, self.wide = self.rows * self.bs, self.bc * self.bs
        self.n_first, self.n_last = n_col - N_LAST, N_LAST


def call(kernel, ins, outs, scratch, in_specs, out_specs, flops, name):
    held = [x for x in scratch if getattr(x, "memory_space", None) == pltpu.VMEM]
    held += [x for x, spec in zip(list(ins) + outs, in_specs + out_specs) if spec.memory_space == pltpu.VMEM]
    size = sum(math.prod(x.shape) * jnp.dtype(x.dtype).itemsize for x in held)
    return pl.pallas_call(
        kernel,
        out_shape=outs,
        in_specs=in_specs,
        out_specs=out_specs,
        scratch_shapes=scratch,
        compiler_params=pltpu.CompilerParams(vmem_limit_bytes=size + VMEM_ROOM),
        cost_estimate=pl.CostEstimate(flops=flops, bytes_accessed=1024, transcendentals=0),
        name=name,
    )(*ins)


def lanes(z, block):
    return pl.ds(pl.multiple_of(block * z.bs, z.bs), z.bs)


def block_rows(z, i, s, slots):
    return slice((i * slots + s) * z.bs, (i * slots + s + 1) * z.bs)


def piece_col(z, n):
    me = lax.axis_index("col")
    hops, core = (n // 2 + 1) // 2, lax.rem(me, 2) ^ (n % 2)
    up = lax.rem(me // 2 + hops, z.n_chip)
    down = lax.rem(me // 2 + z.n_chip - hops, z.n_chip)
    behind = 0 if n // 2 % 2 else 1
    return jnp.where(core == behind, down, up) * 2 + core


def piece_of(z, col):
    me = lax.axis_index("col")
    chip, core = col // 2, lax.rem(col, 2)
    up = lax.rem(chip - me // 2 + z.n_chip, z.n_chip)
    down = lax.rem(me // 2 - chip + z.n_chip, z.n_chip)
    hops = jnp.where(core == 0, down, up)
    step = jnp.where(2 * hops <= z.n_chip, jnp.maximum(2 * hops - 1, 0), 2 * (z.n_chip - hops))
    return step * 2 + (core ^ lax.rem(me, 2))


def pack_kernel(z, vals_in, *refs):
    cols_in, (out, tail) = refs[:-2], refs[-2:]
    tail[...] = jnp.zeros_like(tail)
    first = 0
    for cols in cols_in:
        count = cols.shape[0]
        tail[first:first + count, 0:z.rows] = cols[...].astype(F32)
        first += count
    rows = vals_in.shape[0]
    out[rows:rows + TAIL, :] = tail[...].astype(BF16)
    out[0:rows, :] = vals_in[...]


def read_tails(payloads, ints, idx, sem):
    for n, ref in enumerate(payloads):
        rows = ref.shape[0] - TAIL
        ints[n] = ref[rows:rows + TAIL, :].astype(F32).astype(jnp.int32)[0:8, :]
    copy = pltpu.make_async_copy(ints, idx, sem)
    copy.start()
    copy.wait()


def fill_left(z, idx, n, col, blocks, dense, dense_t, first):
    zero, zero_t = jnp.zeros((z.bs, z.wide), BF16), jnp.zeros((z.wide, z.bs), BF16)
    for i in range(z.rows):
        rows = slice(i * z.bs, (i + 1) * z.bs)
        dense[rows, first:first + z.wide] = zero
        if dense_t is not None:
            dense_t[first:first + z.wide, rows] = zero_t
        for s in range(z.ka):
            k = idx[n, s, i] - col * z.bc
            at = pl.ds(pl.multiple_of(first + k * z.bs, z.bs), z.bs)
            block = blocks[block_rows(z, i, s, z.ka), :]
            dense[rows, at] = block
            if dense_t is not None:
                dense_t[at, rows] = block.T


def fill_right(z, first_slot, slots, idx, payloads, flips, place, dense):
    dense[...] = jnp.zeros_like(dense)
    me = lax.axis_index("col")
    for flip, payload in zip(flips, payloads):
        for i in range(z.rows):
            at = pl.ds(pl.multiple_of(place(flip, i) * z.bs, z.bs), z.bs)
            for s in range(slots):
                j = idx[flip, first_slot + s, i] - me * z.bc
                row, part = (i * slots + s) * z.bs, 0
                while row >= payload[part].shape[0]:
                    row -= payload[part].shape[0]
                    part += 1
                dense[at, lanes(z, j)] = payload[part][row:row + z.bs, :]


def by_piece(z, flip, i):
    k = (lax.axis_index("row") ^ flip) * z.rows + i
    return piece_of(z, k // z.bc) * z.bc + lax.rem(k, z.bc)


def group(refs, counts):
    refs = iter(refs)
    return [[next(refs) for _ in range(count)] for count in counts]


def halves(n):
    return [slice(0, n // 2), slice(n // 2, n)]


def first_kernel(z, counts, *refs):
    left_in, right_in = refs[:z.n_first], group(refs[z.n_first:], counts)
    total, panel, panel_t, right_last, table, right, ints, idx, sem = refs[z.n_first + sum(counts):]
    read_tails([x[-1] for x in right_in] + list(left_in), ints, idx, sem)
    table[...] = ints[0:z.n_row]
    fill_right(z, z.ka, z.kh, idx, right_in, range(z.n_row), functools.partial(by_piece, z), right)
    for n in range(z.n_first):
        fill_left(z, idx, z.n_row + n, piece_col(z, n), left_in[n], panel, None, n * z.wide)
    deep = z.n_first * z.wide
    for rows in halves(z.tall):
        total[rows, :] = jnp.dot(panel[rows, :], right[0:deep, :], preferred_element_type=F32)

    def turn(n, _):
        for i in range(z.rows):
            rows = slice(i * z.bs, (i + 1) * z.bs)
            at = pl.ds(pl.multiple_of(n * z.wide, z.wide), z.wide)
            panel_t[at, rows] = panel[rows, at].T
        return 0

    lax.fori_loop(0, z.n_first, turn, 0)
    right_last[...] = right[deep:, :]


def last_kernel(z, table, right, total_in, panel_t, *refs):
    payloads, (total, m16, panel_last, panel_last_t, *part, ints, idx, sem) = refs[:z.n_last], refs[z.n_last:]
    read_tails(payloads, ints, idx, sem)
    for n, payload in enumerate(payloads):
        fill_left(z, idx, n, piece_col(z, z.n_first + n), payload, panel_last, panel_last_t, n * z.wide)
    for rows in halves(z.tall):
        total[rows, :] = total_in[rows, :] + jnp.dot(panel_last[rows, :], right[...], preferred_element_type=F32)
        m16[rows, :] = total[rows, :].astype(BF16)
    one_part(z, table, z.n_row - 1, m16, panel_t, panel_last_t, part)


def parts_kernel(z, table, m16, panel_t, panel_last_t, *refs):
    cuts = len(refs) // (z.n_row - 2)
    for n in range(1, z.n_row - 1):
        one_part(z, table, n, m16, panel_t, panel_last_t, refs[(n - 1) * cuts:n * cuts])


def one_part(z, table, n, m16, panel_t, panel_last_t, out):
    row = lax.axis_index("row") ^ n
    per, per_out = z.n_col // z.n_row, z.rows // len(out)
    me = lax.axis_index("col")

    def blocks(t, source, first):
        for b in range(z.bc):
            i = t * z.bc + b
            wanted = [m16[:, lanes(z, table[n, s, i] - me * z.bc)] for s in range(z.ka)]
            terms = jnp.dot(
                source[lanes(z, first * z.bc + b), :], jnp.concatenate(wanted, axis=1), preferred_element_type=F32
            )
            for s in range(z.ka):
                ref = out[i // per_out]
                ref[i % per_out, s] = terms[:, s * z.bs:(s + 1) * z.bs].astype(ref.dtype)

    for t in range(per):
        piece = piece_of(z, row * per + t)
        pl.when(piece < z.n_first)(functools.partial(blocks, t, panel_t, piece))
        pl.when(piece >= z.n_first)(functools.partial(blocks, t, panel_last_t, piece - z.n_first))


def filtered(z, filt, total, i, s):
    me = lax.axis_index("col")
    return total[i * z.bs:(i + 1) * z.bs, lanes(z, filt[s, i] - me * z.bc)].astype(BF16)


def base_kernel(z, table, filt, total, m16, panel_t, panel_last_t, mixed, base, held, sem):
    me = lax.axis_index("col")
    for i in range(z.rows):
        for s in range(z.kf):
            held[i, s] = filtered(z, filt, total, i, s)
    copy = pltpu.make_async_copy(held, mixed, sem)
    copy.start()
    one_part(z, table, 0, m16, panel_t, panel_last_t, [base])
    for i in range(z.rows):
        for s in range(z.ka):
            direct = total[i * z.bs:(i + 1) * z.bs, lanes(z, table[0, s, i] - me * z.bc)]
            base[i, s] = 3.0 * direct - 2.0 * base[i, s]
    copy.wait()


def square_kernel(z, counts, table, filt, panel, panel_last, *refs):
    squared, right, total, held, sems = refs[sum(counts):]
    fill_right(z, 0, z.ka, table, group(refs, counts), range(z.n_row), functools.partial(by_piece, z), right)
    deep = z.n_first * z.wide
    copies = []
    for n, rows in enumerate(halves(z.tall)):
        total[rows, :] = jnp.dot(panel[rows, :], right[0:deep, :], preferred_element_type=F32)
        total[rows, :] += jnp.dot(panel_last[rows, :], right[deep:, :], preferred_element_type=F32)
        here = halves(z.rows)[n]
        for i in range(here.start, here.stop):
            for s in range(z.kf):
                held[i, s] = filtered(z, filt, total, i, s)
        copies.append(pltpu.make_async_copy(held.at[here], squared.at[here], sems.at[n]))
        copies[-1].start()
    for copy in copies:
        copy.wait()


def add_kernel(z, x_0, x_1, y_0, y_1, x_out, y_out):
    x_out[...] = (x_0[...].astype(F32) + x_1[...].astype(F32)).astype(x_out.dtype)
    y_out[...] = (y_0[...].astype(F32) + y_1[...].astype(F32)).astype(y_out.dtype)


def gradient_kernel(z, base, *refs):
    terms, out = refs[:-1], refs[-1]
    half = z.rows // 2
    here = [t for t in terms if t.shape[0] == z.rows]
    cut = [t for t in terms if t.shape[0] < z.rows]
    for i in range(z.rows):
        for s in range(z.ka):
            blocks = [t[i, s] for t in here] + [t[i % half, s] for t in cut[i // half::2]]
            cubic = sum(block.astype(F32) for block in blocks)
            out[i, s] = (base[i, s] - 2.0 * cubic).astype(out.dtype)


def local(n_row, n_col, density, density_cols, hamilton, hamilton_cols, filter_cols):
    z = Sizes(n_row, n_col, density, hamilton, filter_cols)
    block = (z.bs, z.bs)
    shape = jax.ShapeDtypeStruct
    smem = pl.BlockSpec(memory_space=pltpu.SMEM)
    vmem = pl.BlockSpec(memory_space=pltpu.VMEM)
    anywhere = pl.BlockSpec(memory_space=pl.ANY)
    dma = pltpu.SemaphoreType.DMA
    d_rows, h_rows = z.rows * z.ka * z.bs, z.rows * z.kh * z.bs
    panel_flops = 2 * z.tall * z.wide * z.nb * z.bs
    part_flops = panel_flops // n_row

    def over_row(x, flip):
        return lax.ppermute(x, "row", [(r, r ^ flip) for r in range(n_row)])

    def next_chip(x, up):
        move = {0: up, 1: -up}
        return lax.ppermute(x, "col", [(c, (c // 2 + move[c % 2]) % z.n_chip * 2 + c % 2) for c in range(n_col)])

    def other_core(x):
        return lax.ppermute(x, "col", [(c, c ^ 1) for c in range(n_col)])

    flat = density.reshape(d_rows, z.bs)

    def pack(vals, cols, name):
        rows = vals.shape[0]
        outs = [shape((rows + TAIL, z.bs), BF16)]
        scratch = [pltpu.VMEM((TAIL, z.bs), F32)]
        return call(functools.partial(pack_kernel, z), [vals, *cols], outs, scratch, [vmem] * (1 + len(cols)), [vmem], 0, name)[0]

    d_pay = pack(flat, [density_cols.T], "pack_d")
    h_pay = pack(hamilton.reshape(h_rows, z.bs), [density_cols.T, hamilton_cols.T], "pack_h")

    flips = sorted(range(1, n_row), key=int.bit_count)
    single = [flip for flip in flips if flip.bit_count() == 1]
    h_half, d_half = h_rows // 2, d_rows // 2

    def forward(blocks):
        for flip in flips:
            if flip not in blocks:
                blocks[flip] = [over_row(blocks[flip & (flip - 1)][0], flip & -flip)]

    pieces = [d_pay, next_chip(d_pay, 1)]
    h_right = {0: [h_pay]}
    for flip in single:
        h_right[flip] = [over_row(h_pay, flip)]
    pieces.append(next_chip(d_pay, -1))
    pieces[1], h_right, twin = lax.optimization_barrier((pieces[1], h_right, other_core(d_pay)))
    if n_row == 4:
        h_right[3] = [over_row(h_right[1][0][:h_half], 2), over_row(h_right[2][0][h_half:], 1)]
    forward(h_right)
    twins = [twin, other_core(pieces[1])]
    d_0, pieces[2], twins[1] = lax.optimization_barrier((d_pay, pieces[2], twins[1]))
    for step in range(3, z.n_chip):
        pieces.append(next_chip(pieces[step - 2], 1 if step % 2 else -1))
    d_right = {0: [d_0]}
    for flip in single:
        d_right[flip] = [over_row(d_0, flip)]
    left = []
    for step, piece in enumerate(pieces):
        left.append(piece)
        if step < z.n_chip - 1:
            left.append(twins[step] if step < 2 else other_core(piece))
    h_right = [h_right[flip] for flip in range(n_row)]

    n_pay = z.n_first + n_row
    total, panel, panel_t, right_last, table = call(
        functools.partial(first_kernel, z, [len(x) for x in h_right]),
        [*left[:z.n_first], *sum(h_right, [])],
        [
            shape((z.tall, z.wide), F32),
            shape((z.tall, z.n_first * z.wide), BF16),
            shape((z.n_first * z.wide, z.tall), BF16),
            shape((z.n_last * z.wide, z.wide), BF16),
            shape((n_row, 8, z.bs), jnp.int32),
        ],
        [
            pltpu.VMEM((z.nb * z.bs, z.wide), BF16),
            pltpu.VMEM((n_pay, 8, z.bs), jnp.int32),
            pltpu.SMEM((n_pay, 8, z.bs), jnp.int32),
            dma,
        ],
        [vmem] * (z.n_first + sum(map(len, h_right))), [vmem] * 5, 0, "first",
    )
    last, total = lax.optimization_barrier((left[-1], total))
    if n_row == 4:
        d_right[3] = [over_row(d_right[1][0][:d_half], 2), over_row(d_right[2][0][d_half:d_rows], 1)]
    forward(d_right)
    d_right = [d_right[flip] for flip in range(n_row)]
    part = shape((z.rows, z.ka) + block, BF16)
    cuts = 2 if n_row == 4 and z.rows % 2 == 0 else 1
    cut_part = shape((z.rows // cuts, z.ka) + block, BF16)
    total, m16, panel_last, panel_last_t, *far = call(
        functools.partial(last_kernel, z),
        [table, right_last, total, panel_t, *left[z.n_first:-1], last, other_core(last)],
        [
            shape((z.tall, z.wide), F32), shape((z.tall, z.wide), BF16),
            shape((z.tall, z.n_last * z.wide), BF16), shape((z.n_last * z.wide, z.tall), BF16),
        ] + [cut_part] * cuts,
        [
            pltpu.VMEM((z.n_last, 8, z.bs), jnp.int32),
            pltpu.SMEM((z.n_last, 8, z.bs), jnp.int32),
            dma,
        ],
        [smem] + [vmem] * (3 + z.n_last), [vmem] * (4 + cuts), panel_flops // 4 + part_flops, "last",
    )
    near = call(
        functools.partial(parts_kernel, z), [table, m16, panel_t, panel_last_t], [cut_part] * (cuts * (n_row - 2)), [],
        [smem] + [vmem] * 3, [vmem] * (cuts * (n_row - 2)), part_flops * (n_row - 2), "parts",
    )
    near, d_right = lax.optimization_barrier((near, d_right))
    if cuts == 2:
        far = over_row(far[0], 1), over_row(far[1], 2)
        x_0, y_1 = over_row(near[0], 1), over_row(near[3], 2)
    else:
        received = [over_row(term, n + 1) for n, term in enumerate([*near, *far])]
    mixed, base = call(
        functools.partial(base_kernel, z),
        [table, filter_cols.T, total, m16, panel_t, panel_last_t],
        [shape((z.rows, z.kf) + block, BF16), shape((z.rows, z.ka) + block, F32)],
        [pltpu.VMEM((z.rows, z.kf) + block, BF16), dma],
        [smem] * 2 + [vmem] * 4, [anywhere, vmem], part_flops, "base",
    )
    if cuts == 2:
        y_0, x_1 = call(
            functools.partial(add_kernel, z), [near[2], far[0], near[1], far[1]], [cut_part] * 2, [],
            [vmem] * 4, [vmem] * 2, 0, "add",
        )
        received = [x_0, over_row(x_1, 1), over_row(y_0, 2), y_1]
    squared, = call(
        functools.partial(square_kernel, z, [len(x) for x in d_right]),
        [table, filter_cols.T, panel, panel_last, *sum(d_right, [])],
        [shape((z.rows, z.kf) + block, BF16)],
        [
            pltpu.VMEM((z.nb * z.bs, z.wide), BF16), pltpu.VMEM((z.tall, z.wide), F32),
            pltpu.VMEM((z.rows, z.kf) + block, BF16), dma((2,)),
        ],
        [smem] * 2 + [vmem] * (2 + sum(map(len, d_right))), [anywhere], panel_flops, "squared",
    )
    gradient, = call(
        functools.partial(gradient_kernel, z), [base, *received], [part], [],
        [vmem] * (1 + len(received)), [vmem], 0, "gradient",
    )
    return squared, mixed, gradient


def solution(mesh):
    spec4 = P("row", "col", None, None)
    spec2 = P("row", "col")
    body = functools.partial(local, mesh.shape["row"], mesh.shape["col"])
    return jax.shard_map(
        body,
        mesh=mesh,
        in_specs=(spec4, spec2, spec4, spec2, spec2),
        out_specs=(spec4, spec4, spec4),
        check_vma=False,
    )
```

```python
import functools
import math

import jax
import jax.numpy as jnp
from jax import lax
from jax.experimental import pallas as pl
from jax.experimental.pallas import tpu as pltpu
from jax.sharding import PartitionSpec as P

VMEM_ROOM = 6 * 1024 * 1024
N_LAST = 3
TAIL = 16
BF16, F32 = jnp.bfloat16, jnp.float32


class Sizes:
    def __init__(self, n_row, n_col, density, hamilton, filt):
        self.n_row, self.n_col, self.n_chip = n_row, n_col, n_col // 2
        self.rows, self.ka, self.bs = density.shape[0], density.shape[1], density.shape[2]
        self.kh, self.kf = hamilton.shape[1], filt.shape[1]
        self.nb = self.rows * n_row
        self.bc = self.nb // n_col
        self.tall, self.wide = self.rows * self.bs, self.bc * self.bs
        self.n_first, self.n_last = n_col - N_LAST, N_LAST


def call(kernel, ins, outs, scratch, in_specs, out_specs, flops, name):
    held = [x for x in scratch if getattr(x, "memory_space", None) == pltpu.VMEM]
    held += [x for x, spec in zip(list(ins) + outs, in_specs + out_specs) if spec.memory_space == pltpu.VMEM]
    size = sum(math.prod(x.shape) * jnp.dtype(x.dtype).itemsize for x in held)
    return pl.pallas_call(
        kernel,
        out_shape=outs,
        in_specs=in_specs,
        out_specs=out_specs,
        scratch_shapes=scratch,
        compiler_params=pltpu.CompilerParams(vmem_limit_bytes=size + VMEM_ROOM),
        cost_estimate=pl.CostEstimate(flops=flops, bytes_accessed=1024, transcendentals=0),
        name=name,
    )(*ins)


def lanes(z, block):
    return pl.ds(pl.multiple_of(block * z.bs, z.bs), z.bs)


def block_rows(z, i, s, slots):
    return slice((i * slots + s) * z.bs, (i * slots + s + 1) * z.bs)


def piece_col(z, n):
    me = lax.axis_index("col")
    hops, core = (n // 2 + 1) // 2, lax.rem(me, 2) ^ (n % 2)
    up = lax.rem(me // 2 + hops, z.n_chip)
    down = lax.rem(me // 2 + z.n_chip - hops, z.n_chip)
    behind = 0 if n // 2 % 2 else 1
    return jnp.where(core == behind, down, up) * 2 + core


def piece_of(z, col):
    me = lax.axis_index("col")
    chip, core = col // 2, lax.rem(col, 2)
    up = lax.rem(chip - me // 2 + z.n_chip, z.n_chip)
    down = lax.rem(me // 2 - chip + z.n_chip, z.n_chip)
    hops = jnp.where(core == 0, down, up)
    step = jnp.where(2 * hops <= z.n_chip, jnp.maximum(2 * hops - 1, 0), 2 * (z.n_chip - hops))
    return step * 2 + (core ^ lax.rem(me, 2))


def pack_kernel(z, vals_in, *refs):
    cols_in, (out, tail) = refs[:-2], refs[-2:]
    tail[...] = jnp.zeros_like(tail)
    first = 0
    for cols in cols_in:
        count = cols.shape[0]
        tail[first:first + count, 0:z.rows] = cols[...].astype(F32)
        first += count
    rows = vals_in.shape[0]
    out[rows:rows + TAIL, :] = tail[...].astype(BF16)
    out[0:rows, :] = vals_in[...]


def read_tails(payloads, ints, idx, sem):
    for n, ref in enumerate(payloads):
        rows = ref.shape[0] - TAIL
        ints[n] = ref[rows:rows + TAIL, :].astype(F32).astype(jnp.int32)[0:8, :]
    copy = pltpu.make_async_copy(ints, idx, sem)
    copy.start()
    copy.wait()


def empty_places(z, wanted):
    if z.bc != 4 or len(wanted) != 2:
        return range(z.bc)
    a, b = wanted
    one = jnp.where((a != 0) & (b != 0), 0, jnp.where((a != 1) & (b != 1), 1, 2))
    return one, 6 - a - b - one


def fill_left(z, idx, n, col, blocks, dense, dense_t, first):
    zero = jnp.zeros((z.bs, z.bs), BF16)
    for i in range(z.rows):
        rows = slice(i * z.bs, (i + 1) * z.bs)
        wanted = [idx[n, s, i] - col * z.bc for s in range(z.ka)]
        for k in empty_places(z, wanted):
            at = pl.ds(pl.multiple_of(first + k * z.bs, z.bs), z.bs)
            dense[rows, at] = zero
            if dense_t is not None:
                dense_t[at, rows] = zero
        for s, k in enumerate(wanted):
            at = pl.ds(pl.multiple_of(first + k * z.bs, z.bs), z.bs)
            block = blocks[block_rows(z, i, s, z.ka), :]
            dense[rows, at] = block
            if dense_t is not None:
                dense_t[at, rows] = block.T


def fill_right(z, first_slot, slots, idx, payloads, flips, place, dense):
    zero = jnp.zeros((z.bs, z.bs), BF16)
    me = lax.axis_index("col")
    for flip, payload in zip(flips, payloads):
        for i in range(z.rows):
            at = pl.ds(pl.multiple_of(place(flip, i) * z.bs, z.bs), z.bs)
            wanted = [idx[flip, first_slot + s, i] - me * z.bc for s in range(slots)]
            for j in empty_places(z, wanted):
                dense[at, lanes(z, j)] = zero
            for s, j in enumerate(wanted):
                row, part = (i * slots + s) * z.bs, 0
                while row >= payload[part].shape[0]:
                    row -= payload[part].shape[0]
                    part += 1
                dense[at, lanes(z, j)] = payload[part][row:row + z.bs, :]


def by_piece(z, flip, i):
    k = (lax.axis_index("row") ^ flip) * z.rows + i
    return piece_of(z, k // z.bc) * z.bc + lax.rem(k, z.bc)


def group(refs, counts):
    refs = iter(refs)
    return [[next(refs) for _ in range(count)] for count in counts]


def halves(n):
    return [slice(0, n // 2), slice(n // 2, n)]


def first_kernel(z, counts, *refs):
    left_in, right_in = refs[:z.n_first], group(refs[z.n_first:], counts)
    total, panel, panel_t, right_last, table, right, ints, idx, sem = refs[z.n_first + sum(counts):]
    read_tails([x[-1] for x in right_in] + list(left_in), ints, idx, sem)
    table[...] = ints[0:z.n_row]
    fill_right(z, z.ka, z.kh, idx, right_in, range(z.n_row), functools.partial(by_piece, z), right)
    for n in range(z.n_first):
        fill_left(z, idx, z.n_row + n, piece_col(z, n), left_in[n], panel, None, n * z.wide)
    deep = z.n_first * z.wide
    for rows in halves(z.tall):
        total[rows, :] = jnp.dot(panel[rows, :], right[0:deep, :], preferred_element_type=F32)

    def turn(n, _):
        for i in range(z.rows):
            rows = slice(i * z.bs, (i + 1) * z.bs)
            at = pl.ds(pl.multiple_of(n * z.wide, z.wide), z.wide)
            panel_t[at, rows] = panel[rows, at].T
        return 0

    lax.fori_loop(0, z.n_first, turn, 0)
    right_last[...] = right[deep:, :]


def last_kernel(z, table, right, total_in, panel_t, *refs):
    payloads, (total, m16, panel_last, panel_last_t, *part, ints, idx, sem) = refs[:z.n_last], refs[z.n_last:]
    read_tails(payloads, ints, idx, sem)
    for n, payload in enumerate(payloads):
        fill_left(z, idx, n, piece_col(z, z.n_first + n), payload, panel_last, panel_last_t, n * z.wide)
    for rows in halves(z.tall):
        total[rows, :] = total_in[rows, :] + jnp.dot(panel_last[rows, :], right[...], preferred_element_type=F32)
        m16[rows, :] = total[rows, :].astype(BF16)
    one_part(z, table, z.n_row - 1, m16, panel_t, panel_last_t, part)


def parts_kernel(z, table, m16, panel_t, panel_last_t, *refs):
    cuts = len(refs) // (z.n_row - 2)
    for n in range(1, z.n_row - 1):
        one_part(z, table, n, m16, panel_t, panel_last_t, refs[(n - 1) * cuts:n * cuts])


def one_part(z, table, n, m16, panel_t, panel_last_t, out):
    row = lax.axis_index("row") ^ n
    per, per_out = z.n_col // z.n_row, z.rows // len(out)
    me = lax.axis_index("col")

    def blocks(t, source, first):
        for b in range(z.bc):
            i = t * z.bc + b
            wanted = [m16[:, lanes(z, table[n, s, i] - me * z.bc)] for s in range(z.ka)]
            terms = jnp.dot(
                source[lanes(z, first * z.bc + b), :], jnp.concatenate(wanted, axis=1), preferred_element_type=F32
            )
            for s in range(z.ka):
                ref = out[i // per_out]
                ref[i % per_out, s] = terms[:, s * z.bs:(s + 1) * z.bs].astype(ref.dtype)

    for t in range(per):
        piece = piece_of(z, row * per + t)
        pl.when(piece < z.n_first)(functools.partial(blocks, t, panel_t, piece))
        pl.when(piece >= z.n_first)(functools.partial(blocks, t, panel_last_t, piece - z.n_first))


def filtered(z, filt, total, i, s):
    me = lax.axis_index("col")
    return total[i * z.bs:(i + 1) * z.bs, lanes(z, filt[s, i] - me * z.bc)].astype(BF16)


def base_kernel(z, table, filt, total, m16, panel_t, panel_last_t, mixed, base, held, sem):
    me = lax.axis_index("col")
    for i in range(z.rows):
        for s in range(z.kf):
            held[i, s] = filtered(z, filt, total, i, s)
    copy = pltpu.make_async_copy(held, mixed, sem)
    copy.start()
    one_part(z, table, 0, m16, panel_t, panel_last_t, [base])
    for i in range(z.rows):
        for s in range(z.ka):
            direct = total[i * z.bs:(i + 1) * z.bs, lanes(z, table[0, s, i] - me * z.bc)]
            base[i, s] = 3.0 * direct - 2.0 * base[i, s]
    copy.wait()


def square_kernel(z, counts, table, filt, panel, panel_last, *refs):
    squared, right, total, held, sems = refs[sum(counts):]
    fill_right(z, 0, z.ka, table, group(refs, counts), range(z.n_row), functools.partial(by_piece, z), right)
    deep = z.n_first * z.wide
    copies = []
    for n, rows in enumerate(halves(z.tall)):
        term = jnp.dot(panel[rows, :], right[0:deep, :], preferred_element_type=F32)
        total[rows, :] = term + jnp.dot(panel_last[rows, :], right[deep:, :], preferred_element_type=F32)
        here = halves(z.rows)[n]
        for i in range(here.start, here.stop):
            for s in range(z.kf):
                held[i, s] = filtered(z, filt, total, i, s)
        copies.append(pltpu.make_async_copy(held.at[here], squared.at[here], sems.at[n]))
        copies[-1].start()
    for copy in copies:
        copy.wait()


def add_kernel(z, x_0, x_1, y_0, y_1, x_out, y_out):
    x_out[...] = (x_0[...].astype(F32) + x_1[...].astype(F32)).astype(x_out.dtype)
    y_out[...] = (y_0[...].astype(F32) + y_1[...].astype(F32)).astype(y_out.dtype)


def gradient_kernel(z, base, *refs):
    terms, out = refs[:-1], refs[-1]
    half = z.rows // 2
    here = [t for t in terms if t.shape[0] == z.rows]
    cut = [t for t in terms if t.shape[0] < z.rows]
    for i in range(z.rows):
        for s in range(z.ka):
            blocks = [t[i, s] for t in here] + [t[i % half, s] for t in cut[i // half::2]]
            cubic = sum(block.astype(F32) for block in blocks)
            out[i, s] = (base[i, s] - 2.0 * cubic).astype(out.dtype)


def local(n_row, n_col, density, density_cols, hamilton, hamilton_cols, filter_cols):
    z = Sizes(n_row, n_col, density, hamilton, filter_cols)
    block = (z.bs, z.bs)
    shape = jax.ShapeDtypeStruct
    smem = pl.BlockSpec(memory_space=pltpu.SMEM)
    vmem = pl.BlockSpec(memory_space=pltpu.VMEM)
    anywhere = pl.BlockSpec(memory_space=pl.ANY)
    dma = pltpu.SemaphoreType.DMA
    d_rows, h_rows = z.rows * z.ka * z.bs, z.rows * z.kh * z.bs
    panel_flops = 2 * z.tall * z.wide * z.nb * z.bs
    part_flops = panel_flops // n_row

    def over_row(x, flip):
        return lax.ppermute(x, "row", [(r, r ^ flip) for r in range(n_row)])

    def next_chip(x, up):
        move = {0: up, 1: -up}
        return lax.ppermute(x, "col", [(c, (c // 2 + move[c % 2]) % z.n_chip * 2 + c % 2) for c in range(n_col)])

    def other_core(x):
        return lax.ppermute(x, "col", [(c, c ^ 1) for c in range(n_col)])

    flat = density.reshape(d_rows, z.bs)

    def pack(vals, cols, name):
        rows = vals.shape[0]
        outs = [shape((rows + TAIL, z.bs), BF16)]
        scratch = [pltpu.VMEM((TAIL, z.bs), F32)]
        return call(functools.partial(pack_kernel, z), [vals, *cols], outs, scratch, [vmem] * (1 + len(cols)), [vmem], 0, name)[0]

    d_pay = pack(flat, [density_cols.T], "pack_d")
    h_pay = pack(hamilton.reshape(h_rows, z.bs), [density_cols.T, hamilton_cols.T], "pack_h")

    flips = sorted(range(1, n_row), key=int.bit_count)
    single = [flip for flip in flips if flip.bit_count() == 1]
    h_half, d_half = h_rows // 2, d_rows // 2

    def forward(blocks):
        for flip in flips:
            if flip not in blocks:
                blocks[flip] = [over_row(blocks[flip & (flip - 1)][0], flip & -flip)]

    pieces = [d_pay, next_chip(d_pay, 1)]
    h_right = {0: [h_pay]}
    for flip in single:
        h_right[flip] = [over_row(h_pay, flip)]
    pieces.append(next_chip(d_pay, -1))
    pieces[1], h_right, twin = lax.optimization_barrier((pieces[1], h_right, other_core(d_pay)))
    if n_row == 4:
        h_right[3] = [over_row(h_right[1][0][:h_half], 2), over_row(h_right[2][0][h_half:], 1)]
    forward(h_right)
    d_0, pieces[2] = lax.optimization_barrier((d_pay, pieces[2]))
    for step in range(3, z.n_chip):
        pieces.append(next_chip(pieces[step - 2], 1 if step % 2 else -1))
    d_right = {0: [d_0]}
    for flip in single:
        d_right[flip] = [over_row(d_0, flip)]
    left = []
    for step, piece in enumerate(pieces):
        left.append(piece)
        if step < z.n_chip - 1:
            left.append(other_core(piece) if step else twin)
    h_right = [h_right[flip] for flip in range(n_row)]

    n_pay = z.n_first + n_row
    total, panel, panel_t, right_last, table = call(
        functools.partial(first_kernel, z, [len(x) for x in h_right]),
        [*left[:z.n_first], *sum(h_right, [])],
        [
            shape((z.tall, z.wide), F32),
            shape((z.tall, z.n_first * z.wide), BF16),
            shape((z.n_first * z.wide, z.tall), BF16),
            shape((z.n_last * z.wide, z.wide), BF16),
            shape((n_row, 8, z.bs), jnp.int32),
        ],
        [
            pltpu.VMEM((z.nb * z.bs, z.wide), BF16),
            pltpu.VMEM((n_pay, 8, z.bs), jnp.int32),
            pltpu.SMEM((n_pay, 8, z.bs), jnp.int32),
            dma,
        ],
        [vmem] * (z.n_first + sum(map(len, h_right))), [vmem] * 5, 0, "first",
    )
    last, total = lax.optimization_barrier((left[-1], total))
    if n_row == 4:
        d_right[3] = [over_row(d_right[1][0][:d_half], 2), over_row(d_right[2][0][d_half:d_rows], 1)]
    forward(d_right)
    d_right = [d_right[flip] for flip in range(n_row)]
    part = shape((z.rows, z.ka) + block, BF16)
    cuts = 2 if n_row == 4 and z.rows % 2 == 0 else 1
    cut_part = shape((z.rows // cuts, z.ka) + block, BF16)
    total, m16, panel_last, panel_last_t, *far = call(
        functools.partial(last_kernel, z),
        [table, right_last, total, panel_t, *left[z.n_first:-1], last, other_core(last)],
        [
            shape((z.tall, z.wide), F32), shape((z.tall, z.wide), BF16),
            shape((z.tall, z.n_last * z.wide), BF16), shape((z.n_last * z.wide, z.tall), BF16),
        ] + [cut_part] * cuts,
        [
            pltpu.VMEM((z.n_last, 8, z.bs), jnp.int32),
            pltpu.SMEM((z.n_last, 8, z.bs), jnp.int32),
            dma,
        ],
        [smem] + [vmem] * (3 + z.n_last), [vmem] * (4 + cuts), panel_flops // 4 + part_flops, "last",
    )
    near = call(
        functools.partial(parts_kernel, z), [table, m16, panel_t, panel_last_t], [cut_part] * (cuts * (n_row - 2)), [],
        [smem] + [vmem] * 3, [vmem] * (cuts * (n_row - 2)), part_flops * (n_row - 2), "parts",
    )
    near, d_right = lax.optimization_barrier((near, d_right))
    if cuts == 2:
        far = over_row(far[0], 1), over_row(far[1], 2)
        x_0, y_1 = over_row(near[0], 1), over_row(near[3], 2)
    else:
        received = [over_row(term, n + 1) for n, term in enumerate([*near, *far])]
    mixed, base = call(
        functools.partial(base_kernel, z),
        [table, filter_cols.T, total, m16, panel_t, panel_last_t],
        [shape((z.rows, z.kf) + block, BF16), shape((z.rows, z.ka) + block, F32)],
        [pltpu.VMEM((z.rows, z.kf) + block, BF16), dma],
        [smem] * 2 + [vmem] * 4, [anywhere, vmem], part_flops, "base",
    )
    if cuts == 2:
        y_0, x_1 = call(
            functools.partial(add_kernel, z), [near[2], far[0], near[1], far[1]], [cut_part] * 2, [],
            [vmem] * 4, [vmem] * 2, 0, "add",
        )
        received = [x_0, over_row(x_1, 1), over_row(y_0, 2), y_1]
    squared, = call(
        functools.partial(square_kernel, z, [len(x) for x in d_right]),
        [table, filter_cols.T, panel, panel_last, *sum(d_right, [])],
        [shape((z.rows, z.kf) + block, BF16)],
        [
            pltpu.VMEM((z.nb * z.bs, z.wide), BF16), pltpu.VMEM((z.tall, z.wide), F32),
            pltpu.VMEM((z.rows, z.kf) + block, BF16), dma((2,)),
        ],
        [smem] * 2 + [vmem] * (2 + sum(map(len, d_right))), [anywhere], panel_flops, "squared",
    )
    gradient, = call(
        functools.partial(gradient_kernel, z), [base, *received], [part], [],
        [vmem] * (1 + len(received)), [vmem], 0, "gradient",
    )
    return squared, mixed, gradient


def solution(mesh):
    spec4 = P("row", "col", None, None)
    spec2 = P("row", "col")
    body = functools.partial(local, mesh.shape["row"], mesh.shape["col"])
    return jax.shard_map(
        body,
        mesh=mesh,
        in_specs=(spec4, spec2, spec4, spec2, spec2),
        out_specs=(spec4, spec4, spec4),
        check_vma=False,
    )
```
